128 devices in a mesh: shard: 8 (over x, y_hi), ctx: 16 (over z, y_lo, core).
Axes of the slice: x: 4, y: 4 (y_hi: 2, y_lo: 2; y = y_hi * 2 + y_lo), z: 4, core: 2. Of those that a mesh axis runs over, the one named last changes fastest.
Arguments:
- tokens: bfloat16 [16384, 2048], P(('shard', 'ctx')), may hold values from -6 to 6
- positions: int32 [8, 2048], P('shard'), may hold values from 0 to 2047, as said below
- out_grad: bfloat16 [16384, 2048], P(('shard', 'ctx')), may hold values from -6 to 6
- attn_gain: bfloat16 [2048], P('shard'), may hold values from 0.5 to 1.5
- w_query: bfloat16 [2048, 2048], P('shard'), may hold values from -0.125 to 0.125
- w_key: bfloat16 [256, 2048], P('shard'), may hold values from -0.125 to 0.125
- w_value: bfloat16 [256, 2048], P('shard'), may hold values from -0.125 to 0.125
- w_out: bfloat16 [2048, 2048], P('shard'), may hold values from -2 to 2
- ffn_gain: bfloat16 [2048], P('shard'), may hold values from 0.5 to 1.5
- w_gate: bfloat16 [5632, 2048], P('shard'), may hold values from -0.125 to 0.125
- w_up: bfloat16 [5632, 2048], P('shard'), may hold values from -0.125 to 0.125
- w_down: bfloat16 [5632, 2048], P('shard'), may hold values from -0.078125 to 0.078125
Outputs:
- activations: bfloat16 [16384, 2048], P(('shard', 'ctx'))
- input_grad: float32 [16384, 2048], P(('shard', 'ctx'))
- attn_gain_grad: float32 [2048], P('shard')
- w_query_grad: float32 [2048, 2048], P('shard')
- w_key_grad: float32 [256, 2048], P('shard')
- w_value_grad: float32 [256, 2048], P('shard')
- w_out_grad: float32 [2048, 2048], P('shard')
- ffn_gain_grad: float32 [2048], P('shard')
- w_gate_grad: float32 [5632, 2048], P('shard')
- w_up_grad: float32 [5632, 2048], P('shard')
- w_down_grad: float32 [5632, 2048], P('shard')
The draws below stay inside these ranges and needn't reach their ends.
Inputs may be any that keep to these rules, and one draw needn't show every extreme that they name: Row s lists the positions of the rows of sequence s: each block of 128 rows is two runs of 64 consecutive positions, from j * 64 and from (31 - j) * 64, every j of 0 to 15 once in a row.
All inputs are finite; a program needn't handle non-finite values.
Results may differ from the reference program's by a relative error of at most 0.023.
Values may be sent and summed in bfloat16 or wider, within the bound.
A program may use at most 320 MiB of HBM per device.

```python
import jax
import jax.numpy as jnp
from jax import lax

D = 2048
HEADS = 32
KV_HEADS = 4
HEAD = 64
FF = 5632
SPAN = 64
PAIRS = 16
LENGTH = 2048
SEQS = 8
TOKENS = 16384


def draw_positions(key, part):
    key = jax.random.fold_in(key, 11)
    offsets = jnp.arange(SPAN, dtype=jnp.int32)

    def one_sequence(seq_key):
        order = jax.random.permutation(seq_key, PAIRS).astype(jnp.int32)
        leading = order[:, None] * SPAN + offsets[None, :]
        trailing = (2 * PAIRS - 1 - order)[:, None] * SPAN + offsets[None, :]
        return jnp.concatenate([leading, trailing], axis=1).reshape(-1)
    return jax.vmap(one_sequence)(jax.random.split(key, SEQS)).astype(jnp.int32)


def block_levels(stream_key, dims, shards, smallest, high):
    loudness, own = 1.0, jax.random.fold_in(stream_key, 6)
    for dim, blocks in shards:
        steps = jnp.exp(jax.random.uniform(jax.random.fold_in(own, dim), (blocks,), jnp.float32, smallest / len(shards), high / len(shards)))
        loudness = loudness * jnp.repeat(steps, dims[dim] // blocks).reshape([-1 if axis == dim else 1 for axis in range(len(dims))])
    return loudness


def noise(key, extent, scale, bound, pieces=(), kind=jnp.bfloat16):
    factor_of = block_levels(key, extent, pieces, -0.22, 0.18) if pieces else 1.0
    values = jax.random.normal(key, extent, jnp.float32) * scale * factor_of
    return jnp.minimum(jnp.maximum(values, -bound), bound).astype(kind)


def setup_inputs(seed: int = 0) -> dict:
    streams_of = jax.random.split(jax.random.key(seed), 13)
    tokens = noise(streams_of[0], (TOKENS, D), 1.0, 6.0, ((0, 128),))
    positions = draw_positions(jax.random.fold_in(streams_of[12], 71), 0)
    out_grad = noise(streams_of[2], (TOKENS, D), 1.0, 6.0, ((0, 128),))
    attn_gain = jnp.clip(1.0 + 0.1 * jax.random.normal(streams_of[3], (D,), jnp.float32), 0.5, 1.5).astype(jnp.bfloat16)
    w_query = noise(streams_of[4], (D, D), D ** -0.5, 0.125, ((0, 8),))
    w_key = noise(streams_of[5], (KV_HEADS * HEAD, D), D ** -0.5, 0.125, ((0, 8),))
    w_value = noise(streams_of[6], (KV_HEADS * HEAD, D), D ** -0.5, 0.125, ((0, 8),))
    w_out = noise(streams_of[7], (D, D), (D // 256) ** -0.5, 2.0, ((0, 8),))
    ffn_gain = jnp.clip(1.0 + 0.1 * jax.random.normal(streams_of[8], (D,), jnp.float32), 0.5, 1.5).astype(jnp.bfloat16)
    w_gate = noise(streams_of[9], (FF, D), D ** -0.5, 0.125, ((0, 8),))
    w_up = noise(streams_of[10], (FF, D), D ** -0.5, 0.125, ((0, 8),))
    w_down = noise(streams_of[11], (FF, D), FF ** -0.5, 0.078125, ((0, 8),))
    return {"tokens": tokens, "positions": positions, "out_grad": out_grad, "attn_gain": attn_gain, "w_query": w_query, "w_key": w_key, "w_value": w_value, "w_out": w_out, "ffn_gain": ffn_gain, "w_gate": w_gate, "w_up": w_up, "w_down": w_down}


EPS = 1e-05
BASE = 10000.0
NEG = -1e+30

@jax.custom_vjp
def low(v):
    return lax.optimization_barrier(v.astype(jnp.bfloat16)).astype(jnp.float32)

@jax.custom_vjp
def low_back(v):
    return v

def low_keep(v):
    return (low(v), None)

def low_pass(kept, grad):
    return (grad,)

def back_keep(v):
    return (v, None)

def back_low(kept, grad):
    return (low(grad),)
low.defvjp(low_keep, low_pass)
low_back.defvjp(back_keep, back_low)

def matmul(left, right):
    return jnp.dot(left, right, precision=lax.Precision.HIGHEST, preferred_element_type=jnp.float32)

def rope_tables(places, width):
    half = width // 2
    freqs = BASE ** (-(jnp.arange(half).astype(jnp.float32) * 2.0 / width))
    angles = places.astype(jnp.float32)[:, None] * freqs[None, :]
    return (jnp.cos(angles), jnp.sin(angles))

def rotate(values, cosine, sine, sign):
    half = values.shape[-1] // 2
    first = values[..., :half]
    second = values[..., half:]
    cosine = cosine[:, None, :]
    sine = sign * sine[:, None, :]
    return jnp.concatenate([first * cosine - second * sine, second * cosine + first * sine], axis=-1)

def rms_norm(values, gain):
    return values * lax.rsqrt(lax.optimization_barrier(jnp.mean(values * values, axis=-1, keepdims=True)) + EPS) * gain

def split_heads(values, rows):
    return values.reshape(rows, KV_HEADS, HEADS // KV_HEADS, HEAD).transpose(1, 2, 0, 3).reshape(KV_HEADS, -1, HEAD)

def merge_heads(values, rows):
    return values.reshape(KV_HEADS, HEADS // KV_HEADS, rows, HEAD).transpose(2, 0, 1, 3).reshape(rows, HEADS * HEAD)

def layer(inputs, places, weights):
    attn_gain, w_query, w_key, w_value, w_out, ffn_gain, w_gate, w_up, w_down = weights
    rows = inputs.shape[0]
    score_scale = HEAD ** (-0.5)
    normed = low(rms_norm(inputs, attn_gain))
    query_pre = low_back(matmul(normed, w_query.T))
    key_pre = low_back(matmul(normed, w_key.T))
    value_pre = matmul(normed, w_value.T)
    cosine, sine = rope_tables(places, HEAD)
    queries = low(rotate(query_pre.reshape(rows, HEADS, HEAD), cosine, sine, 1.0))
    keys = low(rotate(key_pre.reshape(rows, KV_HEADS, HEAD), cosine, sine, 1.0))
    values = low(low_back(value_pre)).reshape(rows, KV_HEADS, HEAD)
    query_heads = split_heads(queries, rows)
    key_heads = keys.transpose(1, 0, 2)
    value_heads = values.transpose(1, 0, 2)
    query_places = jnp.tile(places, HEADS // KV_HEADS)
    allowed = query_places[:, None] >= places[None, :]

    def one_head(operands):
        query_one, key_one, value_one = operands
        scores = matmul(query_one, key_one.T) * score_scale
        scores = low_back(jnp.where(allowed, scores, NEG))
        largest = lax.optimization_barrier(jnp.max(scores, axis=-1, keepdims=True))
        exps = jnp.exp(scores - largest)
        probs = exps / lax.optimization_barrier(jnp.sum(exps, axis=-1, keepdims=True))
        return matmul(low(probs), value_one)
    mixed = lax.map(jax.checkpoint(one_head), (query_heads, key_heads, value_heads))
    attended = low(low_back(merge_heads(mixed, rows)))
    hidden_state = inputs + low_back(matmul(attended, w_out))
    normed_two = low(rms_norm(hidden_state, ffn_gain))
    gate = low_back(matmul(normed_two, w_gate.T))
    up_part = low_back(matmul(normed_two, w_up.T))
    inner = low(jax.nn.silu(gate) * up_part)
    return hidden_state + low_back(matmul(inner, w_down))

def reference(tokens, positions, out_grad, attn_gain, w_query, w_key, w_value, w_out, ffn_gain, w_gate, w_up, w_down):
    weights = tuple((w.astype(jnp.float32) for w in (attn_gain, w_query, w_key, w_value, w_out, ffn_gain, w_gate, w_up, w_down)))
    inputs = tokens.astype(jnp.float32).reshape(SEQS, LENGTH, D)
    cotangent = out_grad.astype(jnp.float32).reshape(SEQS, LENGTH, D)

    def forward(inputs, weights):
        return lax.map(lambda paired: layer(paired[0], paired[1], weights), (inputs, positions))
    outputs, pullback = jax.vjp(forward, inputs, weights)
    input_grad, grads = pullback(cotangent)
    return (outputs.reshape(TOKENS, D).astype(jnp.bfloat16), input_grad.reshape(TOKENS, D), grads[0], grads[1], grads[2], grads[3], grads[4], grads[5], grads[6], grads[7], grads[8])
```

```python
import jax
import jax.numpy as jnp
from jax import lax
from jax.sharding import PartitionSpec as P

D = 2048
HEADS = 32
KV_HEADS = 4
HEAD = 64


EPS = 1e-05
BASE = 10000.0
NEG = -1e30


def times(left, right):
    return jnp.dot(left, right, preferred_element_type=jnp.float32)


def times_transposed(left, right):
    return lax.dot_general(
        left, right, (((1,), (1,)), ((), ())), preferred_element_type=jnp.float32
    )


def transposed_times(left, right):
    return lax.dot_general(
        left, right, (((0,), (0,)), ((), ())), preferred_element_type=jnp.float32
    )


def rope_tables(places, width):
    half = width // 2
    freqs = BASE ** (-(jnp.arange(half).astype(jnp.float32) * 2.0 / width))
    angles = places.astype(jnp.float32)[:, None] * freqs[None, :]
    return (jnp.cos(angles), jnp.sin(angles))


def rotate(values, cosine, sine, sign):
    half = values.shape[-1] // 2
    first = values[..., :half]
    second = values[..., half:]
    cosine = cosine[:, None, :]
    sine = sign * sine[:, None, :]
    return jnp.concatenate(
        [first * cosine - second * sine, second * cosine + first * sine], axis=-1
    )


def rms_forward(values, gain):
    inverse = lax.rsqrt(jnp.mean(values * values, axis=-1, keepdims=True) + EPS)
    return (values * inverse * gain, inverse)


def rms_backward(values, inverse, gain, grads):
    scaled = grads * gain
    values_grad = inverse * scaled - values * inverse * inverse * inverse * jnp.mean(
        scaled * values, axis=-1, keepdims=True
    )
    gain_grad = jnp.sum(grads * values * inverse, axis=0)
    return (values_grad, gain_grad)


def split_heads(values, rows):
    return (
        values.reshape(rows, KV_HEADS, HEADS // KV_HEADS, HEAD)
        .transpose(1, 2, 0, 3)
        .reshape(KV_HEADS, -1, HEAD)
    )


def merge_heads(values, rows):
    return (
        values.reshape(KV_HEADS, HEADS // KV_HEADS, rows, HEAD)
        .transpose(2, 0, 1, 3)
        .reshape(rows, HEADS * HEAD)
    )


def split_rows(stacked_rows, part_rows):
    results = []
    offset = 0
    for row_count in part_rows:
        results.append(stacked_rows[offset : offset + row_count])
        offset += row_count
    return results


def by_shard(matrix, n_shard):
    return matrix.reshape(matrix.shape[0], n_shard, -1)


def swap_columns(matrix):
    return lax.all_to_all(matrix, "shard", split_axis=1, concat_axis=0, tiled=True)


def sum_over_ctx(partial):
    piece = lax.psum_scatter(
        partial.astype(jnp.bfloat16), "ctx", scatter_dimension=0, tiled=True
    )
    return lax.all_gather(piece, "ctx", axis=0, tiled=True).astype(jnp.float32)


def local(
    tokens,
    positions,
    out_grad,
    attn_gain,
    w_query,
    w_key,
    w_value,
    w_out,
    ffn_gain,
    w_gate,
    w_up,
    w_down,
):
    tok_rows = tokens.shape[0]
    n_shard = lax.axis_size("shard")
    n_ctx = lax.axis_size("ctx")
    group_size = HEADS // KV_HEADS
    score_scale = HEAD ** (-0.5)
    places = positions[0]
    own_places = lax.dynamic_slice_in_dim(places, lax.axis_index("ctx") * tok_rows, tok_rows)
    query_full, key_full, value_full, out_full, gain_one, gain_two = (
        lax.all_gather(w_query, "shard", axis=0, tiled=True),
        lax.all_gather(w_key, "shard", axis=0, tiled=True),
        lax.all_gather(w_value, "shard", axis=0, tiled=True),
        lax.all_gather(w_out, "shard", axis=0, tiled=True),
        lax.all_gather(attn_gain, "shard", axis=0, tiled=True),
        lax.all_gather(ffn_gain, "shard", axis=0, tiled=True),
    )
    out_grad_rows = lax.all_gather(out_grad, "shard", axis=0, tiled=True)
    gain_one = gain_one.astype(jnp.float32)
    gain_two = gain_two.astype(jnp.float32)
    inputs = tokens.astype(jnp.float32)
    normed, inverse_one = rms_forward(inputs, gain_one)
    normed_low = normed.astype(jnp.bfloat16)
    normed_rows = lax.all_gather(normed_low, "shard", axis=0, tiled=True)
    cosine, sine = rope_tables(own_places, HEAD)
    query_pre = times_transposed(normed_low, query_full)
    key_pre = times_transposed(normed_low, key_full)
    value_pre = times_transposed(normed_low, value_full)
    queries = rotate(query_pre.reshape(tok_rows, HEADS, HEAD), cosine, sine, 1.0).astype(
        jnp.bfloat16
    )
    keys_own = (
        rotate(key_pre.reshape(tok_rows, KV_HEADS, HEAD), cosine, sine, 1.0)
        .reshape(tok_rows, KV_HEADS * HEAD)
        .astype(jnp.bfloat16)
    )
    values_own = value_pre.astype(jnp.bfloat16)
    keys_all, values_all = (
        lax.all_gather(keys_own, "ctx", axis=0, tiled=True),
        lax.all_gather(values_own, "ctx", axis=0, tiled=True),
    )
    query_heads = split_heads(queries, tok_rows)
    key_heads = keys_all.reshape(-1, KV_HEADS, HEAD).transpose(1, 0, 2)
    value_heads = values_all.reshape(-1, KV_HEADS, HEAD).transpose(1, 0, 2)
    query_places = jnp.tile(own_places, group_size)
    allowed = query_places[:, None] >= places[None, :]

    def head_scores(query_one, key_one):
        return jnp.where(allowed, times_transposed(query_one, key_one) * score_scale, NEG)

    def head_forward(operands):
        query_one, key_one, value_one = operands
        scores = head_scores(query_one, key_one)
        largest = jnp.max(scores, axis=-1, keepdims=True)
        exps = jnp.exp(scores - largest)
        totals = jnp.sum(exps, axis=-1, keepdims=True)
        probs = (exps / totals).astype(jnp.bfloat16)
        return (times(probs, value_one), (largest + jnp.log(totals))[:, 0])

    mixed, log_totals = lax.map(head_forward, (query_heads, key_heads, value_heads))
    attended = merge_heads(mixed, tok_rows).astype(jnp.bfloat16)
    hidden_state = inputs + times(attended, out_full)
    normed_two, inverse_two = rms_forward(hidden_state, gain_two)
    normed_two_low = normed_two.astype(jnp.bfloat16)
    normed_two_rows = lax.all_gather(normed_two_low, "shard", axis=0, tiled=True)
    gate = times_transposed(normed_two_rows, w_gate)
    up_part = times_transposed(normed_two_rows, w_up)
    inner_grad = times_transposed(out_grad_rows, w_down)
    sigmoid = jax.nn.sigmoid(gate)
    activated = gate * sigmoid
    inner = (activated * up_part).astype(jnp.bfloat16)
    gate_grad = (inner_grad * up_part * sigmoid * (1.0 + gate * (1.0 - sigmoid))).astype(
        jnp.bfloat16
    )
    up_grad = (inner_grad * activated).astype(jnp.bfloat16)
    normed_two_grad = lax.psum_scatter(
        (times(gate_grad, w_gate) + times(up_grad, w_up)).astype(jnp.bfloat16),
        "shard",
        scatter_dimension=0,
        tiled=True,
    ).astype(jnp.float32)
    down_sum = lax.psum_scatter(
        times(inner, w_down).astype(jnp.bfloat16), "shard", scatter_dimension=0, tiled=True
    ).astype(jnp.float32)
    outputs = (hidden_state + down_sum).astype(jnp.bfloat16)
    ffn_grads = sum_over_ctx(
        jnp.concatenate(
            [
                transposed_times(gate_grad, normed_two_rows),
                transposed_times(up_grad, normed_two_rows),
                transposed_times(inner, out_grad_rows),
            ],
            axis=0,
        )
    )
    hidden_grad, gain_two_grad = rms_backward(hidden_state, inverse_two, gain_two, normed_two_grad)
    hidden_grad = hidden_grad + out_grad.astype(jnp.float32)
    hidden_low = hidden_grad.astype(jnp.bfloat16)
    hidden_rows = lax.all_gather(hidden_low, "shard", axis=0, tiled=True)
    attended_grad = times_transposed(hidden_low, out_full).astype(jnp.bfloat16)
    grad_heads = split_heads(attended_grad, tok_rows)

    def head_backward(operands):
        query_one, key_one, value_one, grad_one, log_one = operands
        probs = jnp.exp(head_scores(query_one, key_one) - log_one[:, None])
        prob_grad = times_transposed(grad_one, value_one)
        inner_sum = jnp.sum(probs * prob_grad, axis=-1, keepdims=True)
        score_grad = (probs * (prob_grad - inner_sum)).astype(jnp.bfloat16)
        query_grad = times(score_grad, key_one) * score_scale
        key_grad = transposed_times(score_grad, query_one) * score_scale
        value_grad = transposed_times(probs.astype(jnp.bfloat16), grad_one)
        return (query_grad, key_grad, value_grad)

    query_grads, key_grads, value_grads = lax.map(
        head_backward, (query_heads, key_heads, value_heads, grad_heads, log_totals)
    )
    key_rows = key_grads.transpose(1, 0, 2).reshape(-1, KV_HEADS * HEAD)
    value_rows = value_grads.transpose(1, 0, 2).reshape(-1, KV_HEADS * HEAD)
    key_mine, value_mine = (
        lax.psum_scatter(
            key_rows.astype(jnp.bfloat16), "ctx", scatter_dimension=0, tiled=True
        ).astype(jnp.float32),
        lax.psum_scatter(
            value_rows.astype(jnp.bfloat16), "ctx", scatter_dimension=0, tiled=True
        ).astype(jnp.float32),
    )
    query_pre_grad = (
        rotate(
            merge_heads(query_grads, tok_rows).reshape(tok_rows, HEADS, HEAD), cosine, sine, -1.0
        )
        .reshape(tok_rows, HEADS * HEAD)
        .astype(jnp.bfloat16)
    )
    key_pre_grad = (
        rotate(key_mine.reshape(tok_rows, KV_HEADS, HEAD), cosine, sine, -1.0)
        .reshape(tok_rows, KV_HEADS * HEAD)
        .astype(jnp.bfloat16)
    )
    value_pre_grad = value_mine.astype(jnp.bfloat16)
    normed_grad = (
        times(query_pre_grad, query_full)
        + times(key_pre_grad, key_full)
        + times(value_pre_grad, value_full)
    )
    input_grad, gain_one_grad = rms_backward(inputs, inverse_one, gain_one, normed_grad)
    input_grad = input_grad + hidden_grad
    out_grads_attn = transposed_times(swap_columns(attended), hidden_rows)
    factor_grads = transposed_times(
        swap_columns(
            jnp.concatenate(
                [
                    by_shard(query_pre_grad, n_shard),
                    by_shard(key_pre_grad, n_shard),
                    by_shard(value_pre_grad, n_shard),
                ],
                axis=2,
            ).reshape(tok_rows, -1)
        ),
        normed_rows,
    )
    attn_grads = sum_over_ctx(jnp.concatenate([factor_grads, out_grads_attn], axis=0))
    q_rows, kv_rows = w_query.shape[0], w_key.shape[0]
    query_wgrad, key_wgrad, value_wgrad, out_wgrad = split_rows(
        attn_grads, [q_rows, kv_rows, kv_rows, q_rows]
    )
    gate_wgrad, up_wgrad, down_wgrad = split_rows(ffn_grads, [w_gate.shape[0]] * 3)
    gain_one_sum, gain_two_sum = lax.psum((gain_one_grad, gain_two_grad), ("shard", "ctx"))
    slice_start = lax.axis_index("shard") * (D // n_shard)
    gain_one_out = lax.dynamic_slice_in_dim(gain_one_sum, slice_start, D // n_shard)
    gain_two_out = lax.dynamic_slice_in_dim(gain_two_sum, slice_start, D // n_shard)
    return (
        outputs,
        input_grad,
        gain_one_out,
        query_wgrad,
        key_wgrad,
        value_wgrad,
        out_wgrad,
        gain_two_out,
        gate_wgrad,
        up_wgrad,
        down_wgrad,
    )


def solution(mesh):
    in_specs = (
        P(("shard", "ctx"), None),
        P("shard", None),
        P(("shard", "ctx"), None),
        P("shard"),
        P("shard", None),
        P("shard", None),
        P("shard", None),
        P("shard", None),
        P("shard"),
        P("shard", None),
        P("shard", None),
        P("shard", None),
    )
    out_specs = (
        P(("shard", "ctx"), None),
        P(("shard", "ctx"), None),
        P("shard"),
        P("shard", None),
        P("shard", None),
        P("shard", None),
        P("shard", None),
        P("shard"),
        P("shard", None),
        P("shard", None),
        P("shard", None),
    )
    return jax.shard_map(local, mesh=mesh, in_specs=in_specs, out_specs=out_specs, check_vma=False)
```

```python
import functools

import jax
import jax.numpy as jnp
from jax import lax
from jax.experimental import pallas as pl
from jax.experimental.pallas import tpu as pltpu
from jax.sharding import PartitionSpec as P

D = 2048
HEADS = 32
KV_HEADS = 4
HEAD = 64
LANES = 128

EPS = 1e-05
BASE = 10000.0
NEG = -1e30
F32 = jnp.float32
LOW = jnp.bfloat16
MESH = pl.DeviceIdType.MESH
VMEM_LIMIT = 56 * 1024 * 1024


def times(left, right):
    return jnp.dot(left, right, preferred_element_type=F32)


def times_transposed(left, right):
    return lax.dot_general(left, right, (((1,), (1,)), ((), ())), preferred_element_type=F32)


def transposed_times(left, right):
    return lax.dot_general(left, right, (((0,), (0,)), ((), ())), preferred_element_type=F32)


def at(axis, ring, pair, core=0):
    index = lax.axis_index(axis)
    cores = 2 if axis == "ctx" else 1
    ring_at = lax.rem(index // (2 * cores) + ring % 4, 4)
    pair_at = lax.rem(lax.rem(index // cores, 2) + pair, 2)
    core_at = lax.rem(lax.rem(index, cores) + core, cores)
    return (ring_at * 2 + pair_at) * cores + core_at


def chip(axis, ring=0, pair=0):
    return at(axis, ring, pair) // (2 if axis == "ctx" else 1)


class Link:
    def __init__(self, send_sems, recv_sems, local_sems):
        self.send_sems, self.recv_sems, self.local_sems = send_sems, recv_sems, local_sems
        self.sent, self.kept = [], []

    def greet(self, offsets):
        barrier = pltpu.get_barrier_semaphore()
        for axis, ring, pair, core in offsets:
            pl.semaphore_signal(
                barrier, inc=1, device_id={axis: at(axis, ring, pair, core)}, device_id_type=MESH
            )
        pl.semaphore_wait(barrier, len(offsets))

    def send(self, source, target, axis, ring, pair, core=0):
        number = len(self.sent)
        copy = pltpu.make_async_remote_copy(
            src_ref=source,
            dst_ref=target,
            send_sem=self.send_sems.at[number],
            recv_sem=self.recv_sems.at[number],
            device_id={axis: at(axis, ring, pair, core)},
            device_id_type=MESH,
        )
        copy.start()
        self.sent.append(copy)
        return copy

    def keep(self, source, target):
        copy = pltpu.make_async_copy(source, target, self.local_sems.at[len(self.kept)])
        copy.start()
        self.kept.append(copy)
        return copy

    def kept_now(self, copy):
        copy.wait()
        self.kept = [None if other is copy else other for other in self.kept]

    def finish(self):
        for copy in self.kept:
            if copy is not None:
                copy.wait()
        for copy in self.sent:
            copy.wait_send()


NEAR = [(1, 0), (3, 0), (0, 1)]
ALL = [(r, p) for r in range(4) for p in range(2) if (r, p) != (0, 0)]
near = lambda axis: [(axis, r, p, 0) for r, p in NEAR]
whole = lambda axis: [(axis, r, p, 0) for r, p in ALL]
SIBLING = [("ctx", 0, 0, 1)]


def run(*jobs):
    jobs = list(jobs)
    while jobs:
        for job in list(jobs):
            if next(job, "end") == "end":
                jobs.remove(job)


def gather_job(link, axis, own, slot, share=None):
    me, pair = chip(axis), chip(axis, 0, 1)
    sharing = lambda index: share(index, slot(index)) if share else None
    kept = link.keep(own, slot(me))
    to_pair = link.send(own, slot(me), axis, 0, 1)
    down = link.send(own, slot(me), axis, -1, 0)
    up = link.send(own, slot(me), axis, 1, 0)
    if share:
        share(me, own)
    yield
    to_pair.wait_recv()
    pair_down = link.send(slot(pair), slot(pair), axis, -1, 0)
    pair_up = link.send(slot(pair), slot(pair), axis, 1, 0)
    sharing(pair)
    yield
    down.wait_recv()
    next_one = chip(axis, 1, 0)
    far_down = link.send(slot(next_one), slot(next_one), axis, -1, 0)
    sharing(next_one)
    yield
    up.wait_recv()
    sharing(chip(axis, -1, 0))
    yield
    pair_up.wait_recv()
    last_pair = chip(axis, -1, 1)
    far_up = link.send(slot(last_pair), slot(last_pair), axis, 1, 0)
    sharing(last_pair)
    yield
    pair_down.wait_recv()
    sharing(chip(axis, 1, 1))
    yield
    far_down.wait_recv()
    sharing(chip(axis, 2, 0))
    yield
    far_up.wait_recv()
    sharing(chip(axis, 2, 1))
    link.kept_now(kept)


def add_rows(target, terms, step=16):
    def body(i, _):
        rows = pl.ds(pl.multiple_of(i * step, step), step)
        total = terms[0][rows, :].astype(F32)
        for term in terms[1:]:
            total = total + term[rows, :].astype(F32)
        target[rows, :] = total.astype(target.dtype)
        return 0

    lax.fori_loop(0, target.shape[0] // step, body, 0)


def scatter_job(link, axis, part, landing, work, result):
    here = lambda ring, pair: part(chip(axis, ring, pair))
    to_next = link.send(here(2, 0), landing.at[0], axis, 1, 0)
    to_last = link.send(here(2, 1), landing.at[1], axis, -1, 0)
    pair_up = link.send(here(1, 1), landing.at[2], axis, 1, 0)
    mine_down = link.send(here(3, 0), landing.at[3], axis, -1, 0)
    yield
    to_last.wait_recv()
    add_rows(work.at[0], [here(3, 1), landing.at[1]])
    pair_down = link.send(work.at[0], landing.at[4], axis, -1, 0)
    yield
    to_next.wait_recv()
    add_rows(work.at[1], [here(1, 0), landing.at[0]])
    mine_up = link.send(work.at[1], landing.at[5], axis, 1, 0)
    yield
    pair_up.wait_recv()
    yield
    mine_down.wait_recv()
    yield
    pair_down.wait_recv()
    add_rows(work.at[2], [here(0, 1), landing.at[2], landing.at[4]])
    across = link.send(work.at[2], landing.at[6], axis, 0, 1)
    yield
    mine_up.wait_recv()
    yield
    across.wait_recv()
    add_rows(result, [here(0, 0), landing.at[3], landing.at[5], landing.at[6]])


def exchange_job(link, axis, part, slot):
    me = chip(axis)
    kept = link.keep(part(me), slot(me))
    copies = [link.send(part(chip(axis, r, p)), slot(me), axis, r, p) for r, p in ALL]
    yield
    for copy in copies:
        copy.wait_recv()
        yield
    link.kept_now(kept)


ANY = pl.BlockSpec(memory_space=pl.ANY)
INSIDE = pl.BlockSpec(memory_space=pltpu.VMEM)


def comm_call(kernel, number, inputs, in_specs, outputs, out_specs, scratch=()):
    sems = [pltpu.SemaphoreType.DMA((64,)), pltpu.SemaphoreType.DMA((64,)), pltpu.SemaphoreType.DMA((8,))]

    def body(*refs):
        link = Link(*refs[-3:])
        kernel(link, *refs[:-3])
        link.finish()

    return pl.pallas_call(
        body,
        out_shape=outputs,
        in_specs=in_specs,
        out_specs=out_specs,
        scratch_shapes=[*scratch, *sems],
        compiler_params=pltpu.CompilerParams(
            collective_id=number, has_side_effects=True, vmem_limit_bytes=VMEM_LIMIT
        ),
    )(*inputs)


shape = jax.ShapeDtypeStruct


def front_kernel(link, tokens, small, kv_send, w_out, token_rows, smalls, kv_other, out_full):
    link.greet(whole("shard") + [("ctx", 1, 0, 0), ("ctx", 3, 0, 0)] + SIBLING)
    core = lax.rem(lax.axis_index("ctx"), 2)
    ring = lax.axis_index("ctx") // 4

    def strip(ring_index, core_index):
        return pl.ds(pl.multiple_of((core_index * 4 + ring_index) * 32, 32), 32)

    mine = strip(ring, core)

    def out_job():
        yield from gather_job(link, "shard", w_out.at[mine], lambda i: out_full.at[i, mine])
        block = lambda rows, first=0, count=8: out_full.at[pl.ds(first, count), rows]
        up = link.send(block(mine), block(mine), "ctx", 1, 0)
        down = link.send(block(mine), block(mine), "ctx", -1, 0)
        sibs = [link.send(block(mine), block(mine), "ctx", 0, 0, 1)]
        yield
        up.wait_recv()
        rows = strip(lax.rem(ring + 3, 4), core)
        far_up = link.send(block(rows, 0, 4), block(rows, 0, 4), "ctx", 1, 0)
        sibs.append(link.send(block(rows), block(rows), "ctx", 0, 0, 1))
        yield
        down.wait_recv()
        rows = strip(lax.rem(ring + 1, 4), core)
        far_down = link.send(block(rows, 4, 4), block(rows, 4, 4), "ctx", -1, 0)
        sibs.append(link.send(block(rows), block(rows), "ctx", 0, 0, 1))
        yield
        far_up.wait_recv()
        far_down.wait_recv()
        rows = strip(lax.rem(ring + 2, 4), core)
        sibs.append(link.send(block(rows), block(rows), "ctx", 0, 0, 1))
        yield
        for copy in sibs:
            copy.wait_recv()

    def kv_job():
        copy = link.send(kv_send, kv_other, "shard", 0, 1)
        yield
        copy.wait_recv()

    run(
        exchange_job(link, "shard", lambda i: small, lambda i: smalls.at[i]),
        kv_job(),
        out_job(),
        gather_job(link, "shard", tokens, lambda i: token_rows.at[i]),
    )


def qkv_kernel(link, queries, kv, queries_got, kv_all, kv_got, kv_own):
    link.greet(whole("shard") + near("ctx") + SIBLING)
    core = lax.rem(lax.axis_index("ctx"), 2)

    def kv_job():
        yield from exchange_job(link, "shard", lambda i: kv.at[i], lambda i: kv_got.at[i])
        for head in range(KV_HEADS):
            kv_own[:, head * 128 : (head + 1) * 128] = kv_got[2 * head] + kv_got[2 * head + 1]
        slot = lambda i: kv_all.at[i * 2 + core]
        sibs = []

        def share(index, block):
            sibs.append(link.send(block, slot(index), "ctx", 0, 0, 1))

        yield from gather_job(link, "ctx", kv_own, slot, share)
        for copy in sibs:
            copy.wait_recv()

    run(kv_job(), exchange_job(link, "shard", lambda i: queries.at[i], lambda i: queries_got.at[i]))


def gather_kernel(link, own, slots):
    link.greet(near("shard"))
    run(gather_job(link, "shard", own, lambda i: slots.at[i]))


def reduced(link, theirs, mine, from_sibling, landing, work, summed):
    copy = link.send(theirs, from_sibling, "ctx", 0, 0, 1)
    yield
    copy.wait_recv()
    add_rows(from_sibling, [mine, from_sibling])
    columns = lambda i: from_sibling.at[:, pl.ds(pl.multiple_of(i * LANES, LANES), LANES)]
    yield from scatter_job(link, "ctx", columns, landing, work, summed)


def spread(link, summed, full):
    core = lax.rem(lax.axis_index("ctx"), 2)
    slot = lambda i: full.at[:, pl.ds(pl.multiple_of((core * 8 + i) * LANES, LANES), LANES)]
    sibs = []

    def share(index, block):
        sibs.append(link.send(block, slot(index), "ctx", 0, 0, 1))

    yield from gather_job(link, "ctx", summed, slot, share)
    for copy in sibs:
        copy.wait_recv()


def middle_kernel(link, parts, theirs, mine, result, summed, land_a, work_a, sib, land_b, work_b):
    link.greet(near("shard") + near("ctx") + SIBLING)
    run(
        scatter_job(link, "shard", lambda i: parts.at[i], land_a, work_a, result),
        reduced(link, theirs, mine, sib, land_b, work_b, summed),
    )


def back_kernel(link, kv_parts, summed, parts, queries, attended, kv_grad, full, down, query_cols, attended_cols,
                sib, land_k, work_k, land_d, work_d):
    link.greet(whole("shard") + near("ctx") + SIBLING)
    core = lax.rem(lax.axis_index("ctx"), 2)

    def kv_job():
        copies = [
            link.send(kv_parts.at[i * 2 + 1 - core], sib.at[i], "ctx", 0, 0, 1) for i in range(8)
        ]
        yield
        for i, copy in enumerate(copies):
            copy.wait_recv()
            add_rows(sib.at[i], [sib.at[i], kv_parts.at[i * 2 + core]])
        yield from scatter_job(link, "ctx", lambda i: sib.at[i], land_k, work_k, kv_grad)

    columns = lambda ref: lambda i: ref.at[:, pl.ds(pl.multiple_of(i * 256, 256), 256)]
    run(
        kv_job(),
        exchange_job(link, "shard", columns(queries), lambda i: query_cols.at[i]),
        exchange_job(link, "shard", columns(attended), lambda i: attended_cols.at[i]),
        scatter_job(link, "shard", lambda i: parts.at[i], land_d, work_d, down),
        spread(link, summed, full),
    )


def swap_kernel(link, parts, slots):
    link.greet(whole("shard"))
    run(exchange_job(link, "shard", lambda i: parts.at[i], lambda i: slots.at[i]))


def last_kernel(link, parts, theirs, mine, gains, result, full, gain_sum,
                land_a, work_a, sib, land_b, work_b, summed, gain_land, gain_work, gain_ctx):
    link.greet(whole("shard") + whole("ctx") + SIBLING)

    def weight_job():
        yield from reduced(link, theirs, mine, sib, land_b, work_b, summed)
        yield from spread(link, summed, full)

    def gain_job():
        yield from exchange_job(link, "shard", lambda i: gains.at[i], lambda i: gain_land.at[i])
        gain_work[0] = sum(gain_land[i] for i in range(8))
        copy = link.send(gain_work.at[0], gain_work.at[1], "ctx", 0, 0, 1)
        yield
        copy.wait_recv()
        gain_work[2] = gain_work[0] + gain_work[1]
        copies = [
            link.send(gain_work.at[2], gain_ctx.at[i], "ctx", r, p) for i, (r, p) in enumerate(ALL)
        ]
        yield
        for copy in copies:
            copy.wait_recv()
        gain_sum[...] = gain_work[2] + sum(gain_ctx[i] for i in range(7))

    run(
        gain_job(),
        scatter_job(link, "shard", lambda i: parts.at[i], land_a, work_a, result),
        weight_job(),
    )


def rope_tables(places, width):
    half = width // 2
    freqs = BASE ** (-(jnp.arange(half).astype(F32) * 2.0 / width))
    angles = places.astype(F32)[:, None] * freqs[None, :]
    return jnp.cos(angles), jnp.sin(angles)


def wide_tables(places, heads):
    cosine, sine = rope_tables(places, HEAD)
    return (
        jnp.tile(jnp.concatenate([cosine, cosine], axis=1), (1, heads)),
        jnp.tile(jnp.concatenate([-sine, sine], axis=1), (1, heads)),
    )


def swap_halves(values):
    half = HEAD // 2
    lane = lax.broadcasted_iota(jnp.int32, values.shape, 1) % HEAD
    return jnp.where(lane < half, jnp.roll(values, -half, 1), jnp.roll(values, half, 1))


def swap_rows(weight):
    return weight.reshape(-1, 2, HEAD // 2, D)[:, ::-1].reshape(weight.shape)


def rms_forward(values, gain):
    inverse = lax.rsqrt(jnp.mean(values * values, axis=-1, keepdims=True) + EPS)
    return (values * inverse * gain, inverse)


def rms_backward(values, inverse, gain, grads):
    scaled = grads * gain
    return inverse * scaled - values * inverse * inverse * inverse * jnp.mean(
        scaled * values, axis=-1, keepdims=True
    )


def attend(queries, kv_all, places, own_places):
    rows = own_places.shape[0]
    heads = queries.reshape(4, 2, rows, 4, HEAD).transpose(0, 1, 3, 2, 4).reshape(4, -1, HEAD)
    kv = kv_all.reshape(-1, KV_HEADS, 2, HEAD).transpose(2, 1, 0, 3)
    allowed = jnp.tile(own_places, 8)[:, None] >= places[None, :]

    def head_forward(operands):
        query_one, key_one, value_one = operands
        scores = jnp.where(allowed, times_transposed(query_one, key_one) * HEAD**-0.5, NEG)
        largest = jnp.max(scores, axis=-1, keepdims=True)
        exps = jnp.exp(scores - largest)
        totals = jnp.sum(exps, axis=-1, keepdims=True)
        probs = (exps / totals).astype(LOW)
        return (times(probs, value_one), (largest + jnp.log(totals))[:, 0])

    mixed, log_totals = lax.map(head_forward, (heads, kv[0], kv[1]))
    attended = mixed.reshape(4, 8, rows, HEAD).transpose(2, 0, 1, 3).reshape(rows, D).astype(LOW)
    return attended, (heads, log_totals)


def attend_back(kept, attended, attended_grad, kv_all, places, own_places):
    heads, log_totals = kept
    rows = own_places.shape[0]
    kv = kv_all.reshape(-1, KV_HEADS, 2, HEAD).transpose(2, 1, 0, 3)
    grads = attended_grad.reshape(rows, 4, 8, HEAD).transpose(1, 2, 0, 3).reshape(4, -1, HEAD)
    allowed = jnp.tile(own_places, 8)[:, None] >= places[None, :]
    scale = HEAD**-0.5

    def head_backward(operands):
        query_one, key_one, value_one, grad_one, log_one = operands
        scores = jnp.where(allowed, times_transposed(query_one, key_one) * scale, NEG)
        probs = jnp.exp(scores - log_one[:, None])
        prob_grad = times_transposed(grad_one, value_one)
        inner_sum = jnp.sum(probs * prob_grad, axis=-1, keepdims=True)
        score_grad = (probs * (prob_grad - inner_sum)).astype(LOW)
        query_grad = times(score_grad, key_one) * scale
        key_grad = transposed_times(score_grad, query_one) * scale
        value_grad = transposed_times(probs.astype(LOW), grad_one)
        return (query_grad, jnp.concatenate([key_grad, value_grad], axis=1).astype(LOW))

    query_grads, kv_grads = lax.map(head_backward, (heads, kv[0], kv[1], grads, log_totals))
    query_grads = query_grads.reshape(4, 8, rows, HEAD).transpose(2, 0, 1, 3).reshape(rows, D)
    return query_grads, kv_grads.transpose(1, 0, 2).reshape(16, rows, 512)


def local(
    tokens,
    positions,
    out_grad,
    attn_gain,
    w_query,
    w_key,
    w_value,
    w_out,
    ffn_gain,
    w_gate,
    w_up,
    w_down,
):
    rows = tokens.shape[0]
    shard, ctx = lax.axis_index("shard"), lax.axis_index("ctx")
    shard_pair, core = shard % 2, ctx % 2
    score_scale = HEAD ** (-0.5)
    places = positions[0]
    own_places = lax.dynamic_slice_in_dim(places, ctx * rows, rows)
    blocks = lambda m: m.reshape(8, rows, -1)

    small = jnp.stack(
        [attn_gain, ffn_gain, jnp.concatenate([own_places // 64, own_places % 64]).astype(LOW)]
    )
    small = jnp.concatenate([small, jnp.zeros((13, 256), LOW)], axis=0)
    out_grad_rows = lax.all_gather(out_grad, "shard", axis=0, tiled=True)
    token_rows, smalls, kv_other, out_full = comm_call(
        front_kernel,
        0,
        [tokens, small, jnp.where(shard_pair == 0, w_value, w_key), w_out],
        [ANY] * 4,
        [shape((8, rows, D), LOW), shape((8, 16, 256), LOW), shape((32, D), LOW), shape((8, 256, D), LOW)],
        [ANY] * 4,
    )
    token_rows, out_full = token_rows.reshape(-1, D), out_full.reshape(D, D)
    gain_one = smalls[:, 0].reshape(-1).astype(F32)
    gain_two = smalls[:, 1].reshape(-1).astype(F32)
    place_rows = (smalls[:, 2, :rows].astype(F32) * 64.0 + smalls[:, 2, rows:].astype(F32)).reshape(-1)
    nothing = jnp.zeros((64, D), LOW)
    w_first = jnp.where(
        shard_pair == 0,
        jnp.concatenate([w_query, w_key, kv_other, nothing], axis=0),
        jnp.concatenate([w_query, nothing, kv_other, w_value], axis=0),
    )

    inputs_rows = token_rows.astype(F32)
    normed, inverse_rows = rms_forward(inputs_rows, gain_one)
    normed_rows = normed.astype(LOW)
    first = times_transposed(normed_rows, w_first)
    turned = times_transposed(normed_rows, swap_rows(w_first[:320]))
    cosine, sine = wide_tables(place_rows, 5)
    rotated = first[:, :320] * cosine + turned * sine
    queries = rotated[:, :256].astype(LOW)
    plain = jnp.where(shard_pair == 1, first[:, 256:320], rotated[:, 256:])
    kv_part = jnp.concatenate([plain, first[:, 320:]], axis=1).astype(LOW)
    queries, kv_all = comm_call(
        qkv_kernel,
        1,
        [blocks(queries), blocks(kv_part)],
        [ANY] * 2,
        [shape((8, rows, 256), LOW), shape((16, rows, 512), LOW)],
        [ANY] * 2,
        [pltpu.VMEM((8, rows, 128), LOW), pltpu.VMEM((rows, 512), LOW)],
    )

    attended, for_back = attend(queries, kv_all, places, own_places)

    inputs = tokens.astype(F32)
    hidden_state = inputs + times(attended, out_full)
    normed_two, inverse_two = rms_forward(hidden_state, gain_two)
    (normed_two_rows,) = comm_call(
        gather_kernel, 2, [normed_two.astype(LOW)], [ANY], [shape((8, rows, D), LOW)], [ANY]
    )
    normed_two_rows = normed_two_rows.reshape(-1, D)

    gate = times_transposed(normed_two_rows, w_gate)
    up_part = times_transposed(normed_two_rows, w_up)
    inner_grad = times_transposed(out_grad_rows, w_down)
    sigmoid = jax.nn.sigmoid(gate)
    activated = gate * sigmoid
    inner = (activated * up_part).astype(LOW)
    gate_grad = (inner_grad * up_part * sigmoid * (1.0 + gate * (1.0 - sigmoid))).astype(LOW)
    up_grad = (inner_grad * activated).astype(LOW)
    normed_two_parts = (times(gate_grad, w_gate) + times(up_grad, w_up)).astype(LOW)
    down_parts = times(inner, w_down).astype(LOW)

    def halves(terms):
        def one(which):
            cut = lambda m: lax.dynamic_slice_in_dim(m, which * 1024, 1024, axis=1)
            return jnp.concatenate(
                [transposed_times(left, cut(right)).astype(LOW) for left, right in terms], axis=0
            )

        return one(1 - core), one(core)

    ff = w_gate.shape[0]
    theirs, mine = halves(
        [(gate_grad, normed_two_rows), (up_grad, normed_two_rows), (inner, out_grad_rows)]
    )
    vmem = lambda count, *dims: pltpu.VMEM((count, *dims), LOW)
    normed_two_grad, summed = comm_call(
        middle_kernel,
        3,
        [blocks(normed_two_parts), theirs, mine],
        [INSIDE, ANY, INSIDE],
        [shape((rows, D), F32), shape((3 * ff, LANES), LOW)],
        [INSIDE, INSIDE],
        [
            vmem(7, rows, D),
            vmem(3, rows, D),
            pltpu.VMEM((3 * ff, 1024), LOW),
            vmem(7, 3 * ff, LANES),
            vmem(3, 3 * ff, LANES),
        ],
    )

    gain_two_part = jnp.sum(normed_two_grad * hidden_state * inverse_two, axis=0)
    hidden_grad = out_grad.astype(F32) + rms_backward(
        hidden_state, inverse_two, gain_two, normed_two_grad
    )
    hidden_low = hidden_grad.astype(LOW)
    hidden_rows = lax.all_gather(hidden_low, "shard", axis=0, tiled=True)
    attended_grad = times_transposed(hidden_low, out_full).astype(LOW)
    query_grads, kv_parts = attend_back(for_back, attended, attended_grad, kv_all, places, own_places)

    cosine_own, sine_own = wide_tables(own_places, HEADS)
    turn_back = lambda v: v * cosine_own[:, : v.shape[1]] - swap_halves(v) * sine_own[:, : v.shape[1]]
    query_pre_grad = turn_back(query_grads).astype(LOW)
    kv_grad, ffn_full, down_sum, query_cols, attended_cols = comm_call(
        back_kernel,
        4,
        [kv_parts, summed, blocks(down_parts), query_pre_grad, attended],
        [INSIDE, INSIDE, INSIDE, ANY, ANY],
        [
            shape((rows, 512), F32),
            shape((3 * ff, D), LOW),
            shape((rows, D), F32),
            shape((8, rows, 256), LOW),
            shape((8, rows, 256), LOW),
        ],
        [INSIDE, ANY, INSIDE, ANY, ANY],
        [vmem(8, rows, 512), vmem(7, rows, 512), vmem(3, rows, 512), vmem(7, rows, D), vmem(3, rows, D)],
    )
    outputs = (hidden_state + down_sum).astype(LOW)
    gate_wgrad, up_wgrad, down_wgrad = (
        ffn_full[i * ff : (i + 1) * ff].astype(F32) for i in range(3)
    )

    by_head = kv_grad.reshape(rows, KV_HEADS, 2 * HEAD)
    key_grad = turn_back(by_head[:, :, :HEAD].reshape(rows, 256)).astype(LOW)
    value_grad = by_head[:, :, HEAD:].reshape(rows, 256).astype(LOW)
    kv_factors = jnp.concatenate(
        [key_grad.reshape(rows, 8, 32), value_grad.reshape(rows, 8, 32), jnp.zeros((rows, 8, 64), LOW)],
        axis=2,
    ).transpose(1, 0, 2)
    (kv_cols,) = comm_call(
        swap_kernel, 5, [kv_factors], [ANY], [shape((8, rows, 128), LOW)], [ANY]
    )
    query_cols, attended_cols = query_cols.reshape(-1, 256), attended_cols.reshape(-1, 256)
    kv_cols = kv_cols.reshape(-1, 128)
    kv_weights = jnp.concatenate([w_key, w_value, jnp.zeros((64, D), LOW)], axis=0)
    normed_parts = times(query_cols, w_query) + times(kv_cols, kv_weights)
    gain_one_part = jnp.sum(normed_parts * inputs_rows * inverse_rows, axis=0)
    theirs, mine = halves(
        [(query_cols, normed_rows), (kv_cols[:, :64], normed_rows), (attended_cols, hidden_rows)]
    )
    gains = jnp.stack([gain_one_part, gain_two_part]).reshape(2, 8, 256).transpose(1, 0, 2)
    gains = jnp.concatenate([gains, jnp.zeros((8, 6, 256), F32)], axis=1)
    normed_grad, attn_full, gain_sum = comm_call(
        last_kernel,
        6,
        [blocks(normed_parts.astype(LOW)), theirs, mine, gains],
        [INSIDE, ANY, INSIDE, INSIDE],
        [shape((rows, D), F32), shape((576, D), LOW), shape((8, 256), F32)],
        [INSIDE, ANY, INSIDE],
        [
            vmem(7, rows, D),
            vmem(3, rows, D),
            pltpu.VMEM((576, 1024), LOW),
            vmem(7, 576, LANES),
            vmem(3, 576, LANES),
            pltpu.VMEM((576, LANES), LOW),
            pltpu.VMEM((8, 8, 256), F32),
            pltpu.VMEM((3, 8, 256), F32),
            pltpu.VMEM((7, 8, 256), F32),
        ],
    )
    inverse_one = lax.dynamic_slice_in_dim(inverse_rows, shard * rows, rows)
    input_grad = hidden_grad + rms_backward(inputs, inverse_one, gain_one, normed_grad)
    query_wgrad, key_wgrad, value_wgrad, out_wgrad = (
        attn_full[a:b].astype(F32) for a, b in ((0, 256), (256, 288), (288, 320), (320, 576))
    )
    return (
        outputs,
        input_grad,
        gain_sum[0],
        query_wgrad,
        key_wgrad,
        value_wgrad,
        out_wgrad,
        gain_sum[1],
        gate_wgrad,
        up_wgrad,
        down_wgrad,
    )


def solution(mesh):
    rows = P(("shard", "ctx"), None)
    matrix = P("shard", None)
    vector = P("shard")
    in_specs = (rows, matrix, rows, vector, matrix, matrix, matrix, matrix, vector) + (matrix,) * 3
    out_specs = (rows, rows, vector, matrix, matrix, matrix, matrix, vector) + (matrix,) * 3
    return jax.shard_map(local, mesh=mesh, in_specs=in_specs, out_specs=out_specs, check_vma=False)
```

```python
import functools

import jax
import jax.numpy as jnp
from jax import lax
from jax.experimental import pallas as pl
from jax.experimental.pallas import tpu as pltpu
from jax.sharding import PartitionSpec as P

D = 2048
HEADS = 32
KV_HEADS = 4
HEAD = 64
LANES = 128

EPS = 1e-05
BASE = 10000.0
NEG = -1e30
F32 = jnp.float32
LOW = jnp.bfloat16
MESH = pl.DeviceIdType.MESH
VMEM_LIMIT = 56 * 1024 * 1024


def times(left, right):
    return jnp.dot(left, right, preferred_element_type=F32)


def times_transposed(left, right):
    return lax.dot_general(left, right, (((1,), (1,)), ((), ())), preferred_element_type=F32)


def transposed_times(left, right):
    return lax.dot_general(left, right, (((0,), (0,)), ((), ())), preferred_element_type=F32)


def rope_tables(places, width):
    half = width // 2
    freqs = BASE ** (-(jnp.arange(half).astype(F32) * 2.0 / width))
    angles = places.astype(F32)[:, None] * freqs[None, :]
    return jnp.cos(angles), jnp.sin(angles)


def wide_tables(places, heads):
    cosine, sine = rope_tables(places, HEAD)
    return (
        jnp.tile(jnp.concatenate([cosine, cosine], axis=1), (1, heads)),
        jnp.tile(jnp.concatenate([-sine, sine], axis=1), (1, heads)),
    )


def inverse_of(values):
    return lax.rsqrt(jnp.mean(values * values, axis=-1, keepdims=True) + EPS)


def rms_forward(values, gain):
    inverse = inverse_of(values)
    return (values * inverse * gain, inverse)


def rms_backward(values, inverse, gain, grads):
    scaled = grads * gain
    return inverse * scaled - values * inverse * inverse * inverse * jnp.mean(
        scaled * values, axis=-1, keepdims=True
    )


def at(axis, ring, pair, core=0):
    index = lax.axis_index(axis)
    cores = 2 if axis == "ctx" else 1
    ring_at = lax.rem(index // (2 * cores) + ring % 4, 4)
    pair_at = lax.rem(lax.rem(index // cores, 2) + pair, 2)
    core_at = lax.rem(lax.rem(index, cores) + core, cores)
    return (ring_at * 2 + pair_at) * cores + core_at


def chip(axis, ring=0, pair=0):
    return at(axis, ring, pair) // (2 if axis == "ctx" else 1)


class Link:
    def __init__(self, send_sems, recv_sems, local_sems):
        self.send_sems, self.recv_sems, self.local_sems = send_sems, recv_sems, local_sems
        self.sent, self.kept = [], []

    def greet(self, offsets):
        barrier = pltpu.get_barrier_semaphore()
        for axis, ring, pair, core in offsets:
            pl.semaphore_signal(
                barrier, inc=1, device_id={axis: at(axis, ring, pair, core)}, device_id_type=MESH
            )
        pl.semaphore_wait(barrier, len(offsets))

    def send(self, source, target, axis, ring, pair, core=0):
        number = len(self.sent)
        copy = pltpu.make_async_remote_copy(
            src_ref=source,
            dst_ref=target,
            send_sem=self.send_sems.at[number],
            recv_sem=self.recv_sems.at[number],
            device_id={axis: at(axis, ring, pair, core)},
            device_id_type=MESH,
        )
        copy.start()
        self.sent.append(copy)
        return copy

    def keep(self, source, target):
        copy = pltpu.make_async_copy(source, target, self.local_sems.at[len(self.kept)])
        copy.start()
        self.kept.append(copy)
        return copy

    def kept_now(self, copy):
        copy.wait()
        self.kept = [None if other is copy else other for other in self.kept]

    def finish(self):
        for copy in self.kept:
            if copy is not None:
                copy.wait()
        for copy in self.sent:
            copy.wait_send()


NEAR = [(1, 0), (3, 0), (0, 1)]
ALL = [(r, p) for r in range(4) for p in range(2) if (r, p) != (0, 0)]
near = lambda axis: [(axis, r, p, 0) for r, p in NEAR]
whole = lambda axis: [(axis, r, p, 0) for r, p in ALL]
SIBLING = [("ctx", 0, 0, 1)]


def run(*jobs):
    waiting = [(next(job), number, job) for number, job in enumerate(jobs)]
    while waiting:
        waiting.sort(key=lambda entry: entry[:2])
        _, number, job = waiting.pop(0)
        after = next(job, None)
        if after is not None:
            waiting.append((after, number, job))


def gather_job(link, axis, own, slot, share=None, start=0.0, block=10.5):
    me, pair = chip(axis), chip(axis, 0, 1)
    sharing = lambda index: share(index, slot(index)) if share else None
    yield start
    kept = link.keep(own, slot(me))
    to_pair = link.send(own, slot(me), axis, 0, 1)
    down = link.send(own, slot(me), axis, -1, 0)
    up = link.send(own, slot(me), axis, 1, 0)
    if share:
        share(me, own)
    yield start + block + 3.0
    to_pair.wait_recv()
    pair_down = link.send(slot(pair), slot(pair), axis, -1, 0)
    pair_up = link.send(slot(pair), slot(pair), axis, 1, 0)
    sharing(pair)
    yield start + block + 3.1
    down.wait_recv()
    next_one = chip(axis, 1, 0)
    far_down = link.send(slot(next_one), slot(next_one), axis, -1, 0)
    sharing(next_one)
    yield start + block + 3.2
    up.wait_recv()
    sharing(chip(axis, -1, 0))
    yield start + 2 * block + 4.0
    pair_up.wait_recv()
    last_pair = chip(axis, -1, 1)
    far_up = link.send(slot(last_pair), slot(last_pair), axis, 1, 0)
    sharing(last_pair)
    yield start + 2 * block + 4.1
    pair_down.wait_recv()
    sharing(chip(axis, 1, 1))
    yield start + 3 * block + 5.0
    far_down.wait_recv()
    sharing(chip(axis, 2, 0))
    yield start + 3 * block + 5.1
    far_up.wait_recv()
    sharing(chip(axis, 2, 1))
    link.kept_now(kept)


def add_rows(target, terms, step=16):
    def body(i, _):
        rows = pl.ds(pl.multiple_of(i * step, step), step)
        total = terms[0][rows, :].astype(F32)
        for term in terms[1:]:
            total = total + term[rows, :].astype(F32)
        target[rows, :] = total.astype(target.dtype)
        return 0

    lax.fori_loop(0, target.shape[0] // step, body, 0)


def scatter_job(link, axis, part, landing, work, result, start=0.0, block=10.5):
    here = lambda ring, pair: part(chip(axis, ring, pair))
    yield start
    to_last = link.send(here(2, 1), landing.at[1], axis, -1, 0)
    to_next = link.send(here(2, 0), landing.at[0], axis, 1, 0)
    pair_up = link.send(here(1, 1), landing.at[2], axis, 1, 0)
    mine_down = link.send(here(3, 0), landing.at[3], axis, -1, 0)
    spare = [here(3, 1), here(1, 0), here(0, 1), here(0, 0)]
    yield start + block + 3.0
    to_last.wait_recv()
    add_rows(work.at[0], [spare[0], landing.at[1]])
    pair_down = link.send(work.at[0], landing.at[4], axis, -1, 0)
    yield start + block + 3.1
    to_next.wait_recv()
    add_rows(work.at[1], [spare[1], landing.at[0]])
    mine_up = link.send(work.at[1], landing.at[5], axis, 1, 0)
    yield start + 2 * block + 3.0
    pair_up.wait_recv()
    mine_down.wait_recv()
    yield start + 3 * block + 4.0
    pair_down.wait_recv()
    add_rows(work.at[2], [spare[2], landing.at[2], landing.at[4]])
    across = link.send(work.at[2], landing.at[6], axis, 0, 1)
    yield start + 3 * block + 4.1
    mine_up.wait_recv()
    yield start + 4 * block + 8.0
    across.wait_recv()
    add_rows(result, [spare[3], landing.at[3], landing.at[5], landing.at[6]])


def exchange_job(link, axis, part, slot, start=0.0, length=8.0):
    me = chip(axis)
    yield start
    kept = link.keep(part(me), slot(me))
    copies = [link.send(part(chip(axis, r, p)), slot(me), axis, r, p) for r, p in ALL]
    yield start + length
    for copy in copies:
        copy.wait_recv()
    link.kept_now(kept)


ANY = pl.BlockSpec(memory_space=pl.ANY)
INSIDE = pl.BlockSpec(memory_space=pltpu.VMEM)


def comm_call(kernel, number, inputs, in_specs, outputs, out_specs, scratch=()):
    sems = [pltpu.SemaphoreType.DMA((96,)), pltpu.SemaphoreType.DMA((96,)), pltpu.SemaphoreType.DMA((8,))]

    def body(*refs):
        link = Link(*refs[-3:])
        kernel(link, *refs[:-3])
        link.finish()

    return pl.pallas_call(
        body,
        out_shape=outputs,
        in_specs=in_specs,
        out_specs=out_specs,
        scratch_shapes=[*scratch, *sems],
        compiler_params=pltpu.CompilerParams(
            collective_id=number, has_side_effects=True, vmem_limit_bytes=VMEM_LIMIT
        ),
    )(*inputs)


shape = jax.ShapeDtypeStruct


def front_kernel(link, tokens, small, kv_send, w_out, token_rows, smalls, kv_other, out_full):
    link.greet(whole("shard") + [("ctx", 1, 0, 0), ("ctx", 3, 0, 0)] + SIBLING)
    core = lax.rem(lax.axis_index("ctx"), 2)
    ring = lax.axis_index("ctx") // 4

    def block(index, ring_further=0):
        at_ring = lax.rem(ring + ring_further, 4)
        rows = pl.ds(pl.multiple_of((core * 4 + at_ring) * 32, 32), 32)
        return out_full.at[index, rows]

    mine = pl.ds(pl.multiple_of((core * 4 + ring) * 32, 32), 32)
    passing, sibs = [], []

    def share(index, source):
        sibs.append(link.send(source, block(index), "ctx", 0, 0, 1))
        up = link.send(source, block(index), "ctx", 1, 0)
        passing.append((index, up, link.send(source, block(index), "ctx", -1, 0)))

    def ring_job():
        far = []
        for number in range(8):
            yield 10.0 + 3.8 * number
            index, up, down = passing[number]
            up.wait_recv()
            if number % 2 == 0:
                far.append((index, link.send(block(index, 3), block(index, 3), "ctx", 1, 0)))
            sibs.append(link.send(block(index, 3), block(index, 3), "ctx", 0, 0, 1))
            down.wait_recv()
            if number % 2 == 1:
                far.append((index, link.send(block(index, 1), block(index, 1), "ctx", -1, 0)))
            sibs.append(link.send(block(index, 1), block(index, 1), "ctx", 0, 0, 1))
        for number, (index, copy) in enumerate(far):
            yield 38.0 + number
            copy.wait_recv()
            sibs.append(link.send(block(index, 2), block(index, 2), "ctx", 0, 0, 1))
        yield 50.0
        for copy in sibs:
            copy.wait_recv()

    def kv_job():
        yield 0.0
        copy = link.send(kv_send, kv_other, "shard", 0, 1)
        yield 9.0
        copy.wait_recv()

    run(
        gather_job(link, "shard", w_out.at[mine], lambda i: out_full.at[i, mine], share, 0.0, 4.0),
        exchange_job(link, "shard", lambda i: small, lambda i: smalls.at[i], 0.0, 9.0),
        kv_job(),
        gather_job(link, "shard", tokens, lambda i: token_rows.at[i], None, 0.1, 12.0),
        ring_job(),
    )


def qkv_kernel(link, queries, kv, queries_got, kv_all, kv_got, kv_own):
    link.greet(whole("shard") + near("ctx") + SIBLING)
    core = lax.rem(lax.axis_index("ctx"), 2)

    def kv_job():
        yield from exchange_job(link, "shard", lambda i: kv.at[i], lambda i: kv_got.at[i], 0.0, 6.0)
        for head in range(KV_HEADS):
            kv_own[:, head * 128 : (head + 1) * 128] = kv_got[2 * head] + kv_got[2 * head + 1]
        slot = lambda i: kv_all.at[i * 2 + core]
        sibs = []

        def share(index, block):
            sibs.append(link.send(block, slot(index), "ctx", 0, 0, 1))

        yield from gather_job(link, "ctx", kv_own, slot, share, 6.0, 2.7)
        for copy in sibs:
            copy.wait_recv()

    run(
        kv_job(),
        exchange_job(link, "shard", lambda i: queries.at[i], lambda i: queries_got.at[i], 0.1, 30.0),
    )


def gather_kernel(link, own, slots):
    link.greet(near("shard"))
    run(gather_job(link, "shard", own, lambda i: slots.at[i]))


REDUCE_ORDER = [(2, 1), (2, 0), (1, 1), (3, 0), (3, 1), (1, 0), (0, 1), (0, 0)]


def reduced(link, theirs, mine, from_sibling, landing, work, summed, start=0.0, block=10.8):
    columns = lambda ref, i: ref.at[:, pl.ds(pl.multiple_of(i * LANES, LANES), LANES)]
    copies = {}
    for r, p in REDUCE_ORDER:
        i = chip("ctx", r, p)
        copies[r, p] = link.send(columns(theirs, i), columns(from_sibling, i), "ctx", 0, 0, 1)
    offsets = iter(REDUCE_ORDER)

    def part(i):
        r, p = reduce_at[0]
        copies[r, p].wait_recv()
        add_rows(columns(from_sibling, i), [columns(mine, i), columns(from_sibling, i)])
        return columns(from_sibling, i)

    reduce_at = [None]

    class Parts:
        def __call__(self, i):
            reduce_at[0] = next(offsets)
            return part(i)

    yield from scatter_job(link, "ctx", Parts(), landing, work, summed, start, block)


def spread(link, summed, full, start=0.0, block=10.8):
    core = lax.rem(lax.axis_index("ctx"), 2)
    slot = lambda i: full.at[:, pl.ds(pl.multiple_of((core * 8 + i) * LANES, LANES), LANES)]
    sibs = []

    def share(index, block):
        sibs.append(link.send(block, slot(index), "ctx", 0, 0, 1))

    yield from gather_job(link, "ctx", summed, slot, share, start, block)
    for copy in sibs:
        copy.wait_recv()


def middle_kernel(link, parts, theirs, mine, result, summed, land_a, work_a, sib, land_b, work_b):
    link.greet(near("shard") + near("ctx") + SIBLING)
    run(
        scatter_job(link, "shard", lambda i: parts.at[i], land_a, work_a, result),
        reduced(link, theirs, mine, sib, land_b, work_b, summed, 4.0),
    )


def swap_lanes(values):
    width = values.shape[1]
    low_half = lax.broadcasted_iota(jnp.int32, values.shape, 1) % HEAD < 32
    return jnp.where(low_half, pltpu.roll(values, width - 32, 1), pltpu.roll(values, 32, 1))


def back_kernel(link, kv_parts, summed, hidden, queries, attended, cosine, sine,
                full, hidden_rows, query_cols, attended_cols, kv_cols,
                sib, land_k, work_k, kv_grad, kv_turned):
    link.greet(whole("shard") + near("ctx") + SIBLING)
    core = lax.rem(lax.axis_index("ctx"), 2)

    def kv_job():
        yield 0.0
        copies = [
            link.send(kv_parts.at[i * 2 + 1 - core], sib.at[i], "ctx", 0, 0, 1) for i in range(8)
        ]
        yield 3.0
        for i, copy in enumerate(copies):
            copy.wait_recv()
            add_rows(sib.at[i], [sib.at[i], kv_parts.at[i * 2 + core]])
        yield from scatter_job(link, "ctx", lambda i: sib.at[i], land_k, work_k, kv_grad, 4.0, 2.7)
        key_lanes = lax.broadcasted_iota(jnp.int32, cosine.shape, 1) < HEAD
        for head in range(KV_HEADS):
            lanes = slice(head * 128, head * 128 + 128)
            both = kv_grad[:, lanes]
            turned = both * cosine[...] - swap_lanes(both) * sine[...]
            kv_turned[:, lanes] = jnp.where(key_lanes, turned, both).astype(LOW)
        part = lambda i: kv_turned.at[:, pl.ds(pl.multiple_of(i // 2 * 128, 128), 128)]
        yield from exchange_job(link, "shard", part, lambda i: kv_cols.at[i], 26.0, 12.0)

    columns = lambda ref: lambda i: ref.at[:, pl.ds(pl.multiple_of(i * 256, 256), 256)]
    run(
        kv_job(),
        gather_job(link, "shard", hidden, lambda i: hidden_rows.at[i], None, 0.2),
        spread(link, summed, full, 5.0),
        exchange_job(link, "shard", columns(queries), lambda i: query_cols.at[i], 27.0, 20.0),
        exchange_job(link, "shard", columns(attended), lambda i: attended_cols.at[i], 27.1, 21.0),
    )


def last_kernel(link, parts, theirs, mine, gains, result, full, gain_sum,
                land_a, work_a, sib, land_b, work_b, summed, gain_land, gain_work, gain_ctx):
    link.greet(whole("shard") + whole("ctx") + SIBLING)

    def weight_job():
        yield from reduced(link, theirs, mine, sib, land_b, work_b, summed, 0.0, 3.0)
        yield from spread(link, summed, full, 24.0, 3.0)

    def gain_job():
        yield from exchange_job(link, "shard", lambda i: gains.at[i], lambda i: gain_land.at[i], 0.2, 8.0)
        gain_work[0] = sum(gain_land[i] for i in range(8))
        copy = link.send(gain_work.at[0], gain_work.at[1], "ctx", 0, 0, 1)
        yield 11.0
        copy.wait_recv()
        gain_work[2] = gain_work[0] + gain_work[1]
        copies = [
            link.send(gain_work.at[2], gain_ctx.at[i], "ctx", r, p) for i, (r, p) in enumerate(ALL)
        ]
        yield 40.0
        for copy in copies:
            copy.wait_recv()
        gain_sum[...] = gain_work[2] + sum(gain_ctx[i] for i in range(7))

    run(
        scatter_job(link, "shard", lambda i: parts.at[i], land_a, work_a, result),
        weight_job(),
        gain_job(),
    )


def first_kernel(pair_ref, tokens, gain, w_query, w_key, w_value, kv_other, cosine, sine,
                 normed_ref, q_ref, kv_ref, w_kv):
    @pl.when(pl.program_id(0) == 0)
    def _():
        leads = pair_ref[0] == 0
        nothing = jnp.zeros((32, D), LOW)
        choose = lambda yes, ref, other: jnp.where(yes, ref[...], other)
        w_kv[0:32, :] = choose(leads, w_key, nothing)
        w_kv[32:64, :] = choose(leads, kv_other, nothing)
        w_kv[64:96, :] = choose(jnp.logical_not(leads), kv_other, nothing)
        w_kv[96:128, :] = choose(jnp.logical_not(leads), w_value, nothing)

    values = tokens[...].astype(F32)
    normed = rms_forward(values, gain[...])[0].astype(LOW)
    normed_ref[...] = normed
    cosine, sine = cosine[...], sine[...]
    turn = lambda v: v * cosine + swap_lanes(v) * sine
    q = times_transposed(normed, w_query[...])
    for i in range(2):
        lanes = slice(i * 128, i * 128 + 128)
        q_ref[:, :, lanes] = turn(q[:, lanes]).astype(LOW).reshape(2, 128, 128)
    kv = times_transposed(normed, w_kv[...])
    keys = lax.broadcasted_iota(jnp.int32, kv.shape, 1) < HEAD
    kv_ref[...] = jnp.where(keys, turn(kv), kv).astype(LOW).reshape(2, 128, 128)


def first_part(pair, token_rows, gain, w_query, w_key, w_value, kv_other, cosine, sine):
    held = lambda *dims: pl.BlockSpec(dims, lambda i, *_: (0,) * len(dims))
    rows = lambda width: pl.BlockSpec((256, width), lambda i, *_: (i, 0))
    slots = lambda width: pl.BlockSpec((2, 128, width), lambda i, *_: (i, 0, 0))
    return pl.pallas_call(
        first_kernel,
        grid_spec=pltpu.PrefetchScalarGridSpec(
            num_scalar_prefetch=1,
            grid=(4,),
            in_specs=[rows(D), held(1, D), held(256, D), held(32, D), held(32, D), held(32, D), rows(128), rows(128)],
            out_specs=[rows(D), slots(256), slots(128)],
            scratch_shapes=[pltpu.VMEM((128, D), LOW)],
        ),
        out_shape=[shape((1024, D), LOW), shape((8, 128, 256), LOW), shape((8, 128, 128), LOW)],
        compiler_params=pltpu.CompilerParams(vmem_limit_bytes=VMEM_LIMIT),
        cost_estimate=pl.CostEstimate(flops=1 << 31, bytes_accessed=10 << 20, transcendentals=1024),
    )(pair, token_rows, gain, w_query, w_key, w_value, kv_other, cosine, sine)


BLOCK = 256
LOG2E = 1.4426950408889634


def sort_keys(order_ref, kv_ref, sorted_ref, flipped_ref):
    for c in range(16):
        lead = pl.multiple_of(order_ref[c] * 64, 64)
        trail = pl.multiple_of((31 - order_ref[c]) * 64, 64)
        sorted_ref[pl.ds(lead, 64), :] = kv_ref[c, 0:64, :]
        sorted_ref[pl.ds(trail, 64), :] = kv_ref[c, 64:128, :]
    for i in range(8):
        rows = slice(i * BLOCK, (i + 1) * BLOCK)
        flipped_ref[i] = jnp.transpose(sorted_ref[rows, :].astype(F32)).astype(LOW)


def spread_heads(blocks, high):
    pieces = []
    for block in blocks:
        block = block.astype(F32)
        turned = pltpu.roll(block, 64, 1)
        lane = lax.broadcasted_iota(jnp.int32, block.shape, 1)
        keep = (lane >= 64) if high else (lane < 64)
        first, second = (turned, block) if high else (block, turned)
        pieces += [jnp.where(keep, first, 0.0), jnp.where(keep, second, 0.0)]
    return jnp.concatenate(pieces, axis=0)


def join_heads(flipped):
    upright = jnp.transpose(flipped)
    return [
        jnp.concatenate([upright[i * 128 : i * 128 + 64], upright[i * 128 + 64 : i * 128 + 128]], axis=1)
        for i in range(4)
    ]


def query_blocks(ref, run):
    rows = slice(run * 64, run * 64 + 64)
    return [ref[s, rows, p * 128 : p * 128 + 128] for s in range(2) for p in range(2)]


def row_blocks(ref, run):
    rows = slice(run * 64, run * 64 + 64)
    return [ref[rows, i * 128 : i * 128 + 128] for i in range(4)]


def above(block, first_place):
    key = lax.broadcasted_iota(jnp.int32, (BLOCK, 512), 0) + block * BLOCK
    query = lax.broadcasted_iota(jnp.int32, (BLOCK, 512), 1) % 64 + first_place
    return key > query


def dot_kt(left, right):
    return lax.dot_general(left, right, (((1,), (1,)), ((), ())), preferred_element_type=F32)


def attend_kernel(order_ref, own_ref, q_ref, kv_ref, out_ref, lse_ref, sorted_ref, flipped_ref):
    sort_keys(order_ref, kv_ref, sorted_ref, flipped_ref)
    factor = HEAD**-0.5 * LOG2E
    for run in range(2):
        first_place = jnp.where(run == 0, own_ref[0], 31 - own_ref[0]) * 64
        last = first_place // BLOCK
        q = spread_heads(query_blocks(q_ref, run), False).astype(LOW)

        def step(block, carry, masked):
            largest, total, mixed = carry
            rows = pl.ds(pl.multiple_of(block * BLOCK, BLOCK), BLOCK)
            scores = dot_kt(sorted_ref[rows, :], q) * factor
            if masked:
                scores = jnp.where(above(block, first_place), NEG, scores)
            top = jnp.maximum(largest, jnp.max(scores, axis=0, keepdims=True))
            fade = jnp.exp2(largest - top)
            exps = jnp.exp2(scores - top)
            total = total * fade + jnp.sum(exps, axis=0, keepdims=True)
            mixed = mixed * fade + times(flipped_ref[block, 64:128, :], exps.astype(LOW))
            return top, total, mixed

        carry = (jnp.full((1, 512), NEG, F32), jnp.zeros((1, 512), F32), jnp.zeros((64, 512), F32))
        carry = lax.fori_loop(0, last, functools.partial(step, masked=False), carry)
        largest, total, mixed = step(last, carry, True)
        for i, block in enumerate(join_heads(mixed / total)):
            out_ref[run * 64 : run * 64 + 64, i * 128 : i * 128 + 128] = block.astype(LOW)
        lse_ref[0, run : run + 1, :] = largest + jnp.log2(total)


def attend_back_kernel(order_ref, own_ref, q_ref, kv_ref, out_ref, grad_ref, lse_ref, cos_ref, sin_ref,
                       dq_ref, dkv_ref, sorted_ref, flipped_ref, total_ref):
    sort_keys(order_ref, kv_ref, sorted_ref, flipped_ref)
    total_ref[...] = jnp.zeros_like(total_ref)
    scale = HEAD**-0.5
    factor = scale * LOG2E
    for run in range(2):
        first_place = jnp.where(run == 0, own_ref[0], 31 - own_ref[0]) * 64
        last = first_place // BLOCK
        q = spread_heads(query_blocks(q_ref, run), False).astype(LOW)
        grad_wide = spread_heads(row_blocks(grad_ref, run), True)
        out_wide = spread_heads(row_blocks(out_ref, run), True)
        grad = grad_wide.astype(LOW)
        inner = lax.dot_general(
            jnp.ones((8, 128), F32),
            grad_wide * out_wide,
            (((1,), (1,)), ((), ())),
            precision=lax.Precision.HIGHEST,
            preferred_element_type=F32,
        )[:1]
        lse = lse_ref[0, run : run + 1, :]

        def step(block, dq, masked):
            rows = pl.ds(pl.multiple_of(block * BLOCK, BLOCK), BLOCK)
            kv = sorted_ref[rows, :]
            probs = jnp.exp2(dot_kt(kv, q) * factor - lse)
            if masked:
                probs = jnp.where(above(block, first_place), 0.0, probs)
            score_grad = (probs * (dot_kt(kv, grad) - inner)).astype(LOW)
            total_ref[rows, :] += times(score_grad, q) + times(probs.astype(LOW), grad)
            return dq + times(flipped_ref[block, 0:64, :], score_grad)

        dq = lax.fori_loop(0, last, functools.partial(step, masked=False), jnp.zeros((64, 512), F32))
        dq = step(last, dq, True)
        cosine, sine = cos_ref[run * 64 : run * 64 + 64, :], sin_ref[run * 64 : run * 64 + 64, :]
        low_half = lax.broadcasted_iota(jnp.int32, (64, 128), 1) % 64 < 32
        for i, block in enumerate(join_heads(dq * scale)):
            turned = jnp.where(low_half, pltpu.roll(block, 96, 1), pltpu.roll(block, 32, 1))
            dq_ref[run * 64 : run * 64 + 64, i * 128 : i * 128 + 128] = (
                block * cosine - turned * sine
            ).astype(LOW)
    weight = jnp.where(lax.broadcasted_iota(jnp.int32, (64, 128), 1) < 64, scale, 1.0)
    for c in range(16):
        lead = pl.multiple_of(order_ref[c] * 64, 64)
        trail = pl.multiple_of((31 - order_ref[c]) * 64, 64)
        dkv_ref[c, 0:64, :] = (total_ref[pl.ds(lead, 64), :] * weight).astype(LOW)
        dkv_ref[c, 64:128, :] = (total_ref[pl.ds(trail, 64), :] * weight).astype(LOW)


def attention_call(kernel, scalars, inputs, kinds, outputs, out_kinds, scratch, flops):
    specs = {
        "q": pl.BlockSpec((2, 128, 256), lambda g, *_: (g, 0, 0)),
        "kv": pl.BlockSpec((16, 128, 128), lambda g, *_: (0, 0, g)),
        "rows": pl.BlockSpec((128, 512), lambda g, *_: (0, g)),
        "lse": pl.BlockSpec((1, 8, 512), lambda g, *_: (g, 0, 0)),
        "table": pl.BlockSpec((128, 128), lambda g, *_: (0, 0)),
    }
    keys = [pltpu.VMEM((2048, 128), LOW), pltpu.VMEM((8, 128, BLOCK), LOW)]
    return pl.pallas_call(
        kernel,
        grid_spec=pltpu.PrefetchScalarGridSpec(
            num_scalar_prefetch=2,
            grid=(KV_HEADS,),
            in_specs=[specs[k] for k in kinds],
            out_specs=[specs[k] for k in out_kinds],
            scratch_shapes=keys + scratch,
        ),
        out_shape=outputs,
        compiler_params=pltpu.CompilerParams(vmem_limit_bytes=VMEM_LIMIT),
        cost_estimate=pl.CostEstimate(flops=flops, bytes_accessed=8 << 20, transcendentals=8 << 20),
    )(*scalars, *inputs)


def attend(queries, kv_all, order, own):
    return attention_call(
        attend_kernel,
        (order, own),
        (queries, kv_all),
        ("q", "kv"),
        [jax.ShapeDtypeStruct((128, D), LOW), jax.ShapeDtypeStruct((4, 8, 512), F32)],
        ("rows", "lse"),
        [],
        1 << 33,
    )


def attend_back(queries, kv_all, attended, attended_grad, lse, cosine, sine, order, own):
    return attention_call(
        attend_back_kernel,
        (order, own),
        (queries, kv_all, attended, attended_grad, lse, cosine, sine),
        ("q", "kv", "rows", "rows", "lse", "table", "table"),
        [jax.ShapeDtypeStruct((128, D), LOW), jax.ShapeDtypeStruct((16, 128, 512), LOW)],
        ("rows", "kv"),
        [pltpu.VMEM((2048, 128), F32)],
        1 << 34,
    )


def local(
    tokens,
    positions,
    out_grad,
    attn_gain,
    w_query,
    w_key,
    w_value,
    w_out,
    ffn_gain,
    w_gate,
    w_up,
    w_down,
):
    rows = tokens.shape[0]
    shard, ctx = lax.axis_index("shard"), lax.axis_index("ctx")
    shard_pair, core = shard % 2, ctx % 2
    places = positions[0]
    own_places = lax.dynamic_slice_in_dim(places, ctx * rows, rows)
    blocks = lambda m: m.reshape(8, rows, -1)

    small = jnp.stack(
        [attn_gain, ffn_gain, jnp.concatenate([own_places // 64, own_places % 64]).astype(LOW)]
    )
    small = jnp.concatenate([small, jnp.zeros((13, 256), LOW)], axis=0)
    token_rows, smalls, kv_other, out_full = comm_call(
        front_kernel,
        0,
        [tokens, small, jnp.where(shard_pair == 0, w_value, w_key), w_out],
        [ANY] * 4,
        [shape((8, rows, D), LOW), shape((8, 16, 256), LOW), shape((32, D), LOW), shape((8, 256, D), LOW)],
        [ANY] * 4,
    )
    out_grad_late, token_rows = lax.optimization_barrier((out_grad, token_rows))
    out_grad_rows = lax.all_gather(out_grad_late, "shard", axis=0, tiled=True)
    token_rows, out_full = token_rows.reshape(-1, D), out_full.reshape(D, D)
    gain_one = smalls[:, 0].reshape(-1).astype(F32)
    gain_two = smalls[:, 1].reshape(-1).astype(F32)
    place_rows = (smalls[:, 2, :rows].astype(F32) * 64.0 + smalls[:, 2, rows:].astype(F32)).reshape(-1)
    cosine, sine = wide_tables(place_rows, 2)
    inputs_rows = token_rows.astype(F32)
    normed_rows, queries, kv_part = first_part(
        shard_pair[None], token_rows, gain_one[None], w_query, w_key, w_value, kv_other, cosine, sine
    )
    queries, kv_all = comm_call(
        qkv_kernel,
        1,
        [queries, kv_part],
        [ANY] * 2,
        [shape((8, rows, 256), LOW), shape((16, rows, 512), LOW)],
        [ANY] * 2,
        [pltpu.VMEM((8, rows, 128), LOW), pltpu.VMEM((rows, 512), LOW)],
    )

    order = places.reshape(16, rows)[:, 0] // 64
    own_order = own_places[:1] // 64
    attended, lse = attend(queries, kv_all, order, own_order)

    inputs = tokens.astype(F32)
    hidden_state = inputs + times(attended, out_full)
    normed_two, inverse_two = rms_forward(hidden_state, gain_two)
    (normed_two_rows,) = comm_call(
        gather_kernel, 2, [normed_two.astype(LOW)], [ANY], [shape((8, rows, D), LOW)], [ANY]
    )
    normed_two_rows = normed_two_rows.reshape(-1, D)

    gate = times_transposed(normed_two_rows, w_gate)
    up_part = times_transposed(normed_two_rows, w_up)
    inner_grad = times_transposed(out_grad_rows, w_down)
    sigmoid = jax.nn.sigmoid(gate)
    activated = gate * sigmoid
    inner = (activated * up_part).astype(LOW)
    gate_grad = (inner_grad * up_part * sigmoid * (1.0 + gate * (1.0 - sigmoid))).astype(LOW)
    up_grad = (inner_grad * activated).astype(LOW)
    normed_two_parts = (times(gate_grad, w_gate) + times(up_grad, w_up)).astype(LOW)
    down_parts = times(inner, w_down).astype(LOW)

    def halves(terms):
        def one(which):
            cut = lambda m: lax.dynamic_slice_in_dim(m, which * 1024, 1024, axis=1)
            return jnp.concatenate(
                [transposed_times(left, cut(right)).astype(LOW) for left, right in terms], axis=0
            )

        return one(1 - core), one(core)

    ff = w_gate.shape[0]
    theirs, mine = halves(
        [(gate_grad, normed_two_rows), (up_grad, normed_two_rows), (inner, out_grad_rows)]
    )
    vmem = lambda count, *dims: pltpu.VMEM((count, *dims), LOW)
    normed_two_grad, summed = comm_call(
        middle_kernel,
        3,
        [blocks(normed_two_parts), theirs, mine],
        [INSIDE, ANY, INSIDE],
        [shape((rows, D), F32), shape((3 * ff, LANES), LOW)],
        [INSIDE, INSIDE],
        [
            vmem(7, rows, D),
            vmem(3, rows, D),
            pltpu.VMEM((3 * ff, 1024), LOW),
            vmem(7, 3 * ff, LANES),
            vmem(3, 3 * ff, LANES),
        ],
    )

    down_sum = lax.psum_scatter(down_parts, "shard", scatter_dimension=0, tiled=True)
    outputs = (hidden_state + down_sum.astype(F32)).astype(LOW)
    gain_two_part = jnp.sum(normed_two_grad * hidden_state * inverse_two, axis=0)
    hidden_grad = out_grad.astype(F32) + rms_backward(
        hidden_state, inverse_two, gain_two, normed_two_grad
    )
    hidden_low = hidden_grad.astype(LOW)
    attended_grad = times_transposed(hidden_low, out_full).astype(LOW)
    own_table = lambda table: lax.dynamic_slice_in_dim(table, shard * rows, rows)
    cosine_own, sine_own = own_table(cosine), own_table(sine)
    query_pre_grad, kv_parts = attend_back(
        queries, kv_all, attended, attended_grad, lse, cosine_own, sine_own, order, own_order
    )
    ffn_full, hidden_rows, query_cols, attended_cols, kv_cols = comm_call(
        back_kernel,
        4,
        [kv_parts, summed, hidden_low, query_pre_grad, attended, cosine_own, sine_own],
        [INSIDE, INSIDE, ANY, ANY, ANY, INSIDE, INSIDE],
        [
            shape((3 * ff, D), LOW),
            shape((8, rows, D), LOW),
            shape((8, rows, 256), LOW),
            shape((8, rows, 256), LOW),
            shape((8, rows, 128), LOW),
        ],
        [ANY] * 5,
        [
            vmem(8, rows, 512),
            vmem(7, rows, 512),
            vmem(3, rows, 512),
            pltpu.VMEM((rows, 512), F32),
            pltpu.VMEM((rows, 512), LOW),
        ],
    )
    hidden_rows = hidden_rows.reshape(-1, D)
    gate_wgrad, up_wgrad, down_wgrad = (
        ffn_full[i * ff : (i + 1) * ff].astype(F32) for i in range(3)
    )
    query_cols, attended_cols = query_cols.reshape(-1, 256), attended_cols.reshape(-1, 256)
    kv_cols = kv_cols.reshape(-1, 128)
    nothing = jnp.zeros((32, D), LOW)
    kv_weights = jnp.where(
        shard_pair == 0,
        jnp.concatenate([w_key, nothing, w_value, nothing], axis=0),
        jnp.concatenate([nothing, w_key, nothing, w_value], axis=0),
    )
    kv_mine = jnp.where(
        shard_pair == 0,
        jnp.concatenate([kv_cols[:, :32], kv_cols[:, 64:96]], axis=1),
        jnp.concatenate([kv_cols[:, 32:64], kv_cols[:, 96:]], axis=1),
    )
    normed_parts = times(query_cols, w_query) + times(kv_cols, kv_weights)
    gain_one_part = jnp.sum(normed_parts * inputs_rows * inverse_of(inputs_rows), axis=0)
    theirs, mine = halves(
        [(query_cols, normed_rows), (kv_mine, normed_rows), (attended_cols, hidden_rows)]
    )
    gains = jnp.stack([gain_one_part, gain_two_part]).reshape(2, 8, 256).transpose(1, 0, 2)
    gains = jnp.concatenate([gains, jnp.zeros((8, 6, 256), F32)], axis=1)
    normed_grad, attn_full, gain_sum = comm_call(
        last_kernel,
        6,
        [blocks(normed_parts.astype(LOW)), theirs, mine, gains],
        [INSIDE, ANY, INSIDE, INSIDE],
        [shape((rows, D), F32), shape((576, D), LOW), shape((8, 256), F32)],
        [INSIDE, ANY, INSIDE],
        [
            vmem(7, rows, D),
            vmem(3, rows, D),
            pltpu.VMEM((576, 1024), LOW),
            vmem(7, 576, LANES),
            vmem(3, 576, LANES),
            pltpu.VMEM((576, LANES), LOW),
            pltpu.VMEM((8, 8, 256), F32),
            pltpu.VMEM((3, 8, 256), F32),
            pltpu.VMEM((7, 8, 256), F32),
        ],
    )
    inverse_one = inverse_of(inputs)
    input_grad = hidden_grad + rms_backward(inputs, inverse_one, gain_one, normed_grad)
    query_wgrad, key_wgrad, value_wgrad, out_wgrad = (
        attn_full[a:b].astype(F32) for a, b in ((0, 256), (256, 288), (288, 320), (320, 576))
    )
    return (
        outputs,
        input_grad,
        gain_sum[0],
        query_wgrad,
        key_wgrad,
        value_wgrad,
        out_wgrad,
        gain_sum[1],
        gate_wgrad,
        up_wgrad,
        down_wgrad,
    )


def solution(mesh):
    rows = P(("shard", "ctx"), None)
    matrix = P("shard", None)
    vector = P("shard")
    in_specs = (rows, matrix, rows, vector, matrix, matrix, matrix, matrix, vector) + (matrix,) * 3
    out_specs = (rows, rows, vector, matrix, matrix, matrix, matrix, vector) + (matrix,) * 3
    return jax.shard_map(local, mesh=mesh, in_specs=in_specs, out_specs=out_specs, check_vma=False)
```

```python
import functools

import jax
import jax.numpy as jnp
from jax import lax
from jax.experimental import pallas as pl
from jax.experimental.pallas import tpu as pltpu
from jax.sharding import PartitionSpec as P

D = 2048
HEADS = 32
KV_HEADS = 4
HEAD = 64
LANES = 128

EPS = 1e-05
BASE = 10000.0
NEG = -1e30
F32 = jnp.float32
LOW = jnp.bfloat16
MESH = pl.DeviceIdType.MESH
VMEM_LIMIT = 56 * 1024 * 1024


def times(left, right):
    return jnp.dot(left, right, preferred_element_type=F32)


def times_transposed(left, right):
    return lax.dot_general(left, right, (((1,), (1,)), ((), ())), preferred_element_type=F32)


def transposed_times(left, right):
    return lax.dot_general(left, right, (((0,), (0,)), ((), ())), preferred_element_type=F32)


def rope_tables(places, width):
    half = width // 2
    freqs = BASE ** (-(jnp.arange(half).astype(F32) * 2.0 / width))
    angles = places.astype(F32)[:, None] * freqs[None, :]
    return jnp.cos(angles), jnp.sin(angles)


def wide_tables(places, heads):
    cosine, sine = rope_tables(places, HEAD)
    return (
        jnp.tile(jnp.concatenate([cosine, cosine], axis=1), (1, heads)),
        jnp.tile(jnp.concatenate([-sine, sine], axis=1), (1, heads)),
    )


def inverse_of(values):
    return lax.rsqrt(jnp.mean(values * values, axis=-1, keepdims=True) + EPS)


def rms_forward(values, gain):
    inverse = inverse_of(values)
    return (values * inverse * gain, inverse)


def rms_backward(values, inverse, gain, grads):
    scaled = grads * gain
    return inverse * scaled - values * inverse * inverse * inverse * jnp.mean(
        scaled * values, axis=-1, keepdims=True
    )


def at(axis, ring, pair, core=0):
    index = lax.axis_index(axis)
    cores = 2 if axis == "ctx" else 1
    ring_at = lax.rem(index // (2 * cores) + ring % 4, 4)
    pair_at = lax.rem(lax.rem(index // cores, 2) + pair, 2)
    core_at = lax.rem(lax.rem(index, cores) + core, cores)
    return (ring_at * 2 + pair_at) * cores + core_at


def chip(axis, ring=0, pair=0):
    return at(axis, ring, pair) // (2 if axis == "ctx" else 1)


class Link:
    def __init__(self, send_sems, recv_sems, local_sems):
        self.send_sems, self.recv_sems, self.local_sems = send_sems, recv_sems, local_sems
        self.sent, self.kept = [], []

    def greet(self, offsets):
        barrier = pltpu.get_barrier_semaphore()
        for axis, ring, pair, core in offsets:
            pl.semaphore_signal(
                barrier, inc=1, device_id={axis: at(axis, ring, pair, core)}, device_id_type=MESH
            )
        pl.semaphore_wait(barrier, len(offsets))

    def send(self, source, target, axis, ring, pair, core=0):
        number = len(self.sent)
        copy = pltpu.make_async_remote_copy(
            src_ref=source,
            dst_ref=target,
            send_sem=self.send_sems.at[number],
            recv_sem=self.recv_sems.at[number],
            device_id={axis: at(axis, ring, pair, core)},
            device_id_type=MESH,
        )
        copy.start()
        self.sent.append(copy)
        return copy

    def keep(self, source, target):
        copy = pltpu.make_async_copy(source, target, self.local_sems.at[len(self.kept)])
        copy.start()
        self.kept.append(copy)
        return copy

    def kept_now(self, copy):
        copy.wait()
        self.kept = [None if other is copy else other for other in self.kept]

    def finish(self):
        for copy in self.kept:
            if copy is not None:
                copy.wait()
        for copy in self.sent:
            copy.wait_send()


NEAR = [(1, 0), (3, 0), (0, 1)]
ALL = [(r, p) for r in range(4) for p in range(2) if (r, p) != (0, 0)]
near = lambda axis: [(axis, r, p, 0) for r, p in NEAR]
whole = lambda axis: [(axis, r, p, 0) for r, p in ALL]
SIBLING = [("ctx", 0, 0, 1)]


def run(*jobs):
    waiting = [(next(job), number, job) for number, job in enumerate(jobs)]
    while waiting:
        waiting.sort(key=lambda entry: entry[:2])
        _, number, job = waiting.pop(0)
        after = next(job, None)
        if after is not None:
            waiting.append((after, number, job))


def gather_job(link, axis, own, slot, share=None, start=0.0, block=10.5):
    me, pair = chip(axis), chip(axis, 0, 1)
    sharing = lambda index: share(index, slot(index)) if share else None
    yield start
    kept = link.keep(own, slot(me))
    to_pair = link.send(own, slot(me), axis, 0, 1)
    down = link.send(own, slot(me), axis, -1, 0)
    up = link.send(own, slot(me), axis, 1, 0)
    if share:
        share(me, own)
    yield start + block + 3.0
    to_pair.wait_recv()
    pair_down = link.send(slot(pair), slot(pair), axis, -1, 0)
    pair_up = link.send(slot(pair), slot(pair), axis, 1, 0)
    sharing(pair)
    yield start + block + 3.1
    down.wait_recv()
    next_one = chip(axis, 1, 0)
    far_down = link.send(slot(next_one), slot(next_one), axis, -1, 0)
    sharing(next_one)
    yield start + block + 3.2
    up.wait_recv()
    sharing(chip(axis, -1, 0))
    yield start + 2 * block + 4.0
    pair_up.wait_recv()
    last_pair = chip(axis, -1, 1)
    far_up = link.send(slot(last_pair), slot(last_pair), axis, 1, 0)
    sharing(last_pair)
    yield start + 2 * block + 4.1
    pair_down.wait_recv()
    sharing(chip(axis, 1, 1))
    yield start + 3 * block + 5.0
    far_down.wait_recv()
    sharing(chip(axis, 2, 0))
    yield start + 3 * block + 5.1
    far_up.wait_recv()
    sharing(chip(axis, 2, 1))
    link.kept_now(kept)


def gather_halves(link, axis, own, slot, share=None, start=0.0, block=10.5):
    half = own.shape[0] // 2
    cut = lambda ref, k: ref.at[pl.ds(k * half, half)]
    piece = lambda index, k: cut(slot(index), k)
    me, pair, far = chip(axis), chip(axis, 0, 1), chip(axis, 2, 0)
    above_one, below_one = chip(axis, 1, 0), chip(axis, -1, 0)
    last_pair, next_pair, far_pair = chip(axis, -1, 1), chip(axis, 1, 1), chip(axis, 2, 1)
    sharing = lambda index, k: share(piece(index, k), index, k) if share else None
    pass_on = lambda index, k, ring, pair_: link.send(piece(index, k), piece(index, k), axis, ring, pair_)
    yield start
    kept = link.keep(own, slot(me))
    across, down, up = [], [], []
    for k in range(2):
        across.append(link.send(cut(own, k), piece(me, k), axis, 0, 1))
        down.append(link.send(cut(own, k), piece(me, k), axis, -1, 0))
        up.append(link.send(cut(own, k), piece(me, k), axis, 1, 0))
    if share:
        for k in range(2):
            share(cut(own, k), me, k)
    far_in, pair_up, pair_down, over = [], [], [], []
    for k in range(2):
        yield start + (k + 1) * block / 2 + 3.5
        down[k].wait_recv()
        up[k].wait_recv()
        far_in.append(pass_on(above_one, k, -1, 0) if k == 0 else pass_on(below_one, k, 1, 0))
        sharing(above_one, k)
        sharing(below_one, k)
        across[k].wait_recv()
        pair_up.append(pass_on(pair, k, 1, 0))
        pair_down.append(pass_on(pair, k, -1, 0))
        sharing(pair, k)
    link.kept_now(kept)
    for k in range(2):
        yield start + block + 7.0 + k * block / 2
        far_in[k].wait_recv()
        over.append(pass_on(far, k, 0, 1))
        sharing(far, k)
    yield start + 2.5 * block + 6.0
    for k in range(2):
        pair_up[k].wait_recv()
        sharing(last_pair, k)
        pair_down[k].wait_recv()
        sharing(next_pair, k)
    yield start + 2.5 * block + 9.0
    for k in range(2):
        over[k].wait_recv()
        sharing(far_pair, k)


def add_rows(target, terms):
    rows, width = target.shape
    step = max(s for s in range(16, rows + 1, 16) if rows % s == 0 and (s == 16 or s * width <= 32768))

    def body(i, _):
        some = pl.ds(pl.multiple_of(i * step, 16), step)
        total = terms[0][some, :].astype(F32)
        for term in terms[1:]:
            total = total + term[some, :].astype(F32)
        target[some, :] = total.astype(target.dtype)
        return 0

    lax.fori_loop(0, rows // step, body, 0)


def scatter_job(link, axis, part, landing, work, result, start=0.0, block=10.5):
    here = lambda ring, pair: part(chip(axis, ring, pair))
    yield start
    to_last = link.send(here(2, 1), landing.at[1], axis, -1, 0)
    to_next = link.send(here(2, 0), landing.at[0], axis, 1, 0)
    pair_up = link.send(here(1, 1), landing.at[2], axis, 1, 0)
    yield start + block + 3.0
    to_last.wait_recv()
    add_rows(work.at[0], [here(3, 1), landing.at[1]])
    pair_down = link.send(work.at[0], landing.at[4], axis, -1, 0)
    yield start + block + 4.0
    to_next.wait_recv()
    add_rows(work.at[1], [here(1, 0), landing.at[0]])
    yield start + 2 * block + 3.0
    pair_up.wait_recv()
    mine_up = link.send(work.at[1], landing.at[5], axis, 1, 0)
    mine_down = link.send(here(3, 0), landing.at[3], axis, -1, 0)
    yield start + 2 * block + 6.0
    pair_down.wait_recv()
    add_rows(work.at[2], [here(0, 1), landing.at[2], landing.at[4]])
    across = link.send(work.at[2], landing.at[6], axis, 0, 1)
    yield start + 3 * block + 7.0
    mine_down.wait_recv()
    mine_up.wait_recv()
    yield start + 3 * block + 10.0
    across.wait_recv()
    add_rows(result, [here(0, 0), landing.at[3], landing.at[5], landing.at[6]])


def exchange_job(link, axis, part, slot, start=0.0, length=8.0):
    me = chip(axis)
    yield start
    kept = link.keep(part(me), slot(me))
    copies = [link.send(part(chip(axis, r, p)), slot(me), axis, r, p) for r, p in ALL]
    yield start + length
    for copy in copies:
        copy.wait_recv()
    link.kept_now(kept)


ANY = pl.BlockSpec(memory_space=pl.ANY)
INSIDE = pl.BlockSpec(memory_space=pltpu.VMEM)


def comm_call(kernel, number, inputs, in_specs, outputs, out_specs, scratch=(), limit=VMEM_LIMIT):
    sems = [pltpu.SemaphoreType.DMA((96,)), pltpu.SemaphoreType.DMA((96,)), pltpu.SemaphoreType.DMA((8,))]

    def body(*refs):
        link = Link(*refs[-3:])
        kernel(link, *refs[:-3])
        link.finish()

    return pl.pallas_call(
        body,
        out_shape=outputs,
        in_specs=in_specs,
        out_specs=out_specs,
        scratch_shapes=[*scratch, *sems],
        compiler_params=pltpu.CompilerParams(
            collective_id=number, has_side_effects=True, vmem_limit_bytes=limit
        ),
    )(*inputs)


shape = jax.ShapeDtypeStruct


def front_kernel(link, tokens, small, kv_send, w_out, token_rows, smalls, kv_other, out_full):
    link.greet(whole("shard") + [("ctx", 1, 0, 0), ("ctx", 3, 0, 0)] + SIBLING)
    core = lax.rem(lax.axis_index("ctx"), 2)
    ring = lax.axis_index("ctx") // 4

    def block(index, ring_further=0):
        at_ring = lax.rem(ring + ring_further, 4)
        rows = pl.ds(pl.multiple_of((core * 4 + at_ring) * 32, 32), 32)
        return out_full.at[index, rows]

    mine = pl.ds(pl.multiple_of((core * 4 + ring) * 32, 32), 32)
    passing, sibs = [], []

    def share(index, source):
        sibs.append(link.send(source, block(index), "ctx", 0, 0, 1))
        up = link.send(source, block(index), "ctx", 1, 0)
        passing.append((index, up, link.send(source, block(index), "ctx", -1, 0)))

    def ring_job():
        far = []
        for number in range(8):
            yield 10.0 + 3.8 * number
            index, up, down = passing[number]
            up.wait_recv()
            if number % 2 == 0:
                far.append((index, link.send(block(index, 3), block(index, 3), "ctx", 1, 0)))
            sibs.append(link.send(block(index, 3), block(index, 3), "ctx", 0, 0, 1))
            down.wait_recv()
            if number % 2 == 1:
                far.append((index, link.send(block(index, 1), block(index, 1), "ctx", -1, 0)))
            sibs.append(link.send(block(index, 1), block(index, 1), "ctx", 0, 0, 1))
        for number, (index, copy) in enumerate(far):
            yield 38.0 + number
            copy.wait_recv()
            sibs.append(link.send(block(index, 2), block(index, 2), "ctx", 0, 0, 1))
        yield 50.0
        for copy in sibs:
            copy.wait_recv()

    def kv_job():
        yield 0.0
        copy = link.send(kv_send, kv_other, "shard", 0, 1)
        yield 9.0
        copy.wait_recv()

    run(
        gather_job(link, "shard", w_out.at[mine], lambda i: out_full.at[i, mine], share, 0.0, 4.0),
        exchange_job(link, "shard", lambda i: small, lambda i: smalls.at[i], 0.0, 9.0),
        kv_job(),
        gather_halves(link, "shard", tokens, lambda i: token_rows.at[i], None, 0.1, 12.0),
        ring_job(),
    )


def qkv_kernel(link, queries, kv, queries_got, kv_all, kv_got, kv_own):
    link.greet(whole("shard") + near("ctx") + SIBLING)
    core = lax.rem(lax.axis_index("ctx"), 2)

    def kv_job():
        yield from exchange_job(link, "shard", lambda i: kv.at[i], lambda i: kv_got.at[i], 0.0, 6.0)
        for head in range(KV_HEADS):
            kv_own[:, head * 128 : (head + 1) * 128] = kv_got[2 * head] + kv_got[2 * head + 1]
        slot = lambda i: kv_all.at[i * 2 + core]
        sibs = []

        def share(index, block):
            sibs.append(link.send(block, slot(index), "ctx", 0, 0, 1))

        yield from gather_job(link, "ctx", kv_own, slot, share, 6.0, 2.7)
        for copy in sibs:
            copy.wait_recv()

    run(
        kv_job(),
        exchange_job(link, "shard", lambda i: queries.at[i], lambda i: queries_got.at[i], 0.1, 30.0),
    )


def column_block(ref, index, width=LANES):
    return ref.at[:, pl.ds(pl.multiple_of(index * width, width), width)]


def reduced(link, theirs, mine, from_sibling, landing, work, summed, start=0.0, block=10.8):
    copy = link.send(theirs, from_sibling, "ctx", 0, 0, 1)
    yield start
    copy.wait_recv()
    add_rows(from_sibling, [mine, from_sibling])
    part = lambda i: column_block(from_sibling, i)
    yield from scatter_job(link, "ctx", part, landing, work, summed, start + 2.0, block)


def spread(link, summed, full, gather, start=0.0, block=10.8):
    core = lax.rem(lax.axis_index("ctx"), 2)
    slot = lambda i: column_block(full, core * 8 + i)
    sibs = []

    def share(index, source):
        sibs.append(link.send(source, slot(index), "ctx", 0, 0, 1))

    def share_half(source, index, k):
        half = source.shape[0]
        sibs.append(link.send(source, slot(index).at[pl.ds(k * half, half)], "ctx", 0, 0, 1))

    yield from gather(link, "ctx", summed, slot, share if gather is gather_job else share_half, start, block)
    for copy in sibs:
        copy.wait_recv()


def contract_rows(left, right):
    return lax.dot_general(left, right, (((0,), (0,)), ((), ())), preferred_element_type=F32)


def ffn_kernel(link, own, og, w_gate, w_up, w_down, result, down_parts, summed,
               rows_all, gate_t, up_t, inner_t, parts, land_a, work_a, theirs, sib, land_b, work_b):
    link.greet(near("shard") + near("ctx") + SIBLING)
    core = lax.rem(lax.axis_index("ctx"), 2)
    count = own.shape[0]
    ff = w_gate.shape[0]
    here = lambda ref, i: ref.at[pl.ds(pl.multiple_of(i * count, count), count)]
    token_lanes = lambda i: pl.ds(pl.multiple_of(i * count, count), count)

    def pair_of(ref, slots):
        return jnp.concatenate([here(ref, i)[...] for i in slots], axis=0)

    def forward(*offsets):
        slots = [chip("shard", r, p) for r, p in offsets]
        x = pair_of(rows_all, slots)
        gate = times_transposed(w_gate[...], x)
        up = times_transposed(w_up[...], x)
        inner_grad = times_transposed(w_down[...], pair_of(og, slots))
        sigmoid = 1.0 / (1.0 + jnp.exp(-gate))
        activated = gate * sigmoid
        inner = (activated * up).astype(LOW)
        gate_grad = (inner_grad * up * sigmoid * (1.0 + gate * (1.0 - sigmoid))).astype(LOW)
        up_grad = (inner_grad * activated).astype(LOW)
        for k, i in enumerate(slots):
            lanes = slice(k * count, k * count + count)
            inner_t[:, token_lanes(i)] = inner[:, lanes]
            gate_t[:, token_lanes(i)] = gate_grad[:, lanes]
            up_t[:, token_lanes(i)] = up_grad[:, lanes]
        return slots

    def tokens_of(ref, slots):
        return jnp.concatenate([ref[:, token_lanes(i)] for i in slots], axis=1)

    def back(slots):
        gates, ups = tokens_of(gate_t, slots), tokens_of(up_t, slots)
        for c in range(2):
            some = slice(c * 1024, c * 1024 + 1024)
            block = contract_rows(gates, w_gate[:, some]) + contract_rows(ups, w_up[:, some])
            for k, i in enumerate(slots):
                parts[i, :, some] = block[k * count : k * count + count].astype(LOW)

    def down(slots):
        inners = tokens_of(inner_t, slots)
        for c in range(2):
            some = slice(c * 1024, c * 1024 + 1024)
            block = contract_rows(inners, w_down[:, some])
            for k, i in enumerate(slots):
                down_parts[i, :, some] = block[k * count : k * count + count].astype(LOW)

    def every(*offsets):
        slots = forward(*offsets)
        back(slots)
        down(slots)

    last_pair_slots = []

    def compute_job():
        yield 15.0
        every((0, 0), (0, 1))
        yield 21.5
        every((1, 0), (3, 0))
        yield 33.0
        every((2, 0), (1, 1))
        yield 36.0
        slots = forward((3, 1), (2, 1))
        back(slots)
        last_pair_slots.append(slots)

    run(
        gather_halves(link, "shard", own, lambda i: here(rows_all, i)),
        compute_job(),
    )

    ring = chip("ctx") // 2

    def weight_columns(target, half, further, extra=None):
        wide = lax.rem(ring + further, 4)
        columns = pl.ds(pl.multiple_of(half * 1024 + wide * 256, 256), 256)
        into = pl.ds(pl.multiple_of(wide * 256, 256), 256)
        for i, (left, right) in enumerate(((gate_t, rows_all), (up_t, rows_all), (inner_t, og))):
            some = slice(i * ff, i * ff + ff)
            block = times(left[...], right[:, columns])
            if extra is not None:
                block = block + extra[some, into].astype(F32)
            target[some, into] = block.astype(LOW)
        return wide

    def weight_job():
        copies = {}

        def give(further):
            wide = weight_columns(theirs, 1 - core, further)
            copies[further] = link.send(
                column_block(theirs, wide, 256), column_block(sib, wide, 256), "ctx", 0, 0, 1
            )

        def take(further):
            copies[further].wait_recv()
            weight_columns(sib, core, further, sib)

        yield 0.1
        give(2)
        yield 1.0
        give(1)
        yield 2.0
        take(2)
        scatter = scatter_job(link, "ctx", lambda i: column_block(sib, i), land_b, work_b, summed, 6.0, 10.8)
        yield 3.0
        give(3)
        take(1)
        next(scatter)
        later = next(scatter)
        yield 4.0
        down(last_pair_slots[0])
        yield 5.0
        give(0)
        take(3)
        yield 6.0
        take(0)
        yield later
        yield from scatter

    run(
        scatter_job(link, "shard", lambda i: parts.at[i], land_a, work_a, result),
        weight_job(),
    )


def swap_lanes(values):
    width = values.shape[1]
    low_half = lax.broadcasted_iota(jnp.int32, values.shape, 1) % HEAD < 32
    return jnp.where(low_half, pltpu.roll(values, width - 32, 1), pltpu.roll(values, 32, 1))


def back_kernel(link, kv_parts, summed, hidden, queries, attended, cosine, sine,
                full, hidden_rows, query_cols, attended_cols, kv_cols,
                sib, land_k, work_k, kv_grad, kv_turned):
    link.greet(whole("shard") + near("ctx") + SIBLING)
    core = lax.rem(lax.axis_index("ctx"), 2)

    def kv_job():
        yield 0.0
        copies = [
            link.send(kv_parts.at[i * 2 + 1 - core], sib.at[i], "ctx", 0, 0, 1) for i in range(8)
        ]
        yield 3.0
        for i, copy in enumerate(copies):
            copy.wait_recv()
            add_rows(sib.at[i], [sib.at[i], kv_parts.at[i * 2 + core]])
        yield from scatter_job(link, "ctx", lambda i: sib.at[i], land_k, work_k, kv_grad, 4.0, 2.7)
        key_lanes = lax.broadcasted_iota(jnp.int32, cosine.shape, 1) < HEAD
        for head in range(KV_HEADS):
            lanes = slice(head * 128, head * 128 + 128)
            both = kv_grad[:, lanes]
            turned = both * cosine[...] - swap_lanes(both) * sine[...]
            kv_turned[:, lanes] = jnp.where(key_lanes, turned, both).astype(LOW)
        part = lambda i: kv_turned.at[:, pl.ds(pl.multiple_of(i // 2 * 128, 128), 128)]
        yield from exchange_job(link, "shard", part, lambda i: kv_cols.at[i], 26.0, 12.0)

    columns = lambda ref: lambda i: ref.at[:, pl.ds(pl.multiple_of(i * 256, 256), 256)]
    run(
        kv_job(),
        gather_halves(link, "shard", hidden, lambda i: hidden_rows.at[i], None, 0.2),
        spread(link, summed, full, gather_halves, 5.0),
        exchange_job(link, "shard", columns(queries), lambda i: query_cols.at[i], 27.0, 20.0),
        exchange_job(link, "shard", columns(attended), lambda i: attended_cols.at[i], 27.1, 21.0),
    )


def last_kernel(link, parts, theirs, mine, gains, result, full, gain_sum,
                land_a, work_a, sib, land_b, work_b, summed, gain_land, gain_work, gain_ctx):
    link.greet(whole("shard") + whole("ctx") + SIBLING)

    def weight_job():
        yield from reduced(link, theirs, mine, sib, land_b, work_b, summed, 0.0, 3.0)
        yield from spread(link, summed, full, gather_job, 24.0, 3.0)

    def gain_job():
        yield from exchange_job(link, "shard", lambda i: gains.at[i], lambda i: gain_land.at[i], 0.2, 8.0)
        gain_work[0] = sum(gain_land[i] for i in range(8))
        copy = link.send(gain_work.at[0], gain_work.at[1], "ctx", 0, 0, 1)
        yield 11.0
        copy.wait_recv()
        gain_work[2] = gain_work[0] + gain_work[1]
        copies = [
            link.send(gain_work.at[2], gain_ctx.at[i], "ctx", r, p) for i, (r, p) in enumerate(ALL)
        ]
        yield 40.0
        for copy in copies:
            copy.wait_recv()
        gain_sum[...] = gain_work[2] + sum(gain_ctx[i] for i in range(7))

    run(
        scatter_job(link, "shard", lambda i: parts.at[i], land_a, work_a, result),
        weight_job(),
        gain_job(),
    )


def first_kernel(pair_ref, tokens, gain, w_query, w_key, w_value, kv_other, cosine, sine,
                 normed_ref, q_ref, kv_ref, w_kv):
    @pl.when(pl.program_id(0) == 0)
    def _():
        leads = pair_ref[0] == 0
        nothing = jnp.zeros((32, D), LOW)
        choose = lambda yes, ref, other: jnp.where(yes, ref[...], other)
        w_kv[0:32, :] = choose(leads, w_key, nothing)
        w_kv[32:64, :] = choose(leads, kv_other, nothing)
        w_kv[64:96, :] = choose(jnp.logical_not(leads), kv_other, nothing)
        w_kv[96:128, :] = choose(jnp.logical_not(leads), w_value, nothing)

    values = tokens[...].astype(F32)
    normed = rms_forward(values, gain[...])[0].astype(LOW)
    normed_ref[...] = normed
    cosine, sine = cosine[...], sine[...]
    turn = lambda v: v * cosine + swap_lanes(v) * sine
    q = times_transposed(normed, w_query[...])
    for i in range(2):
        lanes = slice(i * 128, i * 128 + 128)
        q_ref[:, :, lanes] = turn(q[:, lanes]).astype(LOW).reshape(2, 128, 128)
    kv = times_transposed(normed, w_kv[...])
    keys = lax.broadcasted_iota(jnp.int32, kv.shape, 1) < HEAD
    kv_ref[...] = jnp.where(keys, turn(kv), kv).astype(LOW).reshape(2, 128, 128)


def first_part(pair, token_rows, gain, w_query, w_key, w_value, kv_other, cosine, sine):
    held = lambda *dims: pl.BlockSpec(dims, lambda i, *_: (0,) * len(dims))
    rows = lambda width: pl.BlockSpec((256, width), lambda i, *_: (i, 0))
    slots = lambda width: pl.BlockSpec((2, 128, width), lambda i, *_: (i, 0, 0))
    return pl.pallas_call(
        first_kernel,
        grid_spec=pltpu.PrefetchScalarGridSpec(
            num_scalar_prefetch=1,
            grid=(4,),
            in_specs=[rows(D), held(1, D), held(256, D), held(32, D), held(32, D), held(32, D), rows(128), rows(128)],
            out_specs=[rows(D), slots(256), slots(128)],
            scratch_shapes=[pltpu.VMEM((128, D), LOW)],
        ),
        out_shape=[shape((1024, D), LOW), shape((8, 128, 256), LOW), shape((8, 128, 128), LOW)],
        compiler_params=pltpu.CompilerParams(vmem_limit_bytes=VMEM_LIMIT),
        cost_estimate=pl.CostEstimate(flops=1 << 31, bytes_accessed=10 << 20, transcendentals=1024),
    )(pair, token_rows, gain, w_query, w_key, w_value, kv_other, cosine, sine)


BLOCK = 256
LOG2E = 1.4426950408889634


def sort_keys(order_ref, kv_ref, sorted_ref, flipped_ref):
    for c in range(16):
        lead = pl.multiple_of(order_ref[c] * 64, 64)
        trail = pl.multiple_of((31 - order_ref[c]) * 64, 64)
        sorted_ref[pl.ds(lead, 64), :] = kv_ref[c, 0:64, :]
        sorted_ref[pl.ds(trail, 64), :] = kv_ref[c, 64:128, :]
    for i in range(8):
        rows = slice(i * BLOCK, (i + 1) * BLOCK)
        flipped_ref[i] = jnp.transpose(sorted_ref[rows, :].astype(F32)).astype(LOW)


def spread_heads(blocks, high):
    pieces = []
    for block in blocks:
        block = block.astype(F32)
        turned = pltpu.roll(block, 64, 1)
        lane = lax.broadcasted_iota(jnp.int32, block.shape, 1)
        keep = (lane >= 64) if high else (lane < 64)
        first, second = (turned, block) if high else (block, turned)
        pieces += [jnp.where(keep, first, 0.0), jnp.where(keep, second, 0.0)]
    return jnp.concatenate(pieces, axis=0)


def join_heads(flipped):
    upright = jnp.transpose(flipped)
    return [
        jnp.concatenate([upright[i * 128 : i * 128 + 64], upright[i * 128 + 64 : i * 128 + 128]], axis=1)
        for i in range(4)
    ]


def query_blocks(ref, run):
    rows = slice(run * 64, run * 64 + 64)
    return [ref[s, rows, p * 128 : p * 128 + 128] for s in range(2) for p in range(2)]


def row_blocks(ref, run):
    rows = slice(run * 64, run * 64 + 64)
    return [ref[rows, i * 128 : i * 128 + 128] for i in range(4)]


def above(block, first_place):
    key = lax.broadcasted_iota(jnp.int32, (BLOCK, 512), 0) + block * BLOCK
    query = lax.broadcasted_iota(jnp.int32, (BLOCK, 512), 1) % 64 + first_place
    return key > query


def dot_kt(left, right):
    return lax.dot_general(left, right, (((1,), (1,)), ((), ())), preferred_element_type=F32)


def attend_kernel(order_ref, own_ref, q_ref, kv_ref, out_ref, lse_ref, sorted_ref, flipped_ref):
    sort_keys(order_ref, kv_ref, sorted_ref, flipped_ref)
    factor = HEAD**-0.5 * LOG2E
    for run in range(2):
        first_place = jnp.where(run == 0, own_ref[0], 31 - own_ref[0]) * 64
        last = first_place // BLOCK
        q = spread_heads(query_blocks(q_ref, run), False).astype(LOW)

        def step(block, carry, masked):
            largest, total, mixed = carry
            rows = pl.ds(pl.multiple_of(block * BLOCK, BLOCK), BLOCK)
            scores = dot_kt(sorted_ref[rows, :], q) * factor
            if masked:
                scores = jnp.where(above(block, first_place), NEG, scores)
            top = jnp.maximum(largest, jnp.max(scores, axis=0, keepdims=True))
            fade = jnp.exp2(largest - top)
            exps = jnp.exp2(scores - top)
            total = total * fade + jnp.sum(exps, axis=0, keepdims=True)
            mixed = mixed * fade + times(flipped_ref[block, 64:128, :], exps.astype(LOW))
            return top, total, mixed

        carry = (jnp.full((1, 512), NEG, F32), jnp.zeros((1, 512), F32), jnp.zeros((64, 512), F32))
        carry = lax.fori_loop(0, last, functools.partial(step, masked=False), carry)
        largest, total, mixed = step(last, carry, True)
        for i, block in enumerate(join_heads(mixed / total)):
            out_ref[run * 64 : run * 64 + 64, i * 128 : i * 128 + 128] = block.astype(LOW)
        lse_ref[0, run : run + 1, :] = largest + jnp.log2(total)


def attend_back_kernel(order_ref, own_ref, q_ref, kv_ref, out_ref, grad_ref, lse_ref, cos_ref, sin_ref,
                       dq_ref, dkv_ref, sorted_ref, flipped_ref, total_ref):
    sort_keys(order_ref, kv_ref, sorted_ref, flipped_ref)
    total_ref[...] = jnp.zeros_like(total_ref)
    scale = HEAD**-0.5
    factor = scale * LOG2E
    for run in range(2):
        first_place = jnp.where(run == 0, own_ref[0], 31 - own_ref[0]) * 64
        last = first_place // BLOCK
        q = spread_heads(query_blocks(q_ref, run), False).astype(LOW)
        grad_wide = spread_heads(row_blocks(grad_ref, run), True)
        out_wide = spread_heads(row_blocks(out_ref, run), True)
        grad = grad_wide.astype(LOW)
        inner = lax.dot_general(
            jnp.ones((8, 128), F32),
            grad_wide * out_wide,
            (((1,), (1,)), ((), ())),
            precision=lax.Precision.HIGHEST,
            preferred_element_type=F32,
        )[:1]
        lse = lse_ref[0, run : run + 1, :]

        def step(block, dq, masked):
            rows = pl.ds(pl.multiple_of(block * BLOCK, BLOCK), BLOCK)
            kv = sorted_ref[rows, :]
            probs = jnp.exp2(dot_kt(kv, q) * factor - lse)
            if masked:
                probs = jnp.where(above(block, first_place), 0.0, probs)
            score_grad = (probs * (dot_kt(kv, grad) - inner)).astype(LOW)
            total_ref[rows, :] += times(score_grad, q) + times(probs.astype(LOW), grad)
            return dq + times(flipped_ref[block, 0:64, :], score_grad)

        dq = lax.fori_loop(0, last, functools.partial(step, masked=False), jnp.zeros((64, 512), F32))
        dq = step(last, dq, True)
        cosine, sine = cos_ref[run * 64 : run * 64 + 64, :], sin_ref[run * 64 : run * 64 + 64, :]
        low_half = lax.broadcasted_iota(jnp.int32, (64, 128), 1) % 64 < 32
        for i, block in enumerate(join_heads(dq * scale)):
            turned = jnp.where(low_half, pltpu.roll(block, 96, 1), pltpu.roll(block, 32, 1))
            dq_ref[run * 64 : run * 64 + 64, i * 128 : i * 128 + 128] = (
                block * cosine - turned * sine
            ).astype(LOW)
    weight = jnp.where(lax.broadcasted_iota(jnp.int32, (64, 128), 1) < 64, scale, 1.0)
    for c in range(16):
        lead = pl.multiple_of(order_ref[c] * 64, 64)
        trail = pl.multiple_of((31 - order_ref[c]) * 64, 64)
        dkv_ref[c, 0:64, :] = (total_ref[pl.ds(lead, 64), :] * weight).astype(LOW)
        dkv_ref[c, 64:128, :] = (total_ref[pl.ds(trail, 64), :] * weight).astype(LOW)


def attention_call(kernel, scalars, inputs, kinds, outputs, out_kinds, scratch, flops):
    specs = {
        "q": pl.BlockSpec((2, 128, 256), lambda g, *_: (g, 0, 0)),
        "kv": pl.BlockSpec((16, 128, 128), lambda g, *_: (0, 0, g)),
        "rows": pl.BlockSpec((128, 512), lambda g, *_: (0, g)),
        "lse": pl.BlockSpec((1, 8, 512), lambda g, *_: (g, 0, 0)),
        "table": pl.BlockSpec((128, 128), lambda g, *_: (0, 0)),
    }
    keys = [pltpu.VMEM((2048, 128), LOW), pltpu.VMEM((8, 128, BLOCK), LOW)]
    return pl.pallas_call(
        kernel,
        grid_spec=pltpu.PrefetchScalarGridSpec(
            num_scalar_prefetch=2,
            grid=(KV_HEADS,),
            in_specs=[specs[k] for k in kinds],
            out_specs=[specs[k] for k in out_kinds],
            scratch_shapes=keys + scratch,
        ),
        out_shape=outputs,
        compiler_params=pltpu.CompilerParams(vmem_limit_bytes=VMEM_LIMIT),
        cost_estimate=pl.CostEstimate(flops=flops, bytes_accessed=8 << 20, transcendentals=8 << 20),
    )(*scalars, *inputs)


def attend(queries, kv_all, order, own):
    return attention_call(
        attend_kernel,
        (order, own),
        (queries, kv_all),
        ("q", "kv"),
        [jax.ShapeDtypeStruct((128, D), LOW), jax.ShapeDtypeStruct((4, 8, 512), F32)],
        ("rows", "lse"),
        [],
        1 << 33,
    )


def attend_back(queries, kv_all, attended, attended_grad, lse, cosine, sine, order, own):
    return attention_call(
        attend_back_kernel,
        (order, own),
        (queries, kv_all, attended, attended_grad, lse, cosine, sine),
        ("q", "kv", "rows", "rows", "lse", "table", "table"),
        [jax.ShapeDtypeStruct((128, D), LOW), jax.ShapeDtypeStruct((16, 128, 512), LOW)],
        ("rows", "kv"),
        [pltpu.VMEM((2048, 128), F32)],
        1 << 34,
    )


def local(
    tokens,
    positions,
    out_grad,
    attn_gain,
    w_query,
    w_key,
    w_value,
    w_out,
    ffn_gain,
    w_gate,
    w_up,
    w_down,
):
    rows = tokens.shape[0]
    shard, ctx = lax.axis_index("shard"), lax.axis_index("ctx")
    shard_pair, core = shard % 2, ctx % 2
    places = positions[0]
    own_places = lax.dynamic_slice_in_dim(places, ctx * rows, rows)
    blocks = lambda m: m.reshape(8, rows, -1)

    small = jnp.stack(
        [attn_gain, ffn_gain, jnp.concatenate([own_places // 64, own_places % 64]).astype(LOW)]
    )
    small = jnp.concatenate([small, jnp.zeros((13, 256), LOW)], axis=0)
    token_rows, smalls, kv_other, out_full = comm_call(
        front_kernel,
        0,
        [tokens, small, jnp.where(shard_pair == 0, w_value, w_key), w_out],
        [ANY] * 4,
        [shape((8, rows, D), LOW), shape((8, 16, 256), LOW), shape((32, D), LOW), shape((8, 256, D), LOW)],
        [ANY] * 4,
    )
    out_grad_late, token_rows = lax.optimization_barrier((out_grad, token_rows))
    out_grad_rows = lax.all_gather(out_grad_late, "shard", axis=0, tiled=True)
    token_rows, out_full = token_rows.reshape(-1, D), out_full.reshape(D, D)
    gain_one = smalls[:, 0].reshape(-1).astype(F32)
    gain_two = smalls[:, 1].reshape(-1).astype(F32)
    place_rows = (smalls[:, 2, :rows].astype(F32) * 64.0 + smalls[:, 2, rows:].astype(F32)).reshape(-1)
    cosine, sine = wide_tables(place_rows, 2)
    inputs_rows = token_rows.astype(F32)
    normed_rows, queries, kv_part = first_part(
        shard_pair[None], token_rows, gain_one[None], w_query, w_key, w_value, kv_other, cosine, sine
    )
    queries, kv_all = comm_call(
        qkv_kernel,
        1,
        [queries, kv_part],
        [ANY] * 2,
        [shape((8, rows, 256), LOW), shape((16, rows, 512), LOW)],
        [ANY] * 2,
        [pltpu.VMEM((8, rows, 128), LOW), pltpu.VMEM((rows, 512), LOW)],
    )

    order = places.reshape(16, rows)[:, 0] // 64
    own_order = own_places[:1] // 64
    attended, lse = attend(queries, kv_all, order, own_order)

    inputs = tokens.astype(F32)
    hidden_state = inputs + times(attended, out_full)
    normed_two, inverse_two = rms_forward(hidden_state, gain_two)
    ff = w_gate.shape[0]
    vmem = lambda count, *dims: pltpu.VMEM((count, *dims), LOW)
    normed_two_grad, down_parts, summed = comm_call(
        ffn_kernel,
        3,
        [normed_two.astype(LOW), out_grad_rows, w_gate, w_up, w_down],
        [ANY] + [INSIDE] * 4,
        [shape((rows, D), F32), shape((8, rows, D), LOW), shape((3 * ff, LANES), LOW)],
        [INSIDE] * 3,
        [
            vmem(8 * rows, D),
            vmem(ff, 8 * rows),
            vmem(ff, 8 * rows),
            vmem(ff, 8 * rows),
            vmem(8, rows, D),
            vmem(7, rows, D),
            vmem(3, rows, D),
            vmem(3 * ff, 1024),
            vmem(3 * ff, 1024),
            vmem(7, 3 * ff, LANES),
            vmem(3, 3 * ff, LANES),
        ],
        62 * 1024 * 1024,
    )
    down_parts = down_parts.reshape(-1, D)
    def halves(terms):
        def one(which):
            cut = lambda m: lax.dynamic_slice_in_dim(m, which * 1024, 1024, axis=1)
            return jnp.concatenate(
                [transposed_times(left, cut(right)).astype(LOW) for left, right in terms], axis=0
            )

        return one(1 - core), one(core)

    down_sum = lax.psum_scatter(down_parts, "shard", scatter_dimension=0, tiled=True)
    outputs = (hidden_state + down_sum.astype(F32)).astype(LOW)
    gain_two_part = jnp.sum(normed_two_grad * hidden_state * inverse_two, axis=0)
    hidden_grad = out_grad.astype(F32) + rms_backward(
        hidden_state, inverse_two, gain_two, normed_two_grad
    )
    hidden_low = hidden_grad.astype(LOW)
    attended_grad = times_transposed(hidden_low, out_full).astype(LOW)
    own_table = lambda table: lax.dynamic_slice_in_dim(table, shard * rows, rows)
    cosine_own, sine_own = own_table(cosine), own_table(sine)
    query_pre_grad, kv_parts = attend_back(
        queries, kv_all, attended, attended_grad, lse, cosine_own, sine_own, order, own_order
    )
    ffn_full, hidden_rows, query_cols, attended_cols, kv_cols = comm_call(
        back_kernel,
        4,
        [kv_parts, summed, hidden_low, query_pre_grad, attended, cosine_own, sine_own],
        [INSIDE, INSIDE, ANY, ANY, ANY, INSIDE, INSIDE],
        [
            shape((3 * ff, D), LOW),
            shape((8, rows, D), LOW),
            shape((8, rows, 256), LOW),
            shape((8, rows, 256), LOW),
            shape((8, rows, 128), LOW),
        ],
        [ANY] * 5,
        [
            vmem(8, rows, 512),
            vmem(7, rows, 512),
            vmem(3, rows, 512),
            pltpu.VMEM((rows, 512), F32),
            pltpu.VMEM((rows, 512), LOW),
        ],
    )
    hidden_rows = hidden_rows.reshape(-1, D)
    gate_wgrad, up_wgrad, down_wgrad = (
        ffn_full[i * ff : (i + 1) * ff].astype(F32) for i in range(3)
    )
    query_cols, attended_cols = query_cols.reshape(-1, 256), attended_cols.reshape(-1, 256)
    kv_cols = kv_cols.reshape(-1, 128)
    nothing = jnp.zeros((32, D), LOW)
    kv_weights = jnp.where(
        shard_pair == 0,
        jnp.concatenate([w_key, nothing, w_value, nothing], axis=0),
        jnp.concatenate([nothing, w_key, nothing, w_value], axis=0),
    )
    kv_mine = jnp.where(
        shard_pair == 0,
        jnp.concatenate([kv_cols[:, :32], kv_cols[:, 64:96]], axis=1),
        jnp.concatenate([kv_cols[:, 32:64], kv_cols[:, 96:]], axis=1),
    )
    normed_parts = times(query_cols, w_query) + times(kv_cols, kv_weights)
    gain_one_part = jnp.sum(normed_parts * inputs_rows * inverse_of(inputs_rows), axis=0)
    theirs, mine = halves(
        [(query_cols, normed_rows), (kv_mine, normed_rows), (attended_cols, hidden_rows)]
    )
    gains = jnp.stack([gain_one_part, gain_two_part]).reshape(2, 8, 256).transpose(1, 0, 2)
    gains = jnp.concatenate([gains, jnp.zeros((8, 6, 256), F32)], axis=1)
    normed_grad, attn_full, gain_sum = comm_call(
        last_kernel,
        6,
        [blocks(normed_parts.astype(LOW)), theirs, mine, gains],
        [INSIDE, ANY, INSIDE, INSIDE],
        [shape((rows, D), F32), shape((576, D), LOW), shape((8, 256), F32)],
        [INSIDE, ANY, INSIDE],
        [
            vmem(7, rows, D),
            vmem(3, rows, D),
            pltpu.VMEM((576, 1024), LOW),
            vmem(7, 576, LANES),
            vmem(3, 576, LANES),
            pltpu.VMEM((576, LANES), LOW),
            pltpu.VMEM((8, 8, 256), F32),
            pltpu.VMEM((3, 8, 256), F32),
            pltpu.VMEM((7, 8, 256), F32),
        ],
    )
    inverse_one = inverse_of(inputs)
    input_grad = hidden_grad + rms_backward(inputs, inverse_one, gain_one, normed_grad)
    query_wgrad, key_wgrad, value_wgrad, out_wgrad = (
        attn_full[a:b].astype(F32) for a, b in ((0, 256), (256, 288), (288, 320), (320, 576))
    )
    return (
        outputs,
        input_grad,
        gain_sum[0],
        query_wgrad,
        key_wgrad,
        value_wgrad,
        out_wgrad,
        gain_sum[1],
        gate_wgrad,
        up_wgrad,
        down_wgrad,
    )


def solution(mesh):
    rows = P(("shard", "ctx"), None)
    matrix = P("shard", None)
    vector = P("shard")
    in_specs = (rows, matrix, rows, vector, matrix, matrix, matrix, matrix, vector) + (matrix,) * 3
    out_specs = (rows, rows, vector, matrix, matrix, matrix, matrix, vector) + (matrix,) * 3
    return jax.shard_map(local, mesh=mesh, in_specs=in_specs, out_specs=out_specs, check_vma=False)
```

```python
import functools

import jax
import jax.numpy as jnp
from jax import lax
from jax.experimental import pallas as pl
from jax.experimental.pallas import tpu as pltpu
from jax.sharding import PartitionSpec as P

D = 2048
HEADS = 32
KV_HEADS = 4
HEAD = 64
LANES = 128

EPS = 1e-05
BASE = 10000.0
NEG = -1e30
F32 = jnp.float32
LOW = jnp.bfloat16
MESH = pl.DeviceIdType.MESH
VMEM_LIMIT = 56 * 1024 * 1024


def times(left, right):
    return jnp.dot(left, right, preferred_element_type=F32)


def times_transposed(left, right):
    return lax.dot_general(left, right, (((1,), (1,)), ((), ())), preferred_element_type=F32)


def transposed_times(left, right):
    return lax.dot_general(left, right, (((0,), (0,)), ((), ())), preferred_element_type=F32)


def rope_tables(places, width):
    half = width // 2
    freqs = BASE ** (-(jnp.arange(half).astype(F32) * 2.0 / width))
    angles = places.astype(F32)[:, None] * freqs[None, :]
    return jnp.cos(angles), jnp.sin(angles)


def wide_tables(places, heads):
    cosine, sine = rope_tables(places, HEAD)
    return (
        jnp.tile(jnp.concatenate([cosine, cosine], axis=1), (1, heads)),
        jnp.tile(jnp.concatenate([-sine, sine], axis=1), (1, heads)),
    )


def inverse_of(values):
    return lax.rsqrt(jnp.mean(values * values, axis=-1, keepdims=True) + EPS)


def rms_forward(values, gain):
    inverse = inverse_of(values)
    return (values * inverse * gain, inverse)


def rms_backward(values, inverse, gain, grads):
    scaled = grads * gain
    return inverse * scaled - values * inverse * inverse * inverse * jnp.mean(
        scaled * values, axis=-1, keepdims=True
    )


def at(axis, ring, pair, core=0):
    index = lax.axis_index(axis)
    cores = 2 if axis == "ctx" else 1
    ring_at = lax.rem(index // (2 * cores) + ring % 4, 4)
    pair_at = lax.rem(lax.rem(index // cores, 2) + pair, 2)
    core_at = lax.rem(lax.rem(index, cores) + core, cores)
    return (ring_at * 2 + pair_at) * cores + core_at


def chip(axis, ring=0, pair=0):
    return at(axis, ring, pair) // (2 if axis == "ctx" else 1)


class Link:
    def __init__(self, send_sems, recv_sems, local_sems):
        self.send_sems, self.recv_sems, self.local_sems = send_sems, recv_sems, local_sems
        self.sent, self.kept = [], []

    def greet(self, offsets):
        barrier = pltpu.get_barrier_semaphore()
        for axis, ring, pair, core in offsets:
            pl.semaphore_signal(
                barrier, inc=1, device_id={axis: at(axis, ring, pair, core)}, device_id_type=MESH
            )
        pl.semaphore_wait(barrier, len(offsets))

    def send(self, source, target, axis, ring, pair, core=0):
        number = len(self.sent)
        copy = pltpu.make_async_remote_copy(
            src_ref=source,
            dst_ref=target,
            send_sem=self.send_sems.at[number],
            recv_sem=self.recv_sems.at[number],
            device_id={axis: at(axis, ring, pair, core)},
            device_id_type=MESH,
        )
        copy.start()
        self.sent.append(copy)
        return copy

    def keep(self, source, target):
        copy = pltpu.make_async_copy(source, target, self.local_sems.at[len(self.kept)])
        copy.start()
        self.kept.append(copy)
        return copy

    def kept_now(self, copy):
        copy.wait()
        self.kept = [None if other is copy else other for other in self.kept]

    def finish(self):
        for copy in self.kept:
            if copy is not None:
                copy.wait()
        for copy in self.sent:
            copy.wait_send()


NEAR = [(1, 0), (3, 0), (0, 1)]
ALL = [(r, p) for r in range(4) for p in range(2) if (r, p) != (0, 0)]
near = lambda axis: [(axis, r, p, 0) for r, p in NEAR]
whole = lambda axis: [(axis, r, p, 0) for r, p in ALL]
SIBLING = [("ctx", 0, 0, 1)]


def run(*jobs):
    waiting = [(next(job), number, job) for number, job in enumerate(jobs)]
    while waiting:
        waiting.sort(key=lambda entry: entry[:2])
        _, number, job = waiting.pop(0)
        after = next(job, None)
        if after is not None:
            waiting.append((after, number, job))


def gather_job(link, axis, own, slot, share=None, start=0.0, block=10.5):
    me, pair = chip(axis), chip(axis, 0, 1)
    sharing = lambda index: share(index, slot(index)) if share else None
    yield start
    kept = link.keep(own, slot(me))
    to_pair = link.send(own, slot(me), axis, 0, 1)
    down = link.send(own, slot(me), axis, -1, 0)
    up = link.send(own, slot(me), axis, 1, 0)
    if share:
        share(me, own)
    yield start + block + 3.0
    to_pair.wait_recv()
    pair_down = link.send(slot(pair), slot(pair), axis, -1, 0)
    pair_up = link.send(slot(pair), slot(pair), axis, 1, 0)
    sharing(pair)
    yield start + block + 3.1
    down.wait_recv()
    next_one = chip(axis, 1, 0)
    far_down = link.send(slot(next_one), slot(next_one), axis, -1, 0)
    sharing(next_one)
    yield start + block + 3.2
    up.wait_recv()
    sharing(chip(axis, -1, 0))
    yield start + 2 * block + 4.0
    pair_up.wait_recv()
    last_pair = chip(axis, -1, 1)
    far_up = link.send(slot(last_pair), slot(last_pair), axis, 1, 0)
    sharing(last_pair)
    yield start + 2 * block + 4.1
    pair_down.wait_recv()
    sharing(chip(axis, 1, 1))
    yield start + 3 * block + 5.0
    far_down.wait_recv()
    sharing(chip(axis, 2, 0))
    yield start + 3 * block + 5.1
    far_up.wait_recv()
    sharing(chip(axis, 2, 1))
    link.kept_now(kept)


def gather_halves(link, axis, own, slot, share=None, start=0.0, block=10.5):
    half = own.shape[0] // 2
    cut = lambda ref, k: ref.at[pl.ds(k * half, half)]
    piece = lambda index, k: cut(slot(index), k)
    me, pair, far = chip(axis), chip(axis, 0, 1), chip(axis, 2, 0)
    above_one, below_one = chip(axis, 1, 0), chip(axis, -1, 0)
    last_pair, next_pair, far_pair = chip(axis, -1, 1), chip(axis, 1, 1), chip(axis, 2, 1)
    sharing = lambda index, k: share(piece(index, k), index, k) if share else None
    pass_on = lambda index, k, ring, pair_: link.send(piece(index, k), piece(index, k), axis, ring, pair_)
    yield start
    kept = link.keep(own, slot(me))
    across, down, up = [], [], []
    for k in range(2):
        across.append(link.send(cut(own, k), piece(me, k), axis, 0, 1))
        down.append(link.send(cut(own, k), piece(me, k), axis, -1, 0))
        up.append(link.send(cut(own, k), piece(me, k), axis, 1, 0))
    if share:
        for k in range(2):
            share(cut(own, k), me, k)
    far_in, pair_up, pair_down, over = [], [], [], []
    for k in range(2):
        yield start + (k + 1) * block / 2 + 3.5
        down[k].wait_recv()
        up[k].wait_recv()
        far_in.append(pass_on(above_one, k, -1, 0) if k == 0 else pass_on(below_one, k, 1, 0))
        sharing(above_one, k)
        sharing(below_one, k)
        across[k].wait_recv()
        pair_up.append(pass_on(pair, k, 1, 0))
        pair_down.append(pass_on(pair, k, -1, 0))
        sharing(pair, k)
    link.kept_now(kept)
    for k in range(2):
        yield start + block + 7.0 + k * block / 2
        far_in[k].wait_recv()
        over.append(pass_on(far, k, 0, 1))
        sharing(far, k)
    yield start + 2.5 * block + 6.0
    for k in range(2):
        pair_up[k].wait_recv()
        sharing(last_pair, k)
        pair_down[k].wait_recv()
        sharing(next_pair, k)
    yield start + 2.5 * block + 9.0
    for k in range(2):
        over[k].wait_recv()
        sharing(far_pair, k)


def add_rows(target, terms):
    rows, width = target.shape
    step = max(s for s in range(16, rows + 1, 16) if rows % s == 0 and (s == 16 or s * width <= 32768))

    def body(i, _):
        some = pl.ds(pl.multiple_of(i * step, 16), step)
        total = terms[0][some, :].astype(F32)
        for term in terms[1:]:
            total = total + term[some, :].astype(F32)
        target[some, :] = total.astype(target.dtype)
        return 0

    lax.fori_loop(0, rows // step, body, 0)


def scatter_job(link, axis, part, landing, work, result, start=0.0, block=10.5):
    here = lambda ring, pair: part(chip(axis, ring, pair))
    yield start
    to_last = link.send(here(2, 1), landing.at[1], axis, -1, 0)
    to_next = link.send(here(2, 0), landing.at[0], axis, 1, 0)
    pair_up = link.send(here(1, 1), landing.at[2], axis, 1, 0)
    yield start + block + 3.0
    to_last.wait_recv()
    add_rows(work.at[0], [here(3, 1), landing.at[1]])
    pair_down = link.send(work.at[0], landing.at[4], axis, -1, 0)
    yield start + block + 4.0
    to_next.wait_recv()
    add_rows(work.at[1], [here(1, 0), landing.at[0]])
    yield start + 2 * block + 3.0
    pair_up.wait_recv()
    mine_up = link.send(work.at[1], landing.at[5], axis, 1, 0)
    mine_down = link.send(here(3, 0), landing.at[3], axis, -1, 0)
    yield start + 2 * block + 6.0
    pair_down.wait_recv()
    add_rows(work.at[2], [here(0, 1), landing.at[2], landing.at[4]])
    across = link.send(work.at[2], landing.at[6], axis, 0, 1)
    yield start + 3 * block + 7.0
    mine_down.wait_recv()
    mine_up.wait_recv()
    yield start + 3 * block + 10.0
    across.wait_recv()
    add_rows(result, [here(0, 0), landing.at[3], landing.at[5], landing.at[6]])


def exchange_job(link, axis, part, slot, start=0.0, length=8.0):
    me = chip(axis)
    yield start
    kept = link.keep(part(me), slot(me))
    copies = [link.send(part(chip(axis, r, p)), slot(me), axis, r, p) for r, p in ALL]
    yield start + length
    for copy in copies:
        copy.wait_recv()
    link.kept_now(kept)


ANY = pl.BlockSpec(memory_space=pl.ANY)
INSIDE = pl.BlockSpec(memory_space=pltpu.VMEM)


def comm_call(kernel, number, inputs, in_specs, outputs, out_specs, scratch=(), limit=VMEM_LIMIT):
    sems = [pltpu.SemaphoreType.DMA((160,)), pltpu.SemaphoreType.DMA((160,)), pltpu.SemaphoreType.DMA((8,))]

    def body(*refs):
        link = Link(*refs[-3:])
        kernel(link, *refs[:-3])
        link.finish()

    return pl.pallas_call(
        body,
        out_shape=outputs,
        in_specs=in_specs,
        out_specs=out_specs,
        scratch_shapes=[*scratch, *sems],
        compiler_params=pltpu.CompilerParams(
            collective_id=number, has_side_effects=True, vmem_limit_bytes=limit
        ),
    )(*inputs)


shape = jax.ShapeDtypeStruct


def front_kernel(link, tokens, small, kv_send, w_out, token_rows, smalls, kv_other, out_full):
    link.greet(whole("shard") + [("ctx", 1, 0, 0), ("ctx", 3, 0, 0)] + SIBLING)
    core = lax.rem(lax.axis_index("ctx"), 2)
    ring = lax.axis_index("ctx") // 4

    def block(index, ring_further=0):
        at_ring = lax.rem(ring + ring_further, 4)
        rows = pl.ds(pl.multiple_of((core * 4 + at_ring) * 32, 32), 32)
        return out_full.at[index, rows]

    mine = pl.ds(pl.multiple_of((core * 4 + ring) * 32, 32), 32)
    passing, sibs = [], []

    def share(index, source):
        sibs.append(link.send(source, block(index), "ctx", 0, 0, 1))
        up = link.send(source, block(index), "ctx", 1, 0)
        passing.append((index, up, link.send(source, block(index), "ctx", -1, 0)))

    def ring_job():
        far = []
        for number in range(8):
            yield 10.0 + 3.8 * number
            index, up, down = passing[number]
            up.wait_recv()
            if number % 2 == 0:
                far.append((index, link.send(block(index, 3), block(index, 3), "ctx", 1, 0)))
            sibs.append(link.send(block(index, 3), block(index, 3), "ctx", 0, 0, 1))
            down.wait_recv()
            if number % 2 == 1:
                far.append((index, link.send(block(index, 1), block(index, 1), "ctx", -1, 0)))
            sibs.append(link.send(block(index, 1), block(index, 1), "ctx", 0, 0, 1))
        for number, (index, copy) in enumerate(far):
            yield 38.0 + number
            copy.wait_recv()
            sibs.append(link.send(block(index, 2), block(index, 2), "ctx", 0, 0, 1))
        yield 50.0
        for copy in sibs:
            copy.wait_recv()

    def kv_job():
        yield 0.0
        copy = link.send(kv_send, kv_other, "shard", 0, 1)
        yield 9.0
        copy.wait_recv()

    run(
        gather_job(link, "shard", w_out.at[mine], lambda i: out_full.at[i, mine], share, 0.0, 4.0),
        exchange_job(link, "shard", lambda i: small, lambda i: smalls.at[i], 0.0, 9.0),
        kv_job(),
        gather_halves(link, "shard", tokens, lambda i: token_rows.at[i], None, 0.1, 12.0),
        ring_job(),
    )


def qkv_kernel(link, queries, kv, queries_got, kv_all, kv_got, kv_own):
    link.greet(whole("shard") + near("ctx") + SIBLING)
    core = lax.rem(lax.axis_index("ctx"), 2)

    def kv_job():
        yield from exchange_job(link, "shard", lambda i: kv.at[i], lambda i: kv_got.at[i], 0.0, 6.0)
        for head in range(KV_HEADS):
            kv_own[:, head * 128 : (head + 1) * 128] = kv_got[2 * head] + kv_got[2 * head + 1]
        slot = lambda i: kv_all.at[i * 2 + core]
        sibs = []

        def share(index, block):
            sibs.append(link.send(block, slot(index), "ctx", 0, 0, 1))

        yield from gather_job(link, "ctx", kv_own, slot, share, 6.0, 2.7)
        for copy in sibs:
            copy.wait_recv()

    run(
        kv_job(),
        exchange_job(link, "shard", lambda i: queries.at[i], lambda i: queries_got.at[i], 0.1, 30.0),
    )


def column_block(ref, index, width=LANES):
    return ref.at[:, pl.ds(pl.multiple_of(index * width, width), width)]


def spread(link, summed, full, gather, start=0.0, block=10.8):
    core = lax.rem(lax.axis_index("ctx"), 2)
    slot = lambda i: column_block(full, core * 8 + i)
    sibs = []

    def share(index, source):
        sibs.append(link.send(source, slot(index), "ctx", 0, 0, 1))

    def share_half(source, index, k):
        half = source.shape[0]
        sibs.append(link.send(source, slot(index).at[pl.ds(k * half, half)], "ctx", 0, 0, 1))

    yield from gather(link, "ctx", summed, slot, share if gather is gather_job else share_half, start, block)
    for copy in sibs:
        copy.wait_recv()


def contract_rows(left, right):
    return lax.dot_general(left, right, (((0,), (0,)), ((), ())), preferred_element_type=F32)


def ffn_kernel(link, own, og, w_gate, w_up, w_down, result, down_parts, summed,
               rows_all, gate_t, up_t, inner_t, parts, land_a, work_a, theirs, sib, land_b, work_b):
    link.greet(near("shard") + near("ctx") + SIBLING)
    core = lax.rem(lax.axis_index("ctx"), 2)
    count = own.shape[0]
    ff = w_gate.shape[0]
    here = lambda ref, i: ref.at[pl.ds(pl.multiple_of(i * count, count), count)]
    token_lanes = lambda i: pl.ds(pl.multiple_of(i * count, count), count)

    def pair_of(ref, slots):
        return jnp.concatenate([here(ref, i)[...] for i in slots], axis=0)

    def forward(*offsets):
        slots = [chip("shard", r, p) for r, p in offsets]
        x = pair_of(rows_all, slots)
        gate = times_transposed(w_gate[...], x)
        up = times_transposed(w_up[...], x)
        inner_grad = times_transposed(w_down[...], pair_of(og, slots))
        sigmoid = 1.0 / (1.0 + jnp.exp(-gate))
        activated = gate * sigmoid
        inner = (activated * up).astype(LOW)
        gate_grad = (inner_grad * up * sigmoid * (1.0 + gate * (1.0 - sigmoid))).astype(LOW)
        up_grad = (inner_grad * activated).astype(LOW)
        for k, i in enumerate(slots):
            lanes = slice(k * count, k * count + count)
            inner_t[:, token_lanes(i)] = inner[:, lanes]
            gate_t[:, token_lanes(i)] = gate_grad[:, lanes]
            up_t[:, token_lanes(i)] = up_grad[:, lanes]
        return slots

    def tokens_of(ref, slots):
        return jnp.concatenate([ref[:, token_lanes(i)] for i in slots], axis=1)

    def back(slots):
        gates, ups = tokens_of(gate_t, slots), tokens_of(up_t, slots)
        for c in range(2):
            some = slice(c * 1024, c * 1024 + 1024)
            block = contract_rows(gates, w_gate[:, some]) + contract_rows(ups, w_up[:, some])
            for k, i in enumerate(slots):
                parts[i, :, some] = block[k * count : k * count + count].astype(LOW)

    def down(slots):
        inners = tokens_of(inner_t, slots)
        for c in range(2):
            some = slice(c * 1024, c * 1024 + 1024)
            block = contract_rows(inners, w_down[:, some])
            for k, i in enumerate(slots):
                down_parts[i, :, some] = block[k * count : k * count + count].astype(LOW)

    def every(*offsets):
        slots = forward(*offsets)
        back(slots)
        down(slots)

    last_pair_slots = []

    def compute_job():
        yield 15.0
        every((0, 0), (0, 1))
        yield 21.5
        every((1, 0), (3, 0))
        yield 33.0
        every((2, 0), (1, 1))
        yield 36.0
        slots = forward((3, 1), (2, 1))
        back(slots)
        last_pair_slots.append(slots)

    run(
        gather_halves(link, "shard", own, lambda i: here(rows_all, i)),
        compute_job(),
    )

    ring = chip("ctx") // 2

    def weight_columns(target, half, further, extra=None):
        wide = lax.rem(ring + further, 4)
        columns = pl.ds(pl.multiple_of(half * 1024 + wide * 256, 256), 256)
        into = pl.ds(pl.multiple_of(wide * 256, 256), 256)
        for i, (left, right) in enumerate(((gate_t, rows_all), (up_t, rows_all), (inner_t, og))):
            some = slice(i * ff, i * ff + ff)
            block = times(left[...], right[:, columns])
            if extra is not None:
                block = block + extra[some, into].astype(F32)
            target[some, into] = block.astype(LOW)
        return wide

    def weight_job():
        copies = {}

        def give(further):
            wide = weight_columns(theirs, 1 - core, further)
            copies[further] = link.send(
                column_block(theirs, wide, 256), column_block(sib, wide, 256), "ctx", 0, 0, 1
            )

        def take(further):
            copies[further].wait_recv()
            weight_columns(sib, core, further, sib)

        yield 0.1
        give(2)
        yield 1.0
        give(1)
        yield 2.0
        take(2)
        scatter = scatter_job(link, "ctx", lambda i: column_block(sib, i), land_b, work_b, summed, 6.0, 10.8)
        yield 3.0
        give(3)
        take(1)
        next(scatter)
        later = next(scatter)
        yield 4.0
        down(last_pair_slots[0])
        yield 5.0
        give(0)
        take(3)
        yield 6.0
        take(0)
        yield later
        yield from scatter

    run(
        scatter_job(link, "shard", lambda i: parts.at[i], land_a, work_a, result),
        weight_job(),
    )


def swap_lanes(values):
    width = values.shape[1]
    low_half = lax.broadcasted_iota(jnp.int32, values.shape, 1) % HEAD < 32
    return jnp.where(low_half, pltpu.roll(values, width - 32, 1), pltpu.roll(values, 32, 1))


def tail_kernel(link, kv_parts, summed, hidden, queries, attended, cosine, sine, normed, w_query, w_key, w_value,
                gains, full, attn_full, result, gain_sum,
                hidden_rows, query_cols, attended_cols, kv_cols, kv_w, left_t, parts, land_a, work_a,
                theirs, sib, land_b, work_b, attn_summed, sib_k, land_k, work_k, kv_grad, kv_turned,
                gain_buf, gain_land, gain_work, gain_ctx):
    link.greet(whole("shard") + whole("ctx") + SIBLING)
    core = lax.rem(lax.axis_index("ctx"), 2)
    leads = lax.rem(lax.axis_index("shard"), 2) == 0
    count = hidden.shape[0]
    here = lambda ref, i: ref.at[pl.ds(pl.multiple_of(i * count, count), count)]
    scatter = scatter_job(link, "shard", lambda i: parts.at[i], land_a, work_a, result, 37.0)

    def make(*offsets):
        slots = [chip("shard", r, p) for r, p in offsets]
        pair_of = lambda ref: jnp.concatenate([here(ref, i)[...] for i in slots], axis=0)
        block = times(pair_of(query_cols), w_query[...]) + times(pair_of(kv_cols), kv_w[...])
        for k, i in enumerate(slots):
            parts[i] = block[k * count : k * count + count].astype(LOW)
        terms = block * pair_of(normed).astype(F32)
        return jnp.sum(terms, axis=0, keepdims=True)

    def main_job():
        yield 0.0
        copies = [
            link.send(kv_parts.at[i * 2 + 1 - core], sib_k.at[i], "ctx", 0, 0, 1) for i in range(8)
        ]
        for half, mine in enumerate((leads, jnp.logical_not(leads))):
            for which, weight in enumerate((w_key, w_value)):
                row = which * 64 + half * 32
                kv_w[row : row + 32, :] = jnp.where(mine, weight[...], jnp.zeros((32, D), LOW))
        yield 3.0
        for i, copy in enumerate(copies):
            copy.wait_recv()
            add_rows(sib_k.at[i], [sib_k.at[i], kv_parts.at[i * 2 + core]])
        yield from scatter_job(link, "ctx", lambda i: sib_k.at[i], land_k, work_k, kv_grad, 4.0, 2.7)
        key_lanes = lax.broadcasted_iota(jnp.int32, cosine.shape, 1) < HEAD
        for head in range(KV_HEADS):
            lanes = slice(head * 128, head * 128 + 128)
            both = kv_grad[:, lanes]
            turned = both * cosine[...] - swap_lanes(both) * sine[...]
            kv_turned[:, lanes] = jnp.where(key_lanes, turned, both).astype(LOW)
        part = lambda i: kv_turned.at[:, pl.ds(pl.multiple_of(i // 2 * 128, 128), 128)]
        yield from exchange_job(link, "shard", part, lambda i: here(kv_cols, i), 24.0, 10.0)
        total = make((2, 0), (2, 1))
        total = total + make((1, 1), (3, 1))
        next(scatter)
        later = next(scatter)
        total = total + make((1, 0), (3, 0))
        total = total + make((0, 0), (0, 1))
        for i in range(8):
            gain_buf[i] = gains[i]
            gain_buf[i, 0:1, :] = total[:, i * 256 : i * 256 + 256]
        yield later
        yield from scatter

    def weight_job():
        yield 41.0
        left_t[0:256, :] = jnp.transpose(query_cols[...].astype(F32)).astype(LOW)
        left_t[256:384, :] = jnp.transpose(kv_cols[...].astype(F32)).astype(LOW)
        left_t[384:640, :] = jnp.transpose(attended_cols[...].astype(F32)).astype(LOW)

        def columns(target, half, add):
            for c in range(4):
                wide = pl.ds(pl.multiple_of(half * 1024 + c * 256, 256), 256)
                into = slice(c * 256, c * 256 + 256)
                for rows, right in ((slice(0, 384), normed), (slice(384, 640), hidden_rows)):
                    block = times(left_t[rows, :], right[:, wide])
                    if add:
                        block = block + target[rows, into].astype(F32)
                    target[rows, into] = block.astype(LOW)

        columns(theirs, 1 - core, False)
        copy = link.send(theirs, sib, "ctx", 0, 0, 1)
        yield 43.5
        copy.wait_recv()
        columns(sib, core, True)
        block = lambda i: column_block(sib, i)
        yield from scatter_job(link, "ctx", block, land_b, work_b, attn_summed, 46.0, 4.5)
        yield from spread(link, attn_summed, attn_full, gather_job, 70.0, 4.0)

    def gain_job():
        yield from exchange_job(link, "shard", lambda i: gain_buf.at[i], lambda i: gain_land.at[i], 40.0, 10.0)
        gain_work[0] = sum(gain_land[i] for i in range(8))
        copy = link.send(gain_work.at[0], gain_work.at[1], "ctx", 0, 0, 1)
        yield 53.0
        copy.wait_recv()
        gain_work[2] = gain_work[0] + gain_work[1]
        copies = [
            link.send(gain_work.at[2], gain_ctx.at[i], "ctx", r, p) for i, (r, p) in enumerate(ALL)
        ]
        yield 69.0
        for copy in copies:
            copy.wait_recv()
        gain_sum[...] = gain_work[2] + sum(gain_ctx[i] for i in range(7))

    columns_of = lambda ref: lambda i: ref.at[:, pl.ds(pl.multiple_of(i * 256, 256), 256)]
    run(
        main_job(),
        exchange_job(link, "shard", columns_of(queries), lambda i: here(query_cols, i), 0.1, 22.0),
        gather_halves(link, "shard", hidden, lambda i: here(hidden_rows, i), None, 0.2, 12.0),
        exchange_job(link, "shard", columns_of(attended), lambda i: here(attended_cols, i), 0.3, 29.0),
        spread(link, summed, full, gather_halves, 10.0),
        gain_job(),
        weight_job(),
    )


def first_kernel(pair_ref, tokens, gain, w_query, w_key, w_value, kv_other, cosine, sine,
                 normed_ref, q_ref, kv_ref, w_kv):
    @pl.when(pl.program_id(0) == 0)
    def _():
        leads = pair_ref[0] == 0
        nothing = jnp.zeros((32, D), LOW)
        choose = lambda yes, ref, other: jnp.where(yes, ref[...], other)
        w_kv[0:32, :] = choose(leads, w_key, nothing)
        w_kv[32:64, :] = choose(leads, kv_other, nothing)
        w_kv[64:96, :] = choose(jnp.logical_not(leads), kv_other, nothing)
        w_kv[96:128, :] = choose(jnp.logical_not(leads), w_value, nothing)

    values = tokens[...].astype(F32)
    normed = rms_forward(values, gain[...])[0].astype(LOW)
    normed_ref[...] = normed
    cosine, sine = cosine[...], sine[...]
    turn = lambda v: v * cosine + swap_lanes(v) * sine
    q = times_transposed(normed, w_query[...])
    for i in range(2):
        lanes = slice(i * 128, i * 128 + 128)
        q_ref[:, :, lanes] = turn(q[:, lanes]).astype(LOW).reshape(2, 128, 128)
    kv = times_transposed(normed, w_kv[...])
    keys = lax.broadcasted_iota(jnp.int32, kv.shape, 1) < HEAD
    kv_ref[...] = jnp.where(keys, turn(kv), kv).astype(LOW).reshape(2, 128, 128)


def first_part(pair, token_rows, gain, w_query, w_key, w_value, kv_other, cosine, sine):
    held = lambda *dims: pl.BlockSpec(dims, lambda i, *_: (0,) * len(dims))
    rows = lambda width: pl.BlockSpec((256, width), lambda i, *_: (i, 0))
    slots = lambda width: pl.BlockSpec((2, 128, width), lambda i, *_: (i, 0, 0))
    return pl.pallas_call(
        first_kernel,
        grid_spec=pltpu.PrefetchScalarGridSpec(
            num_scalar_prefetch=1,
            grid=(4,),
            in_specs=[rows(D), held(1, D), held(256, D), held(32, D), held(32, D), held(32, D), rows(128), rows(128)],
            out_specs=[rows(D), slots(256), slots(128)],
            scratch_shapes=[pltpu.VMEM((128, D), LOW)],
        ),
        out_shape=[shape((1024, D), LOW), shape((8, 128, 256), LOW), shape((8, 128, 128), LOW)],
        compiler_params=pltpu.CompilerParams(vmem_limit_bytes=VMEM_LIMIT),
        cost_estimate=pl.CostEstimate(flops=1 << 31, bytes_accessed=10 << 20, transcendentals=1024),
    )(pair, token_rows, gain, w_query, w_key, w_value, kv_other, cosine, sine)


BLOCK = 256
LOG2E = 1.4426950408889634


def sort_keys(order_ref, kv_ref, sorted_ref, flipped_ref):
    for c in range(16):
        lead = pl.multiple_of(order_ref[c] * 64, 64)
        trail = pl.multiple_of((31 - order_ref[c]) * 64, 64)
        sorted_ref[pl.ds(lead, 64), :] = kv_ref[c, 0:64, :]
        sorted_ref[pl.ds(trail, 64), :] = kv_ref[c, 64:128, :]
    for i in range(8):
        rows = slice(i * BLOCK, (i + 1) * BLOCK)
        flipped_ref[i] = jnp.transpose(sorted_ref[rows, :].astype(F32)).astype(LOW)


def spread_heads(blocks, high):
    pieces = []
    for block in blocks:
        block = block.astype(F32)
        turned = pltpu.roll(block, 64, 1)
        lane = lax.broadcasted_iota(jnp.int32, block.shape, 1)
        keep = (lane >= 64) if high else (lane < 64)
        first, second = (turned, block) if high else (block, turned)
        pieces += [jnp.where(keep, first, 0.0), jnp.where(keep, second, 0.0)]
    return jnp.concatenate(pieces, axis=0)


def join_heads(flipped):
    upright = jnp.transpose(flipped)
    return [
        jnp.concatenate([upright[i * 128 : i * 128 + 64], upright[i * 128 + 64 : i * 128 + 128]], axis=1)
        for i in range(4)
    ]


def query_blocks(ref, run):
    rows = slice(run * 64, run * 64 + 64)
    return [ref[s, rows, p * 128 : p * 128 + 128] for s in range(2) for p in range(2)]


def row_blocks(ref, run):
    rows = slice(run * 64, run * 64 + 64)
    return [ref[rows, i * 128 : i * 128 + 128] for i in range(4)]


def above(block, first_place):
    key = lax.broadcasted_iota(jnp.int32, (BLOCK, 512), 0) + block * BLOCK
    query = lax.broadcasted_iota(jnp.int32, (BLOCK, 512), 1) % 64 + first_place
    return key > query


def dot_kt(left, right):
    return lax.dot_general(left, right, (((1,), (1,)), ((), ())), preferred_element_type=F32)


def attend_kernel(order_ref, own_ref, q_ref, kv_ref, out_ref, lse_ref, sorted_ref, flipped_ref):
    sort_keys(order_ref, kv_ref, sorted_ref, flipped_ref)
    factor = HEAD**-0.5 * LOG2E
    for run in range(2):
        first_place = jnp.where(run == 0, own_ref[0], 31 - own_ref[0]) * 64
        last = first_place // BLOCK
        q = spread_heads(query_blocks(q_ref, run), False).astype(LOW)

        def step(block, carry, masked):
            largest, total, mixed = carry
            rows = pl.ds(pl.multiple_of(block * BLOCK, BLOCK), BLOCK)
            scores = dot_kt(sorted_ref[rows, :], q) * factor
            if masked:
                scores = jnp.where(above(block, first_place), NEG, scores)
            top = jnp.maximum(largest, jnp.max(scores, axis=0, keepdims=True))
            fade = jnp.exp2(largest - top)
            exps = jnp.exp2(scores - top)
            total = total * fade + jnp.sum(exps, axis=0, keepdims=True)
            mixed = mixed * fade + times(flipped_ref[block, 64:128, :], exps.astype(LOW))
            return top, total, mixed

        carry = (jnp.full((1, 512), NEG, F32), jnp.zeros((1, 512), F32), jnp.zeros((64, 512), F32))
        carry = lax.fori_loop(0, last, functools.partial(step, masked=False), carry)
        largest, total, mixed = step(last, carry, True)
        for i, block in enumerate(join_heads(mixed / total)):
            out_ref[run * 64 : run * 64 + 64, i * 128 : i * 128 + 128] = block.astype(LOW)
        lse_ref[0, run : run + 1, :] = largest + jnp.log2(total)


def attend_back_kernel(order_ref, own_ref, q_ref, kv_ref, out_ref, grad_ref, lse_ref, cos_ref, sin_ref,
                       dq_ref, dkv_ref, sorted_ref, flipped_ref, total_ref):
    sort_keys(order_ref, kv_ref, sorted_ref, flipped_ref)
    total_ref[...] = jnp.zeros_like(total_ref)
    scale = HEAD**-0.5
    factor = scale * LOG2E
    for run in range(2):
        first_place = jnp.where(run == 0, own_ref[0], 31 - own_ref[0]) * 64
        last = first_place // BLOCK
        q = spread_heads(query_blocks(q_ref, run), False).astype(LOW)
        grad_wide = spread_heads(row_blocks(grad_ref, run), True)
        out_wide = spread_heads(row_blocks(out_ref, run), True)
        grad = grad_wide.astype(LOW)
        inner = lax.dot_general(
            jnp.ones((8, 128), F32),
            grad_wide * out_wide,
            (((1,), (1,)), ((), ())),
            precision=lax.Precision.HIGHEST,
            preferred_element_type=F32,
        )[:1]
        lse = lse_ref[0, run : run + 1, :]

        def step(block, dq, masked):
            rows = pl.ds(pl.multiple_of(block * BLOCK, BLOCK), BLOCK)
            kv = sorted_ref[rows, :]
            probs = jnp.exp2(dot_kt(kv, q) * factor - lse)
            if masked:
                probs = jnp.where(above(block, first_place), 0.0, probs)
            score_grad = (probs * (dot_kt(kv, grad) - inner)).astype(LOW)
            total_ref[rows, :] += times(score_grad, q) + times(probs.astype(LOW), grad)
            return dq + times(flipped_ref[block, 0:64, :], score_grad)

        dq = lax.fori_loop(0, last, functools.partial(step, masked=False), jnp.zeros((64, 512), F32))
        dq = step(last, dq, True)
        cosine, sine = cos_ref[run * 64 : run * 64 + 64, :], sin_ref[run * 64 : run * 64 + 64, :]
        low_half = lax.broadcasted_iota(jnp.int32, (64, 128), 1) % 64 < 32
        for i, block in enumerate(join_heads(dq * scale)):
            turned = jnp.where(low_half, pltpu.roll(block, 96, 1), pltpu.roll(block, 32, 1))
            dq_ref[run * 64 : run * 64 + 64, i * 128 : i * 128 + 128] = (
                block * cosine - turned * sine
            ).astype(LOW)
    weight = jnp.where(lax.broadcasted_iota(jnp.int32, (64, 128), 1) < 64, scale, 1.0)
    for c in range(16):
        lead = pl.multiple_of(order_ref[c] * 64, 64)
        trail = pl.multiple_of((31 - order_ref[c]) * 64, 64)
        dkv_ref[c, 0:64, :] = (total_ref[pl.ds(lead, 64), :] * weight).astype(LOW)
        dkv_ref[c, 64:128, :] = (total_ref[pl.ds(trail, 64), :] * weight).astype(LOW)


def attention_call(kernel, scalars, inputs, kinds, outputs, out_kinds, scratch, flops):
    specs = {
        "q": pl.BlockSpec((2, 128, 256), lambda g, *_: (g, 0, 0)),
        "kv": pl.BlockSpec((16, 128, 128), lambda g, *_: (0, 0, g)),
        "rows": pl.BlockSpec((128, 512), lambda g, *_: (0, g)),
        "lse": pl.BlockSpec((1, 8, 512), lambda g, *_: (g, 0, 0)),
        "table": pl.BlockSpec((128, 128), lambda g, *_: (0, 0)),
    }
    keys = [pltpu.VMEM((2048, 128), LOW), pltpu.VMEM((8, 128, BLOCK), LOW)]
    return pl.pallas_call(
        kernel,
        grid_spec=pltpu.PrefetchScalarGridSpec(
            num_scalar_prefetch=2,
            grid=(KV_HEADS,),
            in_specs=[specs[k] for k in kinds],
            out_specs=[specs[k] for k in out_kinds],
            scratch_shapes=keys + scratch,
        ),
        out_shape=outputs,
        compiler_params=pltpu.CompilerParams(vmem_limit_bytes=VMEM_LIMIT),
        cost_estimate=pl.CostEstimate(flops=flops, bytes_accessed=8 << 20, transcendentals=8 << 20),
    )(*scalars, *inputs)


def attend(queries, kv_all, order, own):
    return attention_call(
        attend_kernel,
        (order, own),
        (queries, kv_all),
        ("q", "kv"),
        [jax.ShapeDtypeStruct((128, D), LOW), jax.ShapeDtypeStruct((4, 8, 512), F32)],
        ("rows", "lse"),
        [],
        1 << 33,
    )


def attend_back(queries, kv_all, attended, attended_grad, lse, cosine, sine, order, own):
    return attention_call(
        attend_back_kernel,
        (order, own),
        (queries, kv_all, attended, attended_grad, lse, cosine, sine),
        ("q", "kv", "rows", "rows", "lse", "table", "table"),
        [jax.ShapeDtypeStruct((128, D), LOW), jax.ShapeDtypeStruct((16, 128, 512), LOW)],
        ("rows", "kv"),
        [pltpu.VMEM((2048, 128), F32)],
        1 << 34,
    )


def local(
    tokens,
    positions,
    out_grad,
    attn_gain,
    w_query,
    w_key,
    w_value,
    w_out,
    ffn_gain,
    w_gate,
    w_up,
    w_down,
):
    rows = tokens.shape[0]
    shard, ctx = lax.axis_index("shard"), lax.axis_index("ctx")
    shard_pair, core = shard % 2, ctx % 2
    places = positions[0]
    own_places = lax.dynamic_slice_in_dim(places, ctx * rows, rows)

    small = jnp.stack(
        [attn_gain, ffn_gain, jnp.concatenate([own_places // 64, own_places % 64]).astype(LOW)]
    )
    small = jnp.concatenate([small, jnp.zeros((13, 256), LOW)], axis=0)
    token_rows, smalls, kv_other, out_full = comm_call(
        front_kernel,
        0,
        [tokens, small, jnp.where(shard_pair == 0, w_value, w_key), w_out],
        [ANY] * 4,
        [shape((8, rows, D), LOW), shape((8, 16, 256), LOW), shape((32, D), LOW), shape((8, 256, D), LOW)],
        [ANY] * 4,
    )
    out_grad_late, token_rows = lax.optimization_barrier((out_grad, token_rows))
    out_grad_rows = lax.all_gather(out_grad_late, "shard", axis=0, tiled=True)
    token_rows, out_full = token_rows.reshape(-1, D), out_full.reshape(D, D)
    gain_one = smalls[:, 0].reshape(-1).astype(F32)
    gain_two = smalls[:, 1].reshape(-1).astype(F32)
    place_rows = (smalls[:, 2, :rows].astype(F32) * 64.0 + smalls[:, 2, rows:].astype(F32)).reshape(-1)
    cosine, sine = wide_tables(place_rows, 2)
    normed_rows, queries, kv_part = first_part(
        shard_pair[None], token_rows, gain_one[None], w_query, w_key, w_value, kv_other, cosine, sine
    )
    queries, kv_all = comm_call(
        qkv_kernel,
        1,
        [queries, kv_part],
        [ANY] * 2,
        [shape((8, rows, 256), LOW), shape((16, rows, 512), LOW)],
        [ANY] * 2,
        [pltpu.VMEM((8, rows, 128), LOW), pltpu.VMEM((rows, 512), LOW)],
    )

    order = places.reshape(16, rows)[:, 0] // 64
    own_order = own_places[:1] // 64
    attended, lse = attend(queries, kv_all, order, own_order)

    inputs = tokens.astype(F32)
    hidden_state = inputs + times(attended, out_full)
    normed_two, inverse_two = rms_forward(hidden_state, gain_two)
    ff = w_gate.shape[0]
    vmem = lambda count, *dims: pltpu.VMEM((count, *dims), LOW)
    normed_two_grad, down_parts, summed = comm_call(
        ffn_kernel,
        3,
        [normed_two.astype(LOW), out_grad_rows, w_gate, w_up, w_down],
        [ANY] + [INSIDE] * 4,
        [shape((rows, D), F32), shape((8, rows, D), LOW), shape((3 * ff, LANES), LOW)],
        [INSIDE] * 3,
        [
            vmem(8 * rows, D),
            vmem(ff, 8 * rows),
            vmem(ff, 8 * rows),
            vmem(ff, 8 * rows),
            vmem(8, rows, D),
            vmem(7, rows, D),
            vmem(3, rows, D),
            vmem(3 * ff, 1024),
            vmem(3 * ff, 1024),
            vmem(7, 3 * ff, LANES),
            vmem(3, 3 * ff, LANES),
        ],
        62 * 1024 * 1024,
    )
    down_parts = down_parts.reshape(-1, D)
    down_sum = lax.psum_scatter(down_parts, "shard", scatter_dimension=0, tiled=True)
    outputs = (hidden_state + down_sum.astype(F32)).astype(LOW)
    gain_two_part = jnp.sum(normed_two_grad * hidden_state * inverse_two, axis=0)
    hidden_grad = out_grad.astype(F32) + rms_backward(
        hidden_state, inverse_two, gain_two, normed_two_grad
    )
    hidden_low = hidden_grad.astype(LOW)
    attended_grad = times_transposed(hidden_low, out_full).astype(LOW)
    own_table = lambda table: lax.dynamic_slice_in_dim(table, shard * rows, rows)
    cosine_own, sine_own = own_table(cosine), own_table(sine)
    query_pre_grad, kv_parts = attend_back(
        queries, kv_all, attended, attended_grad, lse, cosine_own, sine_own, order, own_order
    )
    gains = jnp.zeros((8, 8, 256), F32).at[:, 1].set(gain_two_part.reshape(8, 256))
    ffn_full, attn_full, normed_grad, gain_sum = comm_call(
        tail_kernel,
        4,
        [kv_parts, summed, hidden_low, query_pre_grad, attended, cosine_own, sine_own, normed_rows]
        + [w_query, w_key, w_value, gains],
        [INSIDE, INSIDE, ANY, ANY, ANY] + [INSIDE] * 7,
        [shape((3 * ff, D), LOW), shape((640, D), LOW), shape((rows, D), F32), shape((8, 256), F32)],
        [ANY, ANY, INSIDE, INSIDE],
        [
            vmem(8 * rows, D),
            vmem(8 * rows, 256),
            vmem(8 * rows, 256),
            vmem(8 * rows, 128),
            vmem(128, D),
            vmem(640, 8 * rows),
            vmem(8, rows, D),
            vmem(7, rows, D),
            vmem(3, rows, D),
            vmem(640, 1024),
            vmem(640, 1024),
            vmem(7, 640, LANES),
            vmem(3, 640, LANES),
            vmem(640, LANES),
            vmem(8, rows, 512),
            vmem(7, rows, 512),
            vmem(3, rows, 512),
            pltpu.VMEM((rows, 512), F32),
            vmem(rows, 512),
            pltpu.VMEM((8, 8, 256), F32),
            pltpu.VMEM((8, 8, 256), F32),
            pltpu.VMEM((3, 8, 256), F32),
            pltpu.VMEM((7, 8, 256), F32),
        ],
    )
    gate_wgrad, up_wgrad, down_wgrad = (
        ffn_full[i * ff : (i + 1) * ff].astype(F32) for i in range(3)
    )
    inverse_one = inverse_of(inputs)
    input_grad = hidden_grad + rms_backward(inputs, inverse_one, gain_one, normed_grad)
    attn_rows = lambda start, size: lax.dynamic_slice_in_dim(attn_full, start, size).astype(F32)
    query_wgrad, out_wgrad = attn_rows(0, 256), attn_rows(384, 256)
    key_wgrad, value_wgrad = attn_rows(256 + shard_pair * 32, 32), attn_rows(320 + shard_pair * 32, 32)
    return (
        outputs,
        input_grad,
        gain_sum[0] / attn_gain.astype(F32),
        query_wgrad,
        key_wgrad,
        value_wgrad,
        out_wgrad,
        gain_sum[1],
        gate_wgrad,
        up_wgrad,
        down_wgrad,
    )


def solution(mesh):
    rows = P(("shard", "ctx"), None)
    matrix = P("shard", None)
    vector = P("shard")
    in_specs = (rows, matrix, rows, vector, matrix, matrix, matrix, matrix, vector) + (matrix,) * 3
    out_specs = (rows, rows, vector, matrix, matrix, matrix, matrix, vector) + (matrix,) * 3
    return jax.shard_map(local, mesh=mesh, in_specs=in_specs, out_specs=out_specs, check_vma=False)
```

```python
import functools

import jax
import jax.numpy as jnp
from jax import lax
from jax.experimental import pallas as pl
from jax.experimental.pallas import tpu as pltpu
from jax.sharding import PartitionSpec as P

D = 2048
HEADS = 32
KV_HEADS = 4
HEAD = 64
LANES = 128

EPS = 1e-05
BASE = 10000.0
NEG = -1e30
F32 = jnp.float32
LOW = jnp.bfloat16
MESH = pl.DeviceIdType.MESH
VMEM_LIMIT = 56 * 1024 * 1024


def times(left, right):
    return jnp.dot(left, right, preferred_element_type=F32)


def times_transposed(left, right):
    return lax.dot_general(left, right, (((1,), (1,)), ((), ())), preferred_element_type=F32)


def transposed_times(left, right):
    return lax.dot_general(left, right, (((0,), (0,)), ((), ())), preferred_element_type=F32)


def rope_tables(places, width):
    half = width // 2
    freqs = BASE ** (-(jnp.arange(half).astype(F32) * 2.0 / width))
    angles = places.astype(F32)[:, None] * freqs[None, :]
    return jnp.cos(angles), jnp.sin(angles)


def wide_tables(places, heads):
    cosine, sine = rope_tables(places, HEAD)
    return (
        jnp.tile(jnp.concatenate([cosine, cosine], axis=1), (1, heads)),
        jnp.tile(jnp.concatenate([-sine, sine], axis=1), (1, heads)),
    )


def inverse_of(values):
    return lax.rsqrt(jnp.mean(values * values, axis=-1, keepdims=True) + EPS)


def rms_forward(values, gain):
    inverse = inverse_of(values)
    return (values * inverse * gain, inverse)


def rms_backward(values, inverse, gain, grads):
    scaled = grads * gain
    return inverse * scaled - values * inverse * inverse * inverse * jnp.mean(
        scaled * values, axis=-1, keepdims=True
    )


def at(axis, ring, pair, core=0):
    index = lax.axis_index(axis)
    cores = 2 if axis == "ctx" else 1
    ring_at = lax.rem(index // (2 * cores) + ring % 4, 4)
    pair_at = lax.rem(lax.rem(index // cores, 2) + pair, 2)
    core_at = lax.rem(lax.rem(index, cores) + core, cores)
    return (ring_at * 2 + pair_at) * cores + core_at


def chip(axis, ring=0, pair=0):
    return at(axis, ring, pair) // (2 if axis == "ctx" else 1)


class Link:
    def __init__(self, send_sems, recv_sems, local_sems):
        self.send_sems, self.recv_sems, self.local_sems = send_sems, recv_sems, local_sems
        self.sent, self.kept = [], []

    def greet(self, offsets):
        barrier = pltpu.get_barrier_semaphore()
        for axis, ring, pair, core in offsets:
            pl.semaphore_signal(
                barrier, inc=1, device_id={axis: at(axis, ring, pair, core)}, device_id_type=MESH
            )
        pl.semaphore_wait(barrier, len(offsets))

    def send(self, source, target, axis, ring, pair, core=0):
        number = len(self.sent)
        copy = pltpu.make_async_remote_copy(
            src_ref=source,
            dst_ref=target,
            send_sem=self.send_sems.at[number],
            recv_sem=self.recv_sems.at[number],
            device_id={axis: at(axis, ring, pair, core)},
            device_id_type=MESH,
        )
        copy.start()
        self.sent.append(copy)
        return copy

    def keep(self, source, target):
        copy = pltpu.make_async_copy(source, target, self.local_sems.at[len(self.kept)])
        copy.start()
        self.kept.append(copy)
        return copy

    def kept_now(self, copy):
        copy.wait()
        self.kept = [None if other is copy else other for other in self.kept]

    def finish(self):
        for copy in self.kept:
            if copy is not None:
                copy.wait()
        for copy in self.sent:
            copy.wait_send()


NEAR = [(1, 0), (3, 0), (0, 1)]
ALL = [(r, p) for r in range(4) for p in range(2) if (r, p) != (0, 0)]
near = lambda axis: [(axis, r, p, 0) for r, p in NEAR]
whole = lambda axis: [(axis, r, p, 0) for r, p in ALL]
SIBLING = [("ctx", 0, 0, 1)]


def run(*jobs):
    waiting = [(next(job), number, job) for number, job in enumerate(jobs)]
    while waiting:
        waiting.sort(key=lambda entry: entry[:2])
        _, number, job = waiting.pop(0)
        after = next(job, None)
        if after is not None:
            waiting.append((after, number, job))


def gather_job(link, axis, own, slot, share=None, start=0.0, block=10.5):
    me, pair = chip(axis), chip(axis, 0, 1)
    sharing = lambda index: share(index, slot(index)) if share else None
    yield start
    kept = link.keep(own, slot(me))
    to_pair = link.send(own, slot(me), axis, 0, 1)
    down = link.send(own, slot(me), axis, -1, 0)
    up = link.send(own, slot(me), axis, 1, 0)
    if share:
        share(me, own)
    yield start + block + 3.0
    to_pair.wait_recv()
    pair_down = link.send(slot(pair), slot(pair), axis, -1, 0)
    pair_up = link.send(slot(pair), slot(pair), axis, 1, 0)
    sharing(pair)
    yield start + block + 3.1
    down.wait_recv()
    next_one = chip(axis, 1, 0)
    far_down = link.send(slot(next_one), slot(next_one), axis, -1, 0)
    sharing(next_one)
    yield start + block + 3.2
    up.wait_recv()
    sharing(chip(axis, -1, 0))
    yield start + 2 * block + 4.0
    pair_up.wait_recv()
    last_pair = chip(axis, -1, 1)
    far_up = link.send(slot(last_pair), slot(last_pair), axis, 1, 0)
    sharing(last_pair)
    yield start + 2 * block + 4.1
    pair_down.wait_recv()
    sharing(chip(axis, 1, 1))
    yield start + 3 * block + 5.0
    far_down.wait_recv()
    sharing(chip(axis, 2, 0))
    yield start + 3 * block + 5.1
    far_up.wait_recv()
    sharing(chip(axis, 2, 1))
    link.kept_now(kept)


def gather_halves(link, axis, own, slot, share=None, start=0.0, block=10.5):
    half = own.shape[0] // 2
    cut = lambda ref, k: ref.at[pl.ds(k * half, half)]
    piece = lambda index, k: cut(slot(index), k)
    me, pair, far = chip(axis), chip(axis, 0, 1), chip(axis, 2, 0)
    above_one, below_one = chip(axis, 1, 0), chip(axis, -1, 0)
    last_pair, next_pair, far_pair = chip(axis, -1, 1), chip(axis, 1, 1), chip(axis, 2, 1)
    sharing = lambda index, k: share(piece(index, k), index, k) if share else None
    pass_on = lambda index, k, ring, pair_: link.send(piece(index, k), piece(index, k), axis, ring, pair_)
    yield start
    kept = link.keep(own, slot(me))
    across, down, up = [], [], []
    for k in range(2):
        across.append(link.send(cut(own, k), piece(me, k), axis, 0, 1))
        down.append(link.send(cut(own, k), piece(me, k), axis, -1, 0))
        up.append(link.send(cut(own, k), piece(me, k), axis, 1, 0))
    if share:
        for k in range(2):
            share(cut(own, k), me, k)
    far_in, pair_up, pair_down, over = [], [], [], []
    for k in range(2):
        yield start + (k + 1) * block / 2 + 3.5
        down[k].wait_recv()
        up[k].wait_recv()
        far_in.append(pass_on(above_one, k, -1, 0) if k == 0 else pass_on(below_one, k, 1, 0))
        sharing(above_one, k)
        sharing(below_one, k)
        across[k].wait_recv()
        pair_up.append(pass_on(pair, k, 1, 0))
        pair_down.append(pass_on(pair, k, -1, 0))
        sharing(pair, k)
    link.kept_now(kept)
    for k in range(2):
        yield start + block + 7.0 + k * block / 2
        far_in[k].wait_recv()
        over.append(pass_on(far, k, 0, 1))
        sharing(far, k)
    yield start + 2.5 * block + 6.0
    for k in range(2):
        pair_up[k].wait_recv()
        sharing(last_pair, k)
        pair_down[k].wait_recv()
        sharing(next_pair, k)
    yield start + 2.5 * block + 9.0
    for k in range(2):
        over[k].wait_recv()
        sharing(far_pair, k)


def add_rows(target, terms):
    rows, width = target.shape
    step = max(s for s in range(16, rows + 1, 16) if rows % s == 0 and (s == 16 or s * width <= 32768))

    def body(i, _):
        some = pl.ds(pl.multiple_of(i * step, 16), step)
        total = terms[0][some, :].astype(F32)
        for term in terms[1:]:
            total = total + term[some, :].astype(F32)
        target[some, :] = total.astype(target.dtype)
        return 0

    lax.fori_loop(0, rows // step, body, 0)


def scatter_job(link, axis, part, landing, work, result, start=0.0, block=10.5):
    here = lambda ring, pair: part(chip(axis, ring, pair))
    yield start
    to_last = link.send(here(2, 1), landing.at[1], axis, -1, 0)
    to_next = link.send(here(2, 0), landing.at[0], axis, 1, 0)
    pair_up = link.send(here(1, 1), landing.at[2], axis, 1, 0)
    yield start + block + 3.0
    to_last.wait_recv()
    add_rows(work.at[0], [here(3, 1), landing.at[1]])
    pair_down = link.send(work.at[0], landing.at[4], axis, -1, 0)
    yield start + block + 4.0
    to_next.wait_recv()
    add_rows(work.at[1], [here(1, 0), landing.at[0]])
    yield start + 2 * block + 3.0
    pair_up.wait_recv()
    mine_up = link.send(work.at[1], landing.at[5], axis, 1, 0)
    mine_down = link.send(here(3, 0), landing.at[3], axis, -1, 0)
    yield start + 2 * block + 6.0
    pair_down.wait_recv()
    add_rows(work.at[2], [here(0, 1), landing.at[2], landing.at[4]])
    across = link.send(work.at[2], landing.at[6], axis, 0, 1)
    yield start + 3 * block + 7.0
    mine_down.wait_recv()
    mine_up.wait_recv()
    yield start + 3 * block + 10.0
    across.wait_recv()
    add_rows(result, [here(0, 0), landing.at[3], landing.at[5], landing.at[6]])


def scatter_halves(link, axis, part, landing, work, result, start=0.0, block=10.5):
    here = lambda ring, pair: part(chip(axis, ring, pair))
    half = result.shape[0] // 2
    cut = lambda ref, k: ref.at[pl.ds(k * half, half)]
    yield start
    far = link.send(here(2, 1), landing.at[0], axis, 0, 1)
    pair_up = link.send(here(1, 1), landing.at[1], axis, 1, 0)
    pair_down = link.send(here(3, 1), landing.at[2], axis, -1, 0)
    mine_up = [link.send(cut(here(1, 0), 1), cut(landing.at[5], 1), axis, 1, 0)]
    mine_down = [link.send(cut(here(3, 0), 0), cut(landing.at[6], 0), axis, -1, 0)]
    yield start + block + 3.5
    far.wait_recv()
    add_rows(work.at[0], [here(2, 0), landing.at[0]])
    half_up = link.send(cut(work.at[0], 0), cut(landing.at[3], 0), axis, 1, 0)
    half_down = link.send(cut(work.at[0], 1), cut(landing.at[3], 1), axis, -1, 0)
    yield start + 1.5 * block + 3.0
    pair_up.wait_recv()
    pair_down.wait_recv()
    add_rows(work.at[1], [here(0, 1), landing.at[1], landing.at[2]])
    across = link.send(work.at[1], landing.at[4], axis, 0, 1)
    yield start + 2 * block + 5.0
    half_up.wait_recv()
    add_rows(cut(work.at[2], 0), [cut(here(1, 0), 0), cut(landing.at[3], 0)])
    mine_up.append(link.send(cut(work.at[2], 0), cut(landing.at[5], 0), axis, 1, 0))
    half_down.wait_recv()
    add_rows(cut(work.at[2], 1), [cut(here(3, 0), 1), cut(landing.at[3], 1)])
    mine_down.append(link.send(cut(work.at[2], 1), cut(landing.at[6], 1), axis, -1, 0))
    yield start + 3 * block + 4.0
    across.wait_recv()
    for copy in mine_up + mine_down:
        copy.wait_recv()
    add_rows(result, [here(0, 0), landing.at[4], landing.at[5], landing.at[6]])


def exchange_job(link, axis, part, slot, start=0.0, length=8.0):
    me = chip(axis)
    yield start
    kept = link.keep(part(me), slot(me))
    copies = [link.send(part(chip(axis, r, p)), slot(me), axis, r, p) for r, p in ALL]
    yield start + length
    for copy in copies:
        copy.wait_recv()
    link.kept_now(kept)


ANY = pl.BlockSpec(memory_space=pl.ANY)
INSIDE = pl.BlockSpec(memory_space=pltpu.VMEM)


def comm_call(kernel, number, inputs, in_specs, outputs, out_specs, scratch=(), limit=VMEM_LIMIT):
    sems = [pltpu.SemaphoreType.DMA((160,)), pltpu.SemaphoreType.DMA((160,)), pltpu.SemaphoreType.DMA((8,))]

    def body(*refs):
        link = Link(*refs[-3:])
        kernel(link, *refs[:-3])
        link.finish()

    return pl.pallas_call(
        body,
        out_shape=outputs,
        in_specs=in_specs,
        out_specs=out_specs,
        scratch_shapes=[*scratch, *sems],
        compiler_params=pltpu.CompilerParams(
            collective_id=number, has_side_effects=True, vmem_limit_bytes=limit
        ),
    )(*inputs)


shape = jax.ShapeDtypeStruct


def front_kernel(link, tokens, small, kv_send, w_out, token_rows, smalls, kv_other, out_full):
    link.greet(whole("shard") + [("ctx", 1, 0, 0), ("ctx", 3, 0, 0)] + SIBLING)
    core = lax.rem(lax.axis_index("ctx"), 2)
    ring = lax.axis_index("ctx") // 4

    def block(index, ring_further=0):
        at_ring = lax.rem(ring + ring_further, 4)
        rows = pl.ds(pl.multiple_of((core * 4 + at_ring) * 32, 32), 32)
        return out_full.at[index, rows]

    mine = pl.ds(pl.multiple_of((core * 4 + ring) * 32, 32), 32)
    passing, sibs = [], []

    def share(index, source):
        sibs.append(link.send(source, block(index), "ctx", 0, 0, 1))
        up = link.send(source, block(index), "ctx", 1, 0)
        passing.append((index, up, link.send(source, block(index), "ctx", -1, 0)))

    def ring_job():
        far = []
        for number in range(8):
            yield 10.0 + 3.8 * number
            index, up, down = passing[number]
            up.wait_recv()
            if number % 2 == 0:
                far.append((index, link.send(block(index, 3), block(index, 3), "ctx", 1, 0)))
            sibs.append(link.send(block(index, 3), block(index, 3), "ctx", 0, 0, 1))
            down.wait_recv()
            if number % 2 == 1:
                far.append((index, link.send(block(index, 1), block(index, 1), "ctx", -1, 0)))
            sibs.append(link.send(block(index, 1), block(index, 1), "ctx", 0, 0, 1))
        for number, (index, copy) in enumerate(far):
            yield 38.0 + number
            copy.wait_recv()
            sibs.append(link.send(block(index, 2), block(index, 2), "ctx", 0, 0, 1))
        yield 50.0
        for copy in sibs:
            copy.wait_recv()

    def kv_job():
        yield 0.0
        copy = link.send(kv_send, kv_other, "shard", 0, 1)
        yield 9.0
        copy.wait_recv()

    run(
        gather_job(link, "shard", w_out.at[mine], lambda i: out_full.at[i, mine], share, 0.0, 4.0),
        exchange_job(link, "shard", lambda i: small, lambda i: smalls.at[i], 0.0, 9.0),
        kv_job(),
        gather_halves(link, "shard", tokens, lambda i: token_rows.at[i], None, 0.1, 12.0),
        ring_job(),
    )


def qkv_kernel(link, queries, kv, queries_got, kv_all, kv_got, kv_own):
    link.greet(whole("shard") + near("ctx") + SIBLING)
    core = lax.rem(lax.axis_index("ctx"), 2)

    def kv_job():
        yield from exchange_job(link, "shard", lambda i: kv.at[i], lambda i: kv_got.at[i], 0.0, 6.0)
        for head in range(KV_HEADS):
            kv_own[:, head * 128 : (head + 1) * 128] = kv_got[2 * head] + kv_got[2 * head + 1]
        slot = lambda i: kv_all.at[i * 2 + core]
        sibs = []

        def share(index, block):
            sibs.append(link.send(block, slot(index), "ctx", 0, 0, 1))

        yield from gather_job(link, "ctx", kv_own, slot, share, 6.0, 2.7)
        for copy in sibs:
            copy.wait_recv()

    run(
        kv_job(),
        exchange_job(link, "shard", lambda i: queries.at[i], lambda i: queries_got.at[i], 0.1, 30.0),
    )


def column_block(ref, index, width=LANES):
    return ref.at[:, pl.ds(pl.multiple_of(index * width, width), width)]


def spread(link, summed, full, gather, start=0.0, block=10.8):
    core = lax.rem(lax.axis_index("ctx"), 2)
    slot = lambda i: column_block(full, core * 8 + i)
    sibs = []

    def share(index, source):
        sibs.append(link.send(source, slot(index), "ctx", 0, 0, 1))

    def share_half(source, index, k):
        half = source.shape[0]
        sibs.append(link.send(source, slot(index).at[pl.ds(k * half, half)], "ctx", 0, 0, 1))

    yield from gather(link, "ctx", summed, slot, share if gather is gather_job else share_half, start, block)
    for copy in sibs:
        copy.wait_recv()


def contract_rows(left, right):
    return lax.dot_general(left, right, (((0,), (0,)), ((), ())), preferred_element_type=F32)


def ffn_kernel(link, own, og, w_gate, w_up, w_down, attended, result, down_parts, summed, attended_cols,
               rows_all, gate_t, up_t, inner_t, parts, land_a, work_a, theirs, sib, land_b, work_b):
    link.greet(whole("shard") + near("ctx") + SIBLING)
    core = lax.rem(lax.axis_index("ctx"), 2)
    count = own.shape[0]
    ff = w_gate.shape[0]
    here = lambda ref, i: ref.at[pl.ds(pl.multiple_of(i * count, count), count)]
    token_lanes = lambda i: pl.ds(pl.multiple_of(i * count, count), count)

    def pair_of(ref, slots):
        return jnp.concatenate([here(ref, i)[...] for i in slots], axis=0)

    def forward(*offsets):
        slots = [chip("shard", r, p) for r, p in offsets]
        x = pair_of(rows_all, slots)
        gate = times_transposed(w_gate[...], x)
        up = times_transposed(w_up[...], x)
        inner_grad = times_transposed(w_down[...], pair_of(og, slots))
        sigmoid = 1.0 / (1.0 + jnp.exp(-gate))
        activated = gate * sigmoid
        inner = (activated * up).astype(LOW)
        gate_grad = (inner_grad * up * sigmoid * (1.0 + gate * (1.0 - sigmoid))).astype(LOW)
        up_grad = (inner_grad * activated).astype(LOW)
        for k, i in enumerate(slots):
            lanes = slice(k * count, k * count + count)
            inner_t[:, token_lanes(i)] = inner[:, lanes]
            gate_t[:, token_lanes(i)] = gate_grad[:, lanes]
            up_t[:, token_lanes(i)] = up_grad[:, lanes]
        return slots

    def tokens_of(ref, slots):
        return jnp.concatenate([ref[:, token_lanes(i)] for i in slots], axis=1)

    def back(slots):
        gates, ups = tokens_of(gate_t, slots), tokens_of(up_t, slots)
        for c in range(2):
            some = slice(c * 1024, c * 1024 + 1024)
            block = contract_rows(gates, w_gate[:, some]) + contract_rows(ups, w_up[:, some])
            for k, i in enumerate(slots):
                parts[i, :, some] = block[k * count : k * count + count].astype(LOW)

    def down(slots):
        inners = tokens_of(inner_t, slots)
        for c in range(2):
            some = slice(c * 1024, c * 1024 + 1024)
            block = contract_rows(inners, w_down[:, some])
            for k, i in enumerate(slots):
                down_parts[i, :, some] = block[k * count : k * count + count].astype(LOW)

    def every(*offsets):
        slots = forward(*offsets)
        back(slots)
        down(slots)

    last_pair_slots = []

    def compute_job():
        yield 15.0
        every((0, 0), (0, 1))
        yield 21.5
        every((1, 0), (3, 0))
        yield 33.0
        every((2, 0), (1, 1))
        yield 36.0
        slots = forward((3, 1), (2, 1))
        back(slots)
        last_pair_slots.append(slots)

    run(
        gather_halves(link, "shard", own, lambda i: here(rows_all, i)),
        compute_job(),
    )

    ring = chip("ctx") // 2

    def weight_columns(target, half, further, extra=None):
        wide = lax.rem(ring + further, 4)
        columns = pl.ds(pl.multiple_of(half * 1024 + wide * 256, 256), 256)
        into = pl.ds(pl.multiple_of(wide * 256, 256), 256)
        for i, (left, right) in enumerate(((gate_t, rows_all), (up_t, rows_all), (inner_t, og))):
            some = slice(i * ff, i * ff + ff)
            block = times(left[...], right[:, columns])
            if extra is not None:
                block = block + extra[some, into].astype(F32)
            target[some, into] = block.astype(LOW)
        return wide

    def weight_job():
        copies = {}

        def give(further):
            wide = weight_columns(theirs, 1 - core, further)
            copies[further] = link.send(
                column_block(theirs, wide, 256), column_block(sib, wide, 256), "ctx", 0, 0, 1
            )

        def take(further):
            copies[further].wait_recv()
            weight_columns(sib, core, further, sib)

        yield 0.1
        give(2)
        yield 1.0
        give(1)
        yield 2.0
        take(2)
        scatter = scatter_job(link, "ctx", lambda i: column_block(sib, i), land_b, work_b, summed, 6.0, 10.8)
        yield 3.0
        give(3)
        take(1)
        next(scatter)
        later = next(scatter)
        yield 4.0
        down(last_pair_slots[0])
        yield 5.0
        give(0)
        take(3)
        yield 6.0
        take(0)
        yield later
        yield from scatter

    run(
        scatter_job(link, "shard", lambda i: parts.at[i], land_a, work_a, result),
        weight_job(),
        exchange_job(
            link, "shard", lambda i: column_block(attended, i, 256), lambda i: here(attended_cols, i), 42.0, 14.0
        ),
    )


def swap_lanes(values):
    width = values.shape[1]
    low_half = lax.broadcasted_iota(jnp.int32, values.shape, 1) % HEAD < 32
    return jnp.where(low_half, pltpu.roll(values, width - 32, 1), pltpu.roll(values, 32, 1))


def tail_kernel(link, kv_parts, summed, hidden, queries, attended_cols, cosine, sine, normed, w_query, w_key, w_value,
                gains, full, attn_full, result, gain_sum,
                hidden_rows, query_cols, kv_cols, kv_w, left_t, parts, land_a, work_a,
                theirs, sib, land_b, work_b, attn_summed, sib_k, land_k, work_k, kv_grad, kv_turned,
                gain_buf, gain_land, gain_work, gain_ctx):
    link.greet(whole("shard") + whole("ctx") + SIBLING)
    core = lax.rem(lax.axis_index("ctx"), 2)
    leads = lax.rem(lax.axis_index("shard"), 2) == 0
    count = hidden.shape[0]
    here = lambda ref, i: ref.at[pl.ds(pl.multiple_of(i * count, count), count)]
    scatter = scatter_halves(link, "shard", lambda i: parts.at[i], land_a, work_a, result, 37.0)

    def make(*offsets):
        slots = [chip("shard", r, p) for r, p in offsets]
        pair_of = lambda ref: jnp.concatenate([here(ref, i)[...] for i in slots], axis=0)
        block = times(pair_of(query_cols), w_query[...]) + times(pair_of(kv_cols), kv_w[...])
        for k, i in enumerate(slots):
            parts[i] = block[k * count : k * count + count].astype(LOW)
        terms = block * pair_of(normed).astype(F32)
        return jnp.sum(terms, axis=0, keepdims=True)

    def main_job():
        yield 0.0
        copies = [
            link.send(kv_parts.at[i * 2 + 1 - core], sib_k.at[i], "ctx", 0, 0, 1) for i in range(8)
        ]
        for half, mine in enumerate((leads, jnp.logical_not(leads))):
            for which, weight in enumerate((w_key, w_value)):
                row = which * 64 + half * 32
                kv_w[row : row + 32, :] = jnp.where(mine, weight[...], jnp.zeros((32, D), LOW))
        yield 3.0
        for i, copy in enumerate(copies):
            copy.wait_recv()
            add_rows(sib_k.at[i], [sib_k.at[i], kv_parts.at[i * 2 + core]])
        yield from scatter_job(link, "ctx", lambda i: sib_k.at[i], land_k, work_k, kv_grad, 4.0, 2.7)
        me = chip("shard")
        own_cosine, own_sine = here(cosine, me)[...], here(sine, me)[...]
        key_lanes = lax.broadcasted_iota(jnp.int32, own_cosine.shape, 1) < HEAD
        for head in range(KV_HEADS):
            lanes = slice(head * 128, head * 128 + 128)
            both = kv_grad[:, lanes]
            turned = both * own_cosine - swap_lanes(both) * own_sine
            kv_turned[:, lanes] = jnp.where(key_lanes, turned, both).astype(LOW)
        part = lambda i: kv_turned.at[:, pl.ds(pl.multiple_of(i // 2 * 128, 128), 128)]
        yield from exchange_job(link, "shard", part, lambda i: here(kv_cols, i), 24.0, 10.0)
        total = make((2, 1), (1, 1))
        total = total + make((3, 1), (3, 0))
        total = total + make((1, 0), (2, 0))
        next(scatter)
        later = next(scatter)
        total = total + make((0, 0), (0, 1))
        for i in range(8):
            gain_buf[i] = gains[i]
            gain_buf[i, 0:1, :] = total[:, i * 256 : i * 256 + 256]
        yield later
        yield from scatter

    def weight_job():
        yield 41.0
        left_t[0:256, :] = jnp.transpose(query_cols[...].astype(F32)).astype(LOW)
        left_t[256:384, :] = jnp.transpose(kv_cols[...].astype(F32)).astype(LOW)
        left_t[384:640, :] = jnp.transpose(attended_cols[...].astype(F32)).astype(LOW)

        def columns(target, half, add):
            for c in range(4):
                wide = pl.ds(pl.multiple_of(half * 1024 + c * 256, 256), 256)
                into = slice(c * 256, c * 256 + 256)
                for rows, right in ((slice(0, 384), normed), (slice(384, 640), hidden_rows)):
                    block = times(left_t[rows, :], right[:, wide])
                    if add:
                        block = block + target[rows, into].astype(F32)
                    target[rows, into] = block.astype(LOW)

        columns(theirs, 1 - core, False)
        copy = link.send(theirs, sib, "ctx", 0, 0, 1)
        yield 43.5
        copy.wait_recv()
        columns(sib, core, True)
        block = lambda i: column_block(sib, i)
        yield from scatter_job(link, "ctx", block, land_b, work_b, attn_summed, 46.0, 4.5)
        yield from spread(link, attn_summed, attn_full, gather_job, 70.0, 4.0)

    def gain_job():
        yield from exchange_job(link, "shard", lambda i: gain_buf.at[i], lambda i: gain_land.at[i], 40.0, 10.0)
        gain_work[0] = sum(gain_land[i] for i in range(8))
        copy = link.send(gain_work.at[0], gain_work.at[1], "ctx", 0, 0, 1)
        yield 53.0
        copy.wait_recv()
        gain_work[2] = gain_work[0] + gain_work[1]
        copies = [
            link.send(gain_work.at[2], gain_ctx.at[i], "ctx", r, p) for i, (r, p) in enumerate(ALL)
        ]
        yield 69.0
        for copy in copies:
            copy.wait_recv()
        gain_sum[...] = gain_work[2] + sum(gain_ctx[i] for i in range(7))

    columns_of = lambda ref: lambda i: ref.at[:, pl.ds(pl.multiple_of(i * 256, 256), 256)]
    run(
        main_job(),
        exchange_job(link, "shard", columns_of(queries), lambda i: here(query_cols, i), 0.1, 22.0),
        gather_halves(link, "shard", hidden, lambda i: here(hidden_rows, i), None, 0.2, 12.0),
        spread(link, summed, full, gather_halves, 10.0),
        gain_job(),
        weight_job(),
    )


def first_kernel(pair_ref, tokens, gain, w_query, w_key, w_value, kv_other, cosine, sine,
                 normed_ref, q_ref, kv_ref, w_kv):
    @pl.when(pl.program_id(0) == 0)
    def _():
        leads = pair_ref[0] == 0
        nothing = jnp.zeros((32, D), LOW)
        choose = lambda yes, ref, other: jnp.where(yes, ref[...], other)
        w_kv[0:32, :] = choose(leads, w_key, nothing)
        w_kv[32:64, :] = choose(leads, kv_other, nothing)
        w_kv[64:96, :] = choose(jnp.logical_not(leads), kv_other, nothing)
        w_kv[96:128, :] = choose(jnp.logical_not(leads), w_value, nothing)

    values = tokens[...].astype(F32)
    normed = rms_forward(values, gain[...])[0].astype(LOW)
    normed_ref[...] = normed
    cosine, sine = cosine[...], sine[...]
    turn = lambda v: v * cosine + swap_lanes(v) * sine
    q = times_transposed(normed, w_query[...])
    for i in range(2):
        lanes = slice(i * 128, i * 128 + 128)
        q_ref[:, :, lanes] = turn(q[:, lanes]).astype(LOW).reshape(2, 128, 128)
    kv = times_transposed(normed, w_kv[...])
    keys = lax.broadcasted_iota(jnp.int32, kv.shape, 1) < HEAD
    kv_ref[...] = jnp.where(keys, turn(kv), kv).astype(LOW).reshape(2, 128, 128)


def first_part(pair, token_rows, gain, w_query, w_key, w_value, kv_other, cosine, sine):
    held = lambda *dims: pl.BlockSpec(dims, lambda i, *_: (0,) * len(dims))
    rows = lambda width: pl.BlockSpec((256, width), lambda i, *_: (i, 0))
    slots = lambda width: pl.BlockSpec((2, 128, width), lambda i, *_: (i, 0, 0))
    return pl.pallas_call(
        first_kernel,
        grid_spec=pltpu.PrefetchScalarGridSpec(
            num_scalar_prefetch=1,
            grid=(4,),
            in_specs=[rows(D), held(1, D), held(256, D), held(32, D), held(32, D), held(32, D), rows(128), rows(128)],
            out_specs=[rows(D), slots(256), slots(128)],
            scratch_shapes=[pltpu.VMEM((128, D), LOW)],
        ),
        out_shape=[shape((1024, D), LOW), shape((8, 128, 256), LOW), shape((8, 128, 128), LOW)],
        compiler_params=pltpu.CompilerParams(vmem_limit_bytes=VMEM_LIMIT),
        cost_estimate=pl.CostEstimate(flops=1 << 31, bytes_accessed=10 << 20, transcendentals=1024),
    )(pair, token_rows, gain, w_query, w_key, w_value, kv_other, cosine, sine)


BLOCK = 512
LOG2E = 1.4426950408889634
GROUPS = 1
COLUMNS = 512 // GROUPS


def sort_keys(order_ref, kv_ref, sorted_ref, flipped_ref):
    for c in range(16):
        lead = pl.multiple_of(order_ref[c] * 64, 64)
        trail = pl.multiple_of((31 - order_ref[c]) * 64, 64)
        sorted_ref[pl.ds(lead, 64), :] = kv_ref[c, 0:64, :]
        sorted_ref[pl.ds(trail, 64), :] = kv_ref[c, 64:128, :]
    for i in range(2048 // BLOCK):
        rows = slice(i * BLOCK, (i + 1) * BLOCK)
        flipped_ref[i] = jnp.transpose(sorted_ref[rows, :].astype(F32)).astype(LOW)


def spread_heads(blocks, high):
    pieces = []
    for block in blocks:
        block = block.astype(F32)
        turned = pltpu.roll(block, 64, 1)
        lane = lax.broadcasted_iota(jnp.int32, block.shape, 1)
        keep = (lane >= 64) if high else (lane < 64)
        first, second = (turned, block) if high else (block, turned)
        pieces += [jnp.where(keep, first, 0.0), jnp.where(keep, second, 0.0)]
    return jnp.concatenate(pieces, axis=0)


def join_heads(flipped):
    upright = jnp.transpose(flipped)
    return [
        jnp.concatenate([upright[i * 128 : i * 128 + 64], upright[i * 128 + 64 : i * 128 + 128]], axis=1)
        for i in range(4)
    ]


def query_blocks(ref, run):
    rows = slice(run * 64, run * 64 + 64)
    return [ref[s, rows, p * 128 : p * 128 + 128] for s in range(2) for p in range(2)]


def row_blocks(ref, run):
    rows = slice(run * 64, run * 64 + 64)
    return [ref[rows, i * 128 : i * 128 + 128] for i in range(4)]


def above(block, first_place):
    key = lax.broadcasted_iota(jnp.int32, (BLOCK, COLUMNS), 0) + block * BLOCK
    query = lax.broadcasted_iota(jnp.int32, (BLOCK, COLUMNS), 1) % 64 + first_place
    return key > query


def dot_kt(left, right):
    return lax.dot_general(left, right, (((1,), (1,)), ((), ())), preferred_element_type=F32)


def column_groups(values, axis):
    pieces = [slice(i * COLUMNS, (i + 1) * COLUMNS) for i in range(GROUPS)]
    return [values[p] if axis == 0 else values[:, p] for p in pieces]


def attend_kernel(order_ref, own_ref, q_ref, kv_ref, w_ref, x_ref, gain_ref, out_ref, lse_ref, hidden_ref, normed_ref,
                  sorted_ref, flipped_ref):
    sort_keys(order_ref, kv_ref, sorted_ref, flipped_ref)
    factor = HEAD**-0.5 * LOG2E
    for run in range(2):
        first_place = jnp.where(run == 0, own_ref[0], 31 - own_ref[0]) * 64
        last = first_place // BLOCK
        q = column_groups(spread_heads(query_blocks(q_ref, run), False).astype(LOW), 0)

        def step(block, carry, masked):
            rows = pl.ds(pl.multiple_of(block * BLOCK, BLOCK), BLOCK)
            keys, values = sorted_ref[rows, :], flipped_ref[block, 64:128, :]
            after = []
            for queries, (largest, total, mixed) in zip(q, carry):
                scores = dot_kt(keys, queries) * factor
                if masked:
                    scores = jnp.where(above(block, first_place), NEG, scores)
                top = jnp.maximum(largest, jnp.max(scores, axis=0, keepdims=True))
                fade = jnp.exp2(largest - top)
                exps = jnp.exp2(scores - top)
                total = total * fade + jnp.sum(exps, axis=0, keepdims=True)
                mixed = mixed * fade + times(values, exps.astype(LOW))
                after.append((top, total, mixed))
            return tuple(after)

        nothing = lambda rows, fill: jnp.full((rows, COLUMNS), fill, F32)
        carry = tuple((nothing(1, NEG), nothing(1, 0.0), nothing(64, 0.0)) for _ in range(GROUPS))
        carry = lax.fori_loop(0, last, functools.partial(step, masked=False), carry)
        carry = step(last, carry, True)
        mixed = jnp.concatenate([m / t for _, t, m in carry], axis=1)
        for i, block in enumerate(join_heads(mixed)):
            out_ref[run * 64 : run * 64 + 64, i * 128 : i * 128 + 128] = block.astype(LOW)
        lse_ref[0, run : run + 1, :] = jnp.concatenate([l + jnp.log2(t) for l, t, _ in carry], axis=1)

    @pl.when(pl.program_id(0) == 0)
    def _():
        hidden_ref[...] = x_ref[...].astype(F32)

    hidden_ref[...] += times(out_ref[...], w_ref[...])

    @pl.when(pl.program_id(0) == KV_HEADS - 1)
    def _():
        normed_ref[...] = rms_forward(hidden_ref[...], gain_ref[...])[0].astype(LOW)


def attend_back_kernel(order_ref, own_ref, q_ref, kv_ref, out_ref, hidden_ref, w_ref, lse_ref, cos_ref, sin_ref,
                       dq_ref, dkv_ref, sorted_ref, flipped_ref, total_ref, grad_ref):
    grad_ref[...] = times_transposed(hidden_ref[...], w_ref[...]).astype(LOW)
    sort_keys(order_ref, kv_ref, sorted_ref, flipped_ref)
    total_ref[...] = jnp.zeros_like(total_ref)
    scale = HEAD**-0.5
    factor = scale * LOG2E
    for run in range(2):
        first_place = jnp.where(run == 0, own_ref[0], 31 - own_ref[0]) * 64
        last = first_place // BLOCK
        q = column_groups(spread_heads(query_blocks(q_ref, run), False).astype(LOW), 0)
        grad_wide = spread_heads(row_blocks(grad_ref, run), True)
        out_wide = spread_heads(row_blocks(out_ref, run), True)
        grad = column_groups(grad_wide.astype(LOW), 0)
        inner = lax.dot_general(
            jnp.ones((8, 128), F32),
            grad_wide * out_wide,
            (((1,), (1,)), ((), ())),
            precision=lax.Precision.HIGHEST,
            preferred_element_type=F32,
        )[:1]
        inner = column_groups(inner, 1)
        lse = column_groups(lse_ref[0, run : run + 1, :], 1)

        def step(block, dq, masked):
            rows = pl.ds(pl.multiple_of(block * BLOCK, BLOCK), BLOCK)
            kv, keys = sorted_ref[rows, :], flipped_ref[block, 0:64, :]
            after, total = [], total_ref[rows, :]
            for i in range(GROUPS):
                probs = jnp.exp2(dot_kt(kv, q[i]) * factor - lse[i])
                if masked:
                    probs = jnp.where(above(block, first_place), 0.0, probs)
                score_grad = (probs * (dot_kt(kv, grad[i]) - inner[i])).astype(LOW)
                total = total + times(score_grad, q[i]) + times(probs.astype(LOW), grad[i])
                after.append(dq[i] + times(keys, score_grad))
            total_ref[rows, :] = total
            return tuple(after)

        dq = tuple(jnp.zeros((64, COLUMNS), F32) for _ in range(GROUPS))
        dq = lax.fori_loop(0, last, functools.partial(step, masked=False), dq)
        dq = jnp.concatenate(step(last, dq, True), axis=1)
        cosine, sine = cos_ref[run * 64 : run * 64 + 64, :], sin_ref[run * 64 : run * 64 + 64, :]
        low_half = lax.broadcasted_iota(jnp.int32, (64, 128), 1) % 64 < 32
        for i, block in enumerate(join_heads(dq * scale)):
            turned = jnp.where(low_half, pltpu.roll(block, 96, 1), pltpu.roll(block, 32, 1))
            dq_ref[run * 64 : run * 64 + 64, i * 128 : i * 128 + 128] = (
                block * cosine - turned * sine
            ).astype(LOW)
    weight = jnp.where(lax.broadcasted_iota(jnp.int32, (64, 128), 1) < 64, scale, 1.0)
    for c in range(16):
        lead = pl.multiple_of(order_ref[c] * 64, 64)
        trail = pl.multiple_of((31 - order_ref[c]) * 64, 64)
        dkv_ref[c, 0:64, :] = (total_ref[pl.ds(lead, 64), :] * weight).astype(LOW)
        dkv_ref[c, 64:128, :] = (total_ref[pl.ds(trail, 64), :] * weight).astype(LOW)


def attention_call(kernel, scalars, inputs, kinds, outputs, out_kinds, scratch, flops):
    specs = {
        "q": pl.BlockSpec((2, 128, 256), lambda g, *_: (g, 0, 0)),
        "kv": pl.BlockSpec((16, 128, 128), lambda g, *_: (0, 0, g)),
        "rows": pl.BlockSpec((128, 512), lambda g, *_: (0, g)),
        "lse": pl.BlockSpec((1, 8, 512), lambda g, *_: (g, 0, 0)),
        "table": pl.BlockSpec((128, 128), lambda g, order, own: (own[1], 0)),
        "weight": pl.BlockSpec((512, D), lambda g, *_: (g, 0)),
        "held": pl.BlockSpec((128, D), lambda g, *_: (0, 0)),
        "gain": pl.BlockSpec((1, D), lambda g, *_: (0, 0)),
    }
    keys = [pltpu.VMEM((2048, 128), LOW), pltpu.VMEM((2048 // BLOCK, 128, BLOCK), LOW)]
    return pl.pallas_call(
        kernel,
        grid_spec=pltpu.PrefetchScalarGridSpec(
            num_scalar_prefetch=2,
            grid=(KV_HEADS,),
            in_specs=[specs[k] for k in kinds],
            out_specs=[specs[k] for k in out_kinds],
            scratch_shapes=keys + scratch,
        ),
        out_shape=outputs,
        compiler_params=pltpu.CompilerParams(vmem_limit_bytes=VMEM_LIMIT),
        cost_estimate=pl.CostEstimate(flops=flops, bytes_accessed=8 << 20, transcendentals=8 << 20),
    )(*scalars, *inputs)


def attend(queries, kv_all, w_out, tokens, gain, order, own):
    whole_rows = lambda kind: jax.ShapeDtypeStruct((128, D), kind)
    return attention_call(
        attend_kernel,
        (order, own),
        (queries, kv_all, w_out, tokens, gain),
        ("q", "kv", "weight", "held", "gain"),
        [whole_rows(LOW), jax.ShapeDtypeStruct((4, 8, 512), F32), whole_rows(F32), whole_rows(LOW)],
        ("rows", "lse", "held", "held"),
        [],
        1 << 33,
    )


def attend_back(queries, kv_all, attended, hidden_low, w_out, lse, cosine, sine, order, own):
    return attention_call(
        attend_back_kernel,
        (order, own),
        (queries, kv_all, attended, hidden_low, w_out, lse, cosine, sine),
        ("q", "kv", "rows", "held", "weight", "lse", "table", "table"),
        [jax.ShapeDtypeStruct((128, D), LOW), jax.ShapeDtypeStruct((16, 128, 512), LOW)],
        ("rows", "kv"),
        [pltpu.VMEM((2048, 128), F32), pltpu.VMEM((128, 512), LOW)],
        1 << 34,
    )


def local(
    tokens,
    positions,
    out_grad,
    attn_gain,
    w_query,
    w_key,
    w_value,
    w_out,
    ffn_gain,
    w_gate,
    w_up,
    w_down,
):
    rows = tokens.shape[0]
    shard, ctx = lax.axis_index("shard"), lax.axis_index("ctx")
    shard_pair, core = shard % 2, ctx % 2
    places = positions[0]
    own_places = lax.dynamic_slice_in_dim(places, ctx * rows, rows)

    small = jnp.stack(
        [attn_gain, ffn_gain, jnp.concatenate([own_places // 64, own_places % 64]).astype(LOW)]
    )
    small = jnp.concatenate([small, jnp.zeros((13, 256), LOW)], axis=0)
    token_rows, smalls, kv_other, out_full = comm_call(
        front_kernel,
        0,
        [tokens, small, jnp.where(shard_pair == 0, w_value, w_key), w_out],
        [ANY] * 4,
        [shape((8, rows, D), LOW), shape((8, 16, 256), LOW), shape((32, D), LOW), shape((8, 256, D), LOW)],
        [ANY] * 4,
    )
    out_grad_late, token_rows = lax.optimization_barrier((out_grad, token_rows))
    out_grad_rows = lax.all_gather(out_grad_late, "shard", axis=0, tiled=True)
    token_rows, out_full = token_rows.reshape(-1, D), out_full.reshape(D, D)
    gain_one = smalls[:, 0].reshape(-1).astype(F32)
    gain_two = smalls[:, 1].reshape(-1).astype(F32)
    place_rows = (smalls[:, 2, :rows].astype(F32) * 64.0 + smalls[:, 2, rows:].astype(F32)).reshape(-1)
    cosine, sine = wide_tables(place_rows, 2)
    normed_rows, queries, kv_part = first_part(
        shard_pair[None], token_rows, gain_one[None], w_query, w_key, w_value, kv_other, cosine, sine
    )
    queries, kv_all = comm_call(
        qkv_kernel,
        1,
        [queries, kv_part],
        [ANY] * 2,
        [shape((8, rows, 256), LOW), shape((16, rows, 512), LOW)],
        [ANY] * 2,
        [pltpu.VMEM((8, rows, 128), LOW), pltpu.VMEM((rows, 512), LOW)],
    )

    order = places.reshape(16, rows)[:, 0] // 64
    own_order = jnp.stack([own_places[0] // 64, shard])
    attended, lse, hidden_state, normed_two = attend(
        queries, kv_all, out_full, tokens, gain_two[None], order, own_order
    )
    ff = w_gate.shape[0]
    vmem = lambda count, *dims: pltpu.VMEM((count, *dims), LOW)
    normed_two_grad, down_parts, summed, attended_cols = comm_call(
        ffn_kernel,
        3,
        [normed_two, out_grad_rows, w_gate, w_up, w_down, attended],
        [ANY] + [INSIDE] * 4 + [ANY],
        [shape((rows, D), F32), shape((8, rows, D), LOW), shape((3 * ff, LANES), LOW), shape((8 * rows, 256), LOW)],
        [INSIDE] * 3 + [ANY],
        [
            vmem(8 * rows, D),
            vmem(ff, 8 * rows),
            vmem(ff, 8 * rows),
            vmem(ff, 8 * rows),
            vmem(8, rows, D),
            vmem(7, rows, D),
            vmem(3, rows, D),
            vmem(3 * ff, 1024),
            vmem(3 * ff, 1024),
            vmem(7, 3 * ff, LANES),
            vmem(3, 3 * ff, LANES),
        ],
        62 * 1024 * 1024,
    )
    down_parts = down_parts.reshape(-1, D)
    down_sum = lax.psum_scatter(down_parts, "shard", scatter_dimension=0, tiled=True)
    outputs = (hidden_state + down_sum.astype(F32)).astype(LOW)
    inverse_two = inverse_of(hidden_state)
    gain_two_part = jnp.sum(normed_two_grad * hidden_state * inverse_two, axis=0)
    hidden_grad = out_grad.astype(F32) + rms_backward(
        hidden_state, inverse_two, gain_two, normed_two_grad
    )
    hidden_low = hidden_grad.astype(LOW)
    query_pre_grad, kv_parts = attend_back(
        queries, kv_all, attended, hidden_low, out_full, lse, cosine, sine, order, own_order
    )
    inputs = tokens.astype(F32)
    gains = jnp.zeros((8, 8, 256), F32).at[:, 1].set(gain_two_part.reshape(8, 256))
    ffn_full, attn_full, normed_grad, gain_sum = comm_call(
        tail_kernel,
        4,
        [kv_parts, summed, hidden_low, query_pre_grad, attended_cols, cosine, sine, normed_rows]
        + [w_query, w_key, w_value, gains],
        [INSIDE, INSIDE, ANY, ANY] + [INSIDE] * 8,
        [shape((3 * ff, D), LOW), shape((640, D), LOW), shape((rows, D), F32), shape((8, 256), F32)],
        [ANY, ANY, INSIDE, INSIDE],
        [
            vmem(8 * rows, D),
            vmem(8 * rows, 256),
            vmem(8 * rows, 128),
            vmem(128, D),
            vmem(640, 8 * rows),
            vmem(8, rows, D),
            vmem(7, rows, D),
            vmem(3, rows, D),
            vmem(640, 1024),
            vmem(640, 1024),
            vmem(7, 640, LANES),
            vmem(3, 640, LANES),
            vmem(640, LANES),
            vmem(8, rows, 512),
            vmem(7, rows, 512),
            vmem(3, rows, 512),
            pltpu.VMEM((rows, 512), F32),
            vmem(rows, 512),
            pltpu.VMEM((8, 8, 256), F32),
            pltpu.VMEM((8, 8, 256), F32),
            pltpu.VMEM((3, 8, 256), F32),
            pltpu.VMEM((7, 8, 256), F32),
        ],
    )
    gate_wgrad, up_wgrad, down_wgrad = (
        ffn_full[i * ff : (i + 1) * ff].astype(F32) for i in range(3)
    )
    inverse_one = inverse_of(inputs)
    input_grad = hidden_grad + rms_backward(inputs, inverse_one, gain_one, normed_grad)
    attn_rows = lambda start, size: lax.dynamic_slice_in_dim(attn_full, start, size).astype(F32)
    query_wgrad, out_wgrad = attn_rows(0, 256), attn_rows(384, 256)
    key_wgrad, value_wgrad = attn_rows(256 + shard_pair * 32, 32), attn_rows(320 + shard_pair * 32, 32)
    return (
        outputs,
        input_grad,
        gain_sum[0] / attn_gain.astype(F32),
        query_wgrad,
        key_wgrad,
        value_wgrad,
        out_wgrad,
        gain_sum[1],
        gate_wgrad,
        up_wgrad,
        down_wgrad,
    )


def solution(mesh):
    rows = P(("shard", "ctx"), None)
    matrix = P("shard", None)
    vector = P("shard")
    in_specs = (rows, matrix, rows, vector, matrix, matrix, matrix, matrix, vector) + (matrix,) * 3
    out_specs = (rows, rows, vector, matrix, matrix, matrix, matrix, vector) + (matrix,) * 3
    return jax.shard_map(local, mesh=mesh, in_specs=in_specs, out_specs=out_specs, check_vma=False)
```

```python
import functools

import jax
import jax.numpy as jnp
from jax import lax
from jax.experimental import pallas as pl
from jax.experimental.pallas import tpu as pltpu
from jax.sharding import PartitionSpec as P

D = 2048
HEADS = 32
KV_HEADS = 4
HEAD = 64
LANES = 128

EPS = 1e-05
BASE = 10000.0
NEG = -1e30
F32 = jnp.float32
LOW = jnp.bfloat16
MESH = pl.DeviceIdType.MESH
VMEM_LIMIT = 56 * 1024 * 1024


def times(left, right):
    return jnp.dot(left, right, preferred_element_type=F32)


def times_transposed(left, right):
    return lax.dot_general(left, right, (((1,), (1,)), ((), ())), preferred_element_type=F32)


def transposed_times(left, right):
    return lax.dot_general(left, right, (((0,), (0,)), ((), ())), preferred_element_type=F32)


def rope_tables(places, width):
    half = width // 2
    freqs = BASE ** (-(jnp.arange(half).astype(F32) * 2.0 / width))
    angles = places.astype(F32)[:, None] * freqs[None, :]
    return jnp.cos(angles), jnp.sin(angles)


def wide_tables(places, heads):
    cosine, sine = rope_tables(places, HEAD)
    return (
        jnp.tile(jnp.concatenate([cosine, cosine], axis=1), (1, heads)),
        jnp.tile(jnp.concatenate([-sine, sine], axis=1), (1, heads)),
    )


def inverse_of(values):
    return lax.rsqrt(jnp.mean(values * values, axis=-1, keepdims=True) + EPS)


def rms_forward(values, gain):
    inverse = inverse_of(values)
    return (values * inverse * gain, inverse)


def rms_backward(values, inverse, gain, grads):
    scaled = grads * gain
    return inverse * scaled - values * inverse * inverse * inverse * jnp.mean(
        scaled * values, axis=-1, keepdims=True
    )


def at(axis, ring, pair, core=0):
    index = lax.axis_index(axis)
    cores = 2 if axis == "ctx" else 1
    ring_at = lax.rem(index // (2 * cores) + ring % 4, 4)
    pair_at = lax.rem(lax.rem(index // cores, 2) + pair, 2)
    core_at = lax.rem(lax.rem(index, cores) + core, cores)
    return (ring_at * 2 + pair_at) * cores + core_at


def chip(axis, ring=0, pair=0):
    return at(axis, ring, pair) // (2 if axis == "ctx" else 1)


class Link:
    def __init__(self, send_sems, recv_sems, local_sems):
        self.send_sems, self.recv_sems, self.local_sems = send_sems, recv_sems, local_sems
        self.sent, self.kept = [], []

    def greet(self, offsets):
        barrier = pltpu.get_barrier_semaphore()
        for axis, ring, pair, core in offsets:
            pl.semaphore_signal(
                barrier, inc=1, device_id={axis: at(axis, ring, pair, core)}, device_id_type=MESH
            )
        pl.semaphore_wait(barrier, len(offsets))

    def send(self, source, target, axis, ring, pair, core=0):
        number = len(self.sent)
        copy = pltpu.make_async_remote_copy(
            src_ref=source,
            dst_ref=target,
            send_sem=self.send_sems.at[number],
            recv_sem=self.recv_sems.at[number],
            device_id={axis: at(axis, ring, pair, core)},
            device_id_type=MESH,
        )
        copy.start()
        self.sent.append(copy)
        return copy

    def keep(self, source, target):
        copy = pltpu.make_async_copy(source, target, self.local_sems.at[len(self.kept)])
        copy.start()
        self.kept.append(copy)
        return copy

    def kept_now(self, copy):
        copy.wait()
        self.kept = [None if other is copy else other for other in self.kept]

    def finish(self):
        for copy in self.kept:
            if copy is not None:
                copy.wait()
        for copy in self.sent:
            copy.wait_send()


NEAR = [(1, 0), (3, 0), (0, 1)]
ALL = [(r, p) for r in range(4) for p in range(2) if (r, p) != (0, 0)]
near = lambda axis: [(axis, r, p, 0) for r, p in NEAR]
whole = lambda axis: [(axis, r, p, 0) for r, p in ALL]
SIBLING = [("ctx", 0, 0, 1)]


def run(*jobs):
    waiting = [(next(job), number, job) for number, job in enumerate(jobs)]
    while waiting:
        waiting.sort(key=lambda entry: entry[:2])
        _, number, job = waiting.pop(0)
        after = next(job, None)
        if after is not None:
            waiting.append((after, number, job))


def gather_job(link, axis, own, slot, share=None, start=0.0, block=10.5):
    me, pair = chip(axis), chip(axis, 0, 1)
    sharing = lambda index: share(index, slot(index)) if share else None
    yield start
    kept = link.keep(own, slot(me))
    to_pair = link.send(own, slot(me), axis, 0, 1)
    down = link.send(own, slot(me), axis, -1, 0)
    up = link.send(own, slot(me), axis, 1, 0)
    if share:
        share(me, own)
    yield start + block + 3.0
    to_pair.wait_recv()
    pair_down = link.send(slot(pair), slot(pair), axis, -1, 0)
    pair_up = link.send(slot(pair), slot(pair), axis, 1, 0)
    sharing(pair)
    yield start + block + 3.1
    down.wait_recv()
    next_one = chip(axis, 1, 0)
    far_down = link.send(slot(next_one), slot(next_one), axis, -1, 0)
    sharing(next_one)
    yield start + block + 3.2
    up.wait_recv()
    sharing(chip(axis, -1, 0))
    yield start + 2 * block + 4.0
    pair_up.wait_recv()
    last_pair = chip(axis, -1, 1)
    far_up = link.send(slot(last_pair), slot(last_pair), axis, 1, 0)
    sharing(last_pair)
    yield start + 2 * block + 4.1
    pair_down.wait_recv()
    sharing(chip(axis, 1, 1))
    yield start + 3 * block + 5.0
    far_down.wait_recv()
    sharing(chip(axis, 2, 0))
    yield start + 3 * block + 5.1
    far_up.wait_recv()
    sharing(chip(axis, 2, 1))
    link.kept_now(kept)


def gather_halves(link, axis, own, slot, share=None, start=0.0, block=10.5):
    half = own.shape[0] // 2
    cut = lambda ref, k: ref.at[pl.ds(k * half, half)]
    piece = lambda index, k: cut(slot(index), k)
    me, pair, far = chip(axis), chip(axis, 0, 1), chip(axis, 2, 0)
    above_one, below_one = chip(axis, 1, 0), chip(axis, -1, 0)
    last_pair, next_pair, far_pair = chip(axis, -1, 1), chip(axis, 1, 1), chip(axis, 2, 1)
    sharing = lambda index, k: share(piece(index, k), index, k) if share else None
    pass_on = lambda index, k, ring, pair_: link.send(piece(index, k), piece(index, k), axis, ring, pair_)
    yield start
    kept = link.keep(own, slot(me))
    across, down, up = [], [], []
    for k in range(2):
        across.append(link.send(cut(own, k), piece(me, k), axis, 0, 1))
        down.append(link.send(cut(own, k), piece(me, k), axis, -1, 0))
        up.append(link.send(cut(own, k), piece(me, k), axis, 1, 0))
    if share:
        for k in range(2):
            share(cut(own, k), me, k)
    far_in, pair_up, pair_down, over = [], [], [], []
    for k in range(2):
        yield start + (k + 1) * block / 2 + 3.5
        down[k].wait_recv()
        up[k].wait_recv()
        far_in.append(pass_on(above_one, k, -1, 0) if k == 0 else pass_on(below_one, k, 1, 0))
        sharing(above_one, k)
        sharing(below_one, k)
        across[k].wait_recv()
        pair_up.append(pass_on(pair, k, 1, 0))
        pair_down.append(pass_on(pair, k, -1, 0))
        sharing(pair, k)
    link.kept_now(kept)
    for k in range(2):
        yield start + block + 7.0 + k * block / 2
        far_in[k].wait_recv()
        over.append(pass_on(far, k, 0, 1))
        sharing(far, k)
    yield start + 2.5 * block + 6.0
    for k in range(2):
        pair_up[k].wait_recv()
        sharing(last_pair, k)
        pair_down[k].wait_recv()
        sharing(next_pair, k)
    yield start + 2.5 * block + 9.0
    for k in range(2):
        over[k].wait_recv()
        sharing(far_pair, k)


def add_rows(target, terms):
    rows, width = target.shape
    step = max(s for s in range(16, rows + 1, 16) if rows % s == 0 and (s == 16 or s * width <= 32768))

    def body(i, _):
        some = pl.ds(pl.multiple_of(i * step, 16), step)
        total = terms[0][some, :].astype(F32)
        for term in terms[1:]:
            total = total + term[some, :].astype(F32)
        target[some, :] = total.astype(target.dtype)
        return 0

    lax.fori_loop(0, rows // step, body, 0)


def scatter_job(link, axis, part, landing, work, result, start=0.0, block=10.5):
    here = lambda ring, pair: part(chip(axis, ring, pair))
    yield start
    to_last = link.send(here(2, 1), landing.at[1], axis, -1, 0)
    to_next = link.send(here(2, 0), landing.at[0], axis, 1, 0)
    pair_up = link.send(here(1, 1), landing.at[2], axis, 1, 0)
    yield start + block + 3.0
    to_last.wait_recv()
    add_rows(work.at[0], [here(3, 1), landing.at[1]])
    pair_down = link.send(work.at[0], landing.at[4], axis, -1, 0)
    yield start + block + 4.0
    to_next.wait_recv()
    add_rows(work.at[1], [here(1, 0), landing.at[0]])
    yield start + 2 * block + 3.0
    pair_up.wait_recv()
    mine_up = link.send(work.at[1], landing.at[5], axis, 1, 0)
    mine_down = link.send(here(3, 0), landing.at[3], axis, -1, 0)
    yield start + 2 * block + 6.0
    pair_down.wait_recv()
    add_rows(work.at[2], [here(0, 1), landing.at[2], landing.at[4]])
    across = link.send(work.at[2], landing.at[6], axis, 0, 1)
    yield start + 3 * block + 7.0
    mine_down.wait_recv()
    mine_up.wait_recv()
    yield start + 3 * block + 10.0
    across.wait_recv()
    add_rows(result, [here(0, 0), landing.at[3], landing.at[5], landing.at[6]])


def scatter_halves(link, axis, part, landing, work, result, start=0.0, block=10.5):
    here = lambda ring, pair: part(chip(axis, ring, pair))
    half = result.shape[0] // 2
    cut = lambda ref, k: ref.at[pl.ds(k * half, half)]
    yield start
    far = link.send(here(2, 1), landing.at[0], axis, 0, 1)
    pair_up = link.send(here(1, 1), landing.at[1], axis, 1, 0)
    pair_down = link.send(here(3, 1), landing.at[2], axis, -1, 0)
    mine_up = [link.send(cut(here(1, 0), 1), cut(landing.at[5], 1), axis, 1, 0)]
    mine_down = [link.send(cut(here(3, 0), 0), cut(landing.at[6], 0), axis, -1, 0)]
    yield start + block + 3.5
    far.wait_recv()
    add_rows(work.at[0], [here(2, 0), landing.at[0]])
    half_up = link.send(cut(work.at[0], 0), cut(landing.at[3], 0), axis, 1, 0)
    half_down = link.send(cut(work.at[0], 1), cut(landing.at[3], 1), axis, -1, 0)
    yield start + 1.5 * block + 3.0
    pair_up.wait_recv()
    pair_down.wait_recv()
    add_rows(work.at[1], [here(0, 1), landing.at[1], landing.at[2]])
    across = link.send(work.at[1], landing.at[4], axis, 0, 1)
    yield start + 2 * block + 5.0
    half_up.wait_recv()
    add_rows(cut(work.at[2], 0), [cut(here(1, 0), 0), cut(landing.at[3], 0)])
    mine_up.append(link.send(cut(work.at[2], 0), cut(landing.at[5], 0), axis, 1, 0))
    half_down.wait_recv()
    add_rows(cut(work.at[2], 1), [cut(here(3, 0), 1), cut(landing.at[3], 1)])
    mine_down.append(link.send(cut(work.at[2], 1), cut(landing.at[6], 1), axis, -1, 0))
    yield start + 3 * block + 4.0
    across.wait_recv()
    for copy in mine_up + mine_down:
        copy.wait_recv()
    add_rows(result, [here(0, 0), landing.at[4], landing.at[5], landing.at[6]])


def exchange_job(link, axis, part, slot, start=0.0, length=8.0):
    me = chip(axis)
    yield start
    kept = link.keep(part(me), slot(me))
    copies = [link.send(part(chip(axis, r, p)), slot(me), axis, r, p) for r, p in ALL]
    yield start + length
    for copy in copies:
        copy.wait_recv()
    link.kept_now(kept)


ANY = pl.BlockSpec(memory_space=pl.ANY)
INSIDE = pl.BlockSpec(memory_space=pltpu.VMEM)


def comm_call(kernel, number, inputs, in_specs, outputs, out_specs, scratch=(), limit=VMEM_LIMIT):
    sems = [pltpu.SemaphoreType.DMA((160,)), pltpu.SemaphoreType.DMA((160,)), pltpu.SemaphoreType.DMA((8,))]

    def body(*refs):
        link = Link(*refs[-3:])
        kernel(link, *refs[:-3])
        link.finish()

    return pl.pallas_call(
        body,
        out_shape=outputs,
        in_specs=in_specs,
        out_specs=out_specs,
        scratch_shapes=[*scratch, *sems],
        compiler_params=pltpu.CompilerParams(
            collective_id=number, has_side_effects=True, vmem_limit_bytes=limit
        ),
    )(*inputs)


shape = jax.ShapeDtypeStruct


def front_kernel(link, tokens, small, kv_send, w_out, token_rows, smalls, kv_other, out_full):
    link.greet(whole("shard") + [("ctx", 1, 0, 0), ("ctx", 3, 0, 0)] + SIBLING)
    core = lax.rem(lax.axis_index("ctx"), 2)
    ring = lax.axis_index("ctx") // 4

    def block(index, ring_further=0):
        at_ring = lax.rem(ring + ring_further, 4)
        rows = pl.ds(pl.multiple_of((core * 4 + at_ring) * 32, 32), 32)
        return out_full.at[index, rows]

    mine = pl.ds(pl.multiple_of((core * 4 + ring) * 32, 32), 32)
    passing, sibs = [], []

    def share(index, source):
        sibs.append(link.send(source, block(index), "ctx", 0, 0, 1))
        up = link.send(source, block(index), "ctx", 1, 0)
        passing.append((index, up, link.send(source, block(index), "ctx", -1, 0)))

    def ring_job():
        far = []
        for number in range(8):
            yield 10.0 + 3.8 * number
            index, up, down = passing[number]
            up.wait_recv()
            if number % 2 == 0:
                far.append((index, link.send(block(index, 3), block(index, 3), "ctx", 1, 0)))
            sibs.append(link.send(block(index, 3), block(index, 3), "ctx", 0, 0, 1))
            down.wait_recv()
            if number % 2 == 1:
                far.append((index, link.send(block(index, 1), block(index, 1), "ctx", -1, 0)))
            sibs.append(link.send(block(index, 1), block(index, 1), "ctx", 0, 0, 1))
        for number, (index, copy) in enumerate(far):
            yield 38.0 + number
            copy.wait_recv()
            sibs.append(link.send(block(index, 2), block(index, 2), "ctx", 0, 0, 1))
        yield 50.0
        for copy in sibs:
            copy.wait_recv()

    def kv_job():
        yield 0.0
        copy = link.send(kv_send, kv_other, "shard", 0, 1)
        yield 9.0
        copy.wait_recv()

    run(
        gather_job(link, "shard", w_out.at[mine], lambda i: out_full.at[i, mine], share, 0.0, 4.0),
        exchange_job(link, "shard", lambda i: small, lambda i: smalls.at[i], 0.0, 9.0),
        kv_job(),
        gather_halves(link, "shard", tokens, lambda i: token_rows.at[i], None, 0.1, 12.0),
        ring_job(),
    )


def qkv_kernel(link, queries, kv, queries_got, kv_all, kv_got, kv_own):
    link.greet(whole("shard") + near("ctx") + SIBLING)
    core = lax.rem(lax.axis_index("ctx"), 2)

    def kv_job():
        yield from exchange_job(link, "shard", lambda i: kv.at[i], lambda i: kv_got.at[i], 0.0, 6.0)
        for head in range(KV_HEADS):
            kv_own[:, head * 128 : (head + 1) * 128] = kv_got[2 * head] + kv_got[2 * head + 1]
        slot = lambda i: kv_all.at[i * 2 + core]
        sibs = []

        def share(index, block):
            sibs.append(link.send(block, slot(index), "ctx", 0, 0, 1))

        yield from gather_job(link, "ctx", kv_own, slot, share, 6.0, 2.7)
        for copy in sibs:
            copy.wait_recv()

    run(
        kv_job(),
        exchange_job(link, "shard", lambda i: queries.at[i], lambda i: queries_got.at[i], 0.1, 30.0),
    )


def column_block(ref, index, width=LANES):
    return ref.at[:, pl.ds(pl.multiple_of(index * width, width), width)]


def spread(link, summed, full, gather, start=0.0, block=10.8):
    core = lax.rem(lax.axis_index("ctx"), 2)
    slot = lambda i: column_block(full, core * 8 + i)
    sibs = []

    def share(index, source):
        sibs.append(link.send(source, slot(index), "ctx", 0, 0, 1))

    def share_half(source, index, k):
        half = source.shape[0]
        sibs.append(link.send(source, slot(index).at[pl.ds(k * half, half)], "ctx", 0, 0, 1))

    yield from gather(link, "ctx", summed, slot, share if gather is gather_job else share_half, start, block)
    for copy in sibs:
        copy.wait_recv()


def contract_rows(left, right):
    return lax.dot_general(left, right, (((0,), (0,)), ((), ())), preferred_element_type=F32)


def ffn_kernel(link, own, og, w_gate, w_up, w_down, attended, result, down_parts, summed, attended_cols,
               rows_all, gate_t, up_t, inner_t, parts, land_a, work_a, theirs, sib, land_b, work_b):
    link.greet(whole("shard") + near("ctx") + SIBLING)
    core = lax.rem(lax.axis_index("ctx"), 2)
    count = own.shape[0]
    ff = w_gate.shape[0]
    here = lambda ref, i: ref.at[pl.ds(pl.multiple_of(i * count, count), count)]
    token_lanes = lambda i: pl.ds(pl.multiple_of(i * count, count), count)

    def pair_of(ref, slots):
        return jnp.concatenate([here(ref, i)[...] for i in slots], axis=0)

    def forward(*offsets):
        slots = [chip("shard", r, p) for r, p in offsets]
        x = pair_of(rows_all, slots)
        gate = times_transposed(w_gate[...], x)
        up = times_transposed(w_up[...], x)
        inner_grad = times_transposed(w_down[...], pair_of(og, slots))
        sigmoid = 1.0 / (1.0 + jnp.exp(-gate))
        activated = gate * sigmoid
        inner = (activated * up).astype(LOW)
        gate_grad = (inner_grad * up * sigmoid * (1.0 + gate * (1.0 - sigmoid))).astype(LOW)
        up_grad = (inner_grad * activated).astype(LOW)
        for k, i in enumerate(slots):
            lanes = slice(k * count, k * count + count)
            inner_t[:, token_lanes(i)] = inner[:, lanes]
            gate_t[:, token_lanes(i)] = gate_grad[:, lanes]
            up_t[:, token_lanes(i)] = up_grad[:, lanes]
        return slots

    def tokens_of(ref, slots):
        return jnp.concatenate([ref[:, token_lanes(i)] for i in slots], axis=1)

    def back(slots):
        gates, ups = tokens_of(gate_t, slots), tokens_of(up_t, slots)
        for c in range(2):
            some = slice(c * 1024, c * 1024 + 1024)
            block = contract_rows(gates, w_gate[:, some]) + contract_rows(ups, w_up[:, some])
            for k, i in enumerate(slots):
                parts[i, :, some] = block[k * count : k * count + count].astype(LOW)

    def down(slots):
        inners = tokens_of(inner_t, slots)
        for c in range(2):
            some = slice(c * 1024, c * 1024 + 1024)
            block = contract_rows(inners, w_down[:, some])
            for k, i in enumerate(slots):
                down_parts[i, :, some] = block[k * count : k * count + count].astype(LOW)

    def every(*offsets):
        slots = forward(*offsets)
        back(slots)
        down(slots)

    last_pair_slots = []

    def compute_job():
        yield 15.0
        every((0, 0), (0, 1))
        yield 21.5
        every((1, 0), (3, 0))
        yield 33.0
        every((2, 0), (1, 1))
        yield 36.0
        slots = forward((3, 1), (2, 1))
        back(slots)
        last_pair_slots.append(slots)

    run(
        gather_halves(link, "shard", own, lambda i: here(rows_all, i)),
        compute_job(),
    )

    ring = chip("ctx") // 2

    def weight_columns(target, half, further, extra=None):
        wide = lax.rem(ring + further, 4)
        columns = pl.ds(pl.multiple_of(half * 1024 + wide * 256, 256), 256)
        into = pl.ds(pl.multiple_of(wide * 256, 256), 256)
        for i, (left, right) in enumerate(((gate_t, rows_all), (up_t, rows_all), (inner_t, og))):
            some = slice(i * ff, i * ff + ff)
            block = times(left[...], right[:, columns])
            if extra is not None:
                block = block + extra[some, into].astype(F32)
            target[some, into] = block.astype(LOW)
        return wide

    def weight_job():
        copies = {}

        def give(further):
            wide = weight_columns(theirs, 1 - core, further)
            copies[further] = link.send(
                column_block(theirs, wide, 256), column_block(sib, wide, 256), "ctx", 0, 0, 1
            )

        def take(further):
            copies[further].wait_recv()
            weight_columns(sib, core, further, sib)

        yield 0.1
        give(2)
        yield 1.0
        give(1)
        yield 2.0
        take(2)
        scatter = scatter_job(link, "ctx", lambda i: column_block(sib, i), land_b, work_b, summed, 6.0, 10.8)
        yield 3.0
        give(3)
        take(1)
        next(scatter)
        later = next(scatter)
        yield 4.0
        down(last_pair_slots[0])
        yield 5.0
        give(0)
        take(3)
        yield 6.0
        take(0)
        yield later
        yield from scatter

    run(
        scatter_job(link, "shard", lambda i: parts.at[i], land_a, work_a, result),
        weight_job(),
        exchange_job(
            link, "shard", lambda i: column_block(attended, i, 256), lambda i: here(attended_cols, i), 42.0, 14.0
        ),
    )


def swap_lanes(values):
    width = values.shape[1]
    low_half = lax.broadcasted_iota(jnp.int32, values.shape, 1) % HEAD < 32
    return jnp.where(low_half, pltpu.roll(values, width - 32, 1), pltpu.roll(values, 32, 1))


def tail_kernel(link, kv_parts, summed, hidden, queries, attended_cols, cosine, sine, normed, w_query, w_key, w_value,
                gains, full, attn_full, result, gain_sum,
                hidden_rows, query_cols, kv_cols, kv_w, left_t, parts, land_a, work_a,
                theirs, sib, land_b, work_b, attn_summed, sib_k, land_k, work_k, kv_grad, kv_turned,
                gain_buf, gain_land, gain_work, gain_ctx):
    link.greet(whole("shard") + whole("ctx") + SIBLING)
    core = lax.rem(lax.axis_index("ctx"), 2)
    leads = lax.rem(lax.axis_index("shard"), 2) == 0
    count = hidden.shape[0]
    here = lambda ref, i: ref.at[pl.ds(pl.multiple_of(i * count, count), count)]
    scatter = scatter_halves(link, "shard", lambda i: parts.at[i], land_a, work_a, result, 37.0)

    def make(*offsets):
        slots = [chip("shard", r, p) for r, p in offsets]
        pair_of = lambda ref: jnp.concatenate([here(ref, i)[...] for i in slots], axis=0)
        block = times(pair_of(query_cols), w_query[...]) + times(pair_of(kv_cols), kv_w[...])
        for k, i in enumerate(slots):
            parts[i] = block[k * count : k * count + count].astype(LOW)
        terms = block * pair_of(normed).astype(F32)
        return jnp.sum(terms, axis=0, keepdims=True)

    def main_job():
        yield 0.0
        copies = [
            link.send(kv_parts.at[i * 2 + 1 - core], sib_k.at[i], "ctx", 0, 0, 1) for i in range(8)
        ]
        for half, mine in enumerate((leads, jnp.logical_not(leads))):
            for which, weight in enumerate((w_key, w_value)):
                row = which * 64 + half * 32
                kv_w[row : row + 32, :] = jnp.where(mine, weight[...], jnp.zeros((32, D), LOW))
        yield 3.0
        for i, copy in enumerate(copies):
            copy.wait_recv()
            add_rows(sib_k.at[i], [sib_k.at[i], kv_parts.at[i * 2 + core]])
        yield from scatter_job(link, "ctx", lambda i: sib_k.at[i], land_k, work_k, kv_grad, 4.0, 2.7)
        me = chip("shard")
        own_cosine, own_sine = here(cosine, me)[...], here(sine, me)[...]
        key_lanes = lax.broadcasted_iota(jnp.int32, own_cosine.shape, 1) < HEAD
        for head in range(KV_HEADS):
            lanes = slice(head * 128, head * 128 + 128)
            both = kv_grad[:, lanes]
            turned = both * own_cosine - swap_lanes(both) * own_sine
            kv_turned[:, lanes] = jnp.where(key_lanes, turned, both).astype(LOW)
        part = lambda i: kv_turned.at[:, pl.ds(pl.multiple_of(i // 2 * 128, 128), 128)]
        yield from exchange_job(link, "shard", part, lambda i: here(kv_cols, i), 24.0, 10.0)
        total = make((2, 1), (1, 1))
        total = total + make((3, 1), (3, 0))
        total = total + make((1, 0), (2, 0))
        next(scatter)
        later = next(scatter)
        total = total + make((0, 0), (0, 1))
        for i in range(8):
            gain_buf[i] = gains[i]
            gain_buf[i, 0:1, :] = total[:, i * 256 : i * 256 + 256]
        yield later
        yield from scatter

    def weight_job():
        yield 46.0
        left_t[0:256, :] = jnp.transpose(query_cols[...].astype(F32)).astype(LOW)
        left_t[256:384, :] = jnp.transpose(kv_cols[...].astype(F32)).astype(LOW)
        left_t[384:640, :] = jnp.transpose(attended_cols[...].astype(F32)).astype(LOW)

        def columns(target, half, add):
            for c in range(4):
                wide = pl.ds(pl.multiple_of(half * 1024 + c * 256, 256), 256)
                into = slice(c * 256, c * 256 + 256)
                for rows, right in ((slice(0, 384), normed), (slice(384, 640), hidden_rows)):
                    block = times(left_t[rows, :], right[:, wide])
                    if add:
                        block = block + target[rows, into].astype(F32)
                    target[rows, into] = block.astype(LOW)

        columns(theirs, 1 - core, False)
        copy = link.send(theirs, sib, "ctx", 0, 0, 1)
        yield 48.5
        copy.wait_recv()
        columns(sib, core, True)
        block = lambda i: column_block(sib, i)
        yield from scatter_job(link, "ctx", block, land_b, work_b, attn_summed, 51.0, 4.5)
        yield from spread(link, attn_summed, attn_full, gather_job, 75.0, 4.0)

    def gain_job():
        yield from exchange_job(link, "shard", lambda i: gain_buf.at[i], lambda i: gain_land.at[i], 40.0, 10.0)
        gain_work[0] = sum(gain_land[i] for i in range(8))
        copy = link.send(gain_work.at[0], gain_work.at[1], "ctx", 0, 0, 1)
        yield 53.0
        copy.wait_recv()
        gain_work[2] = gain_work[0] + gain_work[1]
        copies = [
            link.send(gain_work.at[2], gain_ctx.at[i], "ctx", r, p) for i, (r, p) in enumerate(ALL)
        ]
        yield 69.0
        for copy in copies:
            copy.wait_recv()
        gain_sum[...] = gain_work[2] + sum(gain_ctx[i] for i in range(7))

    columns_of = lambda ref: lambda i: ref.at[:, pl.ds(pl.multiple_of(i * 256, 256), 256)]
    run(
        main_job(),
        exchange_job(link, "shard", columns_of(queries), lambda i: here(query_cols, i), 0.1, 22.0),
        gather_halves(link, "shard", hidden, lambda i: here(hidden_rows, i), None, 0.2, 14.5),
        spread(link, summed, full, gather_halves, 10.0),
        gain_job(),
        weight_job(),
    )


def first_kernel(pair_ref, tokens, gain, w_query, w_key, w_value, kv_other, cosine, sine,
                 normed_ref, q_ref, kv_ref, w_kv):
    @pl.when(pl.program_id(0) == 0)
    def _():
        leads = pair_ref[0] == 0
        nothing = jnp.zeros((32, D), LOW)
        choose = lambda yes, ref, other: jnp.where(yes, ref[...], other)
        w_kv[0:32, :] = choose(leads, w_key, nothing)
        w_kv[32:64, :] = choose(leads, kv_other, nothing)
        w_kv[64:96, :] = choose(jnp.logical_not(leads), kv_other, nothing)
        w_kv[96:128, :] = choose(jnp.logical_not(leads), w_value, nothing)

    values = tokens[...].astype(F32)
    normed = rms_forward(values, gain[...])[0].astype(LOW)
    normed_ref[...] = normed
    cosine, sine = cosine[...], sine[...]
    turn = lambda v: v * cosine + swap_lanes(v) * sine
    q = times_transposed(normed, w_query[...])
    for i in range(2):
        lanes = slice(i * 128, i * 128 + 128)
        q_ref[:, :, lanes] = turn(q[:, lanes]).astype(LOW).reshape(2, 128, 128)
    kv = times_transposed(normed, w_kv[...])
    keys = lax.broadcasted_iota(jnp.int32, kv.shape, 1) < HEAD
    kv_ref[...] = jnp.where(keys, turn(kv), kv).astype(LOW).reshape(2, 128, 128)


def first_part(pair, token_rows, gain, w_query, w_key, w_value, kv_other, cosine, sine):
    held = lambda *dims: pl.BlockSpec(dims, lambda i, *_: (0,) * len(dims))
    rows = lambda width: pl.BlockSpec((256, width), lambda i, *_: (i, 0))
    slots = lambda width: pl.BlockSpec((2, 128, width), lambda i, *_: (i, 0, 0))
    return pl.pallas_call(
        first_kernel,
        grid_spec=pltpu.PrefetchScalarGridSpec(
            num_scalar_prefetch=1,
            grid=(4,),
            in_specs=[rows(D), held(1, D), held(256, D), held(32, D), held(32, D), held(32, D), rows(128), rows(128)],
            out_specs=[rows(D), slots(256), slots(128)],
            scratch_shapes=[pltpu.VMEM((128, D), LOW)],
        ),
        out_shape=[shape((1024, D), LOW), shape((8, 128, 256), LOW), shape((8, 128, 128), LOW)],
        compiler_params=pltpu.CompilerParams(vmem_limit_bytes=VMEM_LIMIT),
        cost_estimate=pl.CostEstimate(flops=1 << 31, bytes_accessed=10 << 20, transcendentals=1024),
    )(pair, token_rows, gain, w_query, w_key, w_value, kv_other, cosine, sine)


BLOCK = 512
LOG2E = 1.4426950408889634
GROUPS = 1
COLUMNS = 512 // GROUPS


def sort_keys(order_ref, kv_ref, sorted_ref, flipped_ref):
    for c in range(16):
        lead = pl.multiple_of(order_ref[c] * 64, 64)
        trail = pl.multiple_of((31 - order_ref[c]) * 64, 64)
        sorted_ref[pl.ds(lead, 64), :] = kv_ref[c, 0:64, :]
        sorted_ref[pl.ds(trail, 64), :] = kv_ref[c, 64:128, :]
    for i in range(2048 // BLOCK):
        rows = slice(i * BLOCK, (i + 1) * BLOCK)
        flipped_ref[i] = jnp.transpose(sorted_ref[rows, :].astype(F32)).astype(LOW)


def spread_heads(blocks, high):
    pieces = []
    for block in blocks:
        block = block.astype(F32)
        turned = pltpu.roll(block, 64, 1)
        lane = lax.broadcasted_iota(jnp.int32, block.shape, 1)
        keep = (lane >= 64) if high else (lane < 64)
        first, second = (turned, block) if high else (block, turned)
        pieces += [jnp.where(keep, first, 0.0), jnp.where(keep, second, 0.0)]
    return jnp.concatenate(pieces, axis=0)


def join_heads(flipped):
    upright = jnp.transpose(flipped)
    return [
        jnp.concatenate([upright[i * 128 : i * 128 + 64], upright[i * 128 + 64 : i * 128 + 128]], axis=1)
        for i in range(4)
    ]


def query_blocks(ref, run):
    rows = slice(run * 64, run * 64 + 64)
    return [ref[s, rows, p * 128 : p * 128 + 128] for s in range(2) for p in range(2)]


def row_blocks(ref, run):
    rows = slice(run * 64, run * 64 + 64)
    return [ref[rows, i * 128 : i * 128 + 128] for i in range(4)]


def above(block, first_place):
    key = lax.broadcasted_iota(jnp.int32, (BLOCK, COLUMNS), 0) + block * BLOCK
    query = lax.broadcasted_iota(jnp.int32, (BLOCK, COLUMNS), 1) % 64 + first_place
    return key > query


def dot_kt(left, right):
    return lax.dot_general(left, right, (((1,), (1,)), ((), ())), preferred_element_type=F32)


def column_groups(values, axis):
    pieces = [slice(i * COLUMNS, (i + 1) * COLUMNS) for i in range(GROUPS)]
    return [values[p] if axis == 0 else values[:, p] for p in pieces]


def attend_kernel(order_ref, own_ref, q_ref, kv_ref, w_ref, x_ref, gain_ref, out_ref, lse_ref, hidden_ref, normed_ref,
                  sorted_ref, flipped_ref):
    sort_keys(order_ref, kv_ref, sorted_ref, flipped_ref)
    factor = HEAD**-0.5 * LOG2E
    for run in range(2):
        first_place = jnp.where(run == 0, own_ref[0], 31 - own_ref[0]) * 64
        last = first_place // BLOCK
        q = column_groups(spread_heads(query_blocks(q_ref, run), False).astype(LOW), 0)

        def step(block, carry, masked):
            rows = pl.ds(pl.multiple_of(block * BLOCK, BLOCK), BLOCK)
            keys, values = sorted_ref[rows, :], flipped_ref[block, 64:128, :]
            after = []
            for queries, (largest, total, mixed) in zip(q, carry):
                scores = dot_kt(keys, queries) * factor
                if masked:
                    scores = jnp.where(above(block, first_place), NEG, scores)
                top = jnp.maximum(largest, jnp.max(scores, axis=0, keepdims=True))
                fade = jnp.exp2(largest - top)
                exps = jnp.exp2(scores - top)
                total = total * fade + jnp.sum(exps, axis=0, keepdims=True)
                mixed = mixed * fade + times(values, exps.astype(LOW))
                after.append((top, total, mixed))
            return tuple(after)

        nothing = lambda rows, fill: jnp.full((rows, COLUMNS), fill, F32)
        carry = tuple((nothing(1, NEG), nothing(1, 0.0), nothing(64, 0.0)) for _ in range(GROUPS))
        carry = lax.fori_loop(0, last, functools.partial(step, masked=False), carry)
        carry = step(last, carry, True)
        mixed = jnp.concatenate([m / t for _, t, m in carry], axis=1)
        for i, block in enumerate(join_heads(mixed)):
            out_ref[run * 64 : run * 64 + 64, i * 128 : i * 128 + 128] = block.astype(LOW)
        lse_ref[0, run : run + 1, :] = jnp.concatenate([l + jnp.log2(t) for l, t, _ in carry], axis=1)

    @pl.when(pl.program_id(0) == 0)
    def _():
        hidden_ref[...] = x_ref[...].astype(F32)

    hidden_ref[...] += times(out_ref[...], w_ref[...])

    @pl.when(pl.program_id(0) == KV_HEADS - 1)
    def _():
        normed_ref[...] = rms_forward(hidden_ref[...], gain_ref[...])[0].astype(LOW)


def attend_back_kernel(order_ref, own_ref, q_ref, kv_ref, out_ref, hidden_ref, w_ref, lse_ref, cos_ref, sin_ref,
                       dq_ref, dkv_ref, sorted_ref, flipped_ref, total_ref, grad_ref):
    grad_ref[...] = times_transposed(hidden_ref[...], w_ref[...]).astype(LOW)
    sort_keys(order_ref, kv_ref, sorted_ref, flipped_ref)
    total_ref[...] = jnp.zeros_like(total_ref)
    scale = HEAD**-0.5
    factor = scale * LOG2E
    for run in range(2):
        first_place = jnp.where(run == 0, own_ref[0], 31 - own_ref[0]) * 64
        last = first_place // BLOCK
        q = column_groups(spread_heads(query_blocks(q_ref, run), False).astype(LOW), 0)
        grad_wide = spread_heads(row_blocks(grad_ref, run), True)
        out_wide = spread_heads(row_blocks(out_ref, run), True)
        grad = column_groups(grad_wide.astype(LOW), 0)
        inner = lax.dot_general(
            jnp.ones((8, 128), F32),
            grad_wide * out_wide,
            (((1,), (1,)), ((), ())),
            precision=lax.Precision.HIGHEST,
            preferred_element_type=F32,
        )[:1]
        inner = column_groups(inner, 1)
        lse = column_groups(lse_ref[0, run : run + 1, :], 1)

        def step(block, dq, masked):
            rows = pl.ds(pl.multiple_of(block * BLOCK, BLOCK), BLOCK)
            kv, keys = sorted_ref[rows, :], flipped_ref[block, 0:64, :]
            after, total = [], total_ref[rows, :]
            for i in range(GROUPS):
                probs = jnp.exp2(dot_kt(kv, q[i]) * factor - lse[i])
                if masked:
                    probs = jnp.where(above(block, first_place), 0.0, probs)
                score_grad = (probs * (dot_kt(kv, grad[i]) - inner[i])).astype(LOW)
                total = total + times(score_grad, q[i]) + times(probs.astype(LOW), grad[i])
                after.append(dq[i] + times(keys, score_grad))
            total_ref[rows, :] = total
            return tuple(after)

        dq = tuple(jnp.zeros((64, COLUMNS), F32) for _ in range(GROUPS))
        dq = lax.fori_loop(0, last, functools.partial(step, masked=False), dq)
        dq = jnp.concatenate(step(last, dq, True), axis=1)
        cosine, sine = cos_ref[run * 64 : run * 64 + 64, :], sin_ref[run * 64 : run * 64 + 64, :]
        low_half = lax.broadcasted_iota(jnp.int32, (64, 128), 1) % 64 < 32
        for i, block in enumerate(join_heads(dq * scale)):
            turned = jnp.where(low_half, pltpu.roll(block, 96, 1), pltpu.roll(block, 32, 1))
            dq_ref[run * 64 : run * 64 + 64, i * 128 : i * 128 + 128] = (
                block * cosine - turned * sine
            ).astype(LOW)
    weight = jnp.where(lax.broadcasted_iota(jnp.int32, (64, 128), 1) < 64, scale, 1.0)
    for c in range(16):
        lead = pl.multiple_of(order_ref[c] * 64, 64)
        trail = pl.multiple_of((31 - order_ref[c]) * 64, 64)
        dkv_ref[c, 0:64, :] = (total_ref[pl.ds(lead, 64), :] * weight).astype(LOW)
        dkv_ref[c, 64:128, :] = (total_ref[pl.ds(trail, 64), :] * weight).astype(LOW)


def attention_call(kernel, scalars, inputs, kinds, outputs, out_kinds, scratch, flops):
    specs = {
        "q": pl.BlockSpec((2, 128, 256), lambda g, *_: (g, 0, 0)),
        "kv": pl.BlockSpec((16, 128, 128), lambda g, *_: (0, 0, g)),
        "rows": pl.BlockSpec((128, 512), lambda g, *_: (0, g)),
        "lse": pl.BlockSpec((1, 8, 512), lambda g, *_: (g, 0, 0)),
        "table": pl.BlockSpec((128, 128), lambda g, order, own: (own[1], 0)),
        "weight": pl.BlockSpec((512, D), lambda g, *_: (g, 0)),
        "held": pl.BlockSpec((128, D), lambda g, *_: (0, 0)),
        "gain": pl.BlockSpec((1, D), lambda g, *_: (0, 0)),
    }
    keys = [pltpu.VMEM((2048, 128), LOW), pltpu.VMEM((2048 // BLOCK, 128, BLOCK), LOW)]
    return pl.pallas_call(
        kernel,
        grid_spec=pltpu.PrefetchScalarGridSpec(
            num_scalar_prefetch=2,
            grid=(KV_HEADS,),
            in_specs=[specs[k] for k in kinds],
            out_specs=[specs[k] for k in out_kinds],
            scratch_shapes=keys + scratch,
        ),
        out_shape=outputs,
        compiler_params=pltpu.CompilerParams(vmem_limit_bytes=VMEM_LIMIT),
        cost_estimate=pl.CostEstimate(flops=flops, bytes_accessed=8 << 20, transcendentals=8 << 20),
    )(*scalars, *inputs)


def attend(queries, kv_all, w_out, tokens, gain, order, own):
    whole_rows = lambda kind: jax.ShapeDtypeStruct((128, D), kind)
    return attention_call(
        attend_kernel,
        (order, own),
        (queries, kv_all, w_out, tokens, gain),
        ("q", "kv", "weight", "held", "gain"),
        [whole_rows(LOW), jax.ShapeDtypeStruct((4, 8, 512), F32), whole_rows(F32), whole_rows(LOW)],
        ("rows", "lse", "held", "held"),
        [],
        1 << 33,
    )


def attend_back(queries, kv_all, attended, hidden_low, w_out, lse, cosine, sine, order, own):
    return attention_call(
        attend_back_kernel,
        (order, own),
        (queries, kv_all, attended, hidden_low, w_out, lse, cosine, sine),
        ("q", "kv", "rows", "held", "weight", "lse", "table", "table"),
        [jax.ShapeDtypeStruct((128, D), LOW), jax.ShapeDtypeStruct((16, 128, 512), LOW)],
        ("rows", "kv"),
        [pltpu.VMEM((2048, 128), F32), pltpu.VMEM((128, 512), LOW)],
        1 << 34,
    )


def local(
    tokens,
    positions,
    out_grad,
    attn_gain,
    w_query,
    w_key,
    w_value,
    w_out,
    ffn_gain,
    w_gate,
    w_up,
    w_down,
):
    rows = tokens.shape[0]
    shard, ctx = lax.axis_index("shard"), lax.axis_index("ctx")
    shard_pair, core = shard % 2, ctx % 2
    places = positions[0]
    own_places = lax.dynamic_slice_in_dim(places, ctx * rows, rows)

    small = jnp.stack(
        [attn_gain, ffn_gain, jnp.concatenate([own_places // 64, own_places % 64]).astype(LOW)]
    )
    small = jnp.concatenate([small, jnp.zeros((13, 256), LOW)], axis=0)
    token_rows, smalls, kv_other, out_full = comm_call(
        front_kernel,
        0,
        [tokens, small, jnp.where(shard_pair == 0, w_value, w_key), w_out],
        [ANY] * 4,
        [shape((8, rows, D), LOW), shape((8, 16, 256), LOW), shape((32, D), LOW), shape((8, 256, D), LOW)],
        [ANY] * 4,
    )
    out_grad_late, token_rows = lax.optimization_barrier((out_grad, token_rows))
    out_grad_rows = lax.all_gather(out_grad_late, "shard", axis=0, tiled=True)
    token_rows, out_full = token_rows.reshape(-1, D), out_full.reshape(D, D)
    gain_one = smalls[:, 0].reshape(-1).astype(F32)
    gain_two = smalls[:, 1].reshape(-1).astype(F32)
    place_rows = (smalls[:, 2, :rows].astype(F32) * 64.0 + smalls[:, 2, rows:].astype(F32)).reshape(-1)
    cosine, sine = wide_tables(place_rows, 2)
    normed_rows, queries, kv_part = first_part(
        shard_pair[None], token_rows, gain_one[None], w_query, w_key, w_value, kv_other, cosine, sine
    )
    queries, kv_all = comm_call(
        qkv_kernel,
        1,
        [queries, kv_part],
        [ANY] * 2,
        [shape((8, rows, 256), LOW), shape((16, rows, 512), LOW)],
        [ANY] * 2,
        [pltpu.VMEM((8, rows, 128), LOW), pltpu.VMEM((rows, 512), LOW)],
    )

    order = places.reshape(16, rows)[:, 0] // 64
    own_order = jnp.stack([own_places[0] // 64, shard])
    attended, lse, hidden_state, normed_two = attend(
        queries, kv_all, out_full, tokens, gain_two[None], order, own_order
    )
    ff = w_gate.shape[0]
    vmem = lambda count, *dims: pltpu.VMEM((count, *dims), LOW)
    normed_two_grad, down_parts, summed, attended_cols = comm_call(
        ffn_kernel,
        3,
        [normed_two, out_grad_rows, w_gate, w_up, w_down, attended],
        [ANY] + [INSIDE] * 4 + [ANY],
        [shape((rows, D), F32), shape((8, rows, D), LOW), shape((3 * ff, LANES), LOW), shape((8 * rows, 256), LOW)],
        [INSIDE] * 3 + [ANY],
        [
            vmem(8 * rows, D),
            vmem(ff, 8 * rows),
            vmem(ff, 8 * rows),
            vmem(ff, 8 * rows),
            vmem(8, rows, D),
            vmem(7, rows, D),
            vmem(3, rows, D),
            vmem(3 * ff, 1024),
            vmem(3 * ff, 1024),
            vmem(7, 3 * ff, LANES),
            vmem(3, 3 * ff, LANES),
        ],
        62 * 1024 * 1024,
    )
    down_parts = down_parts.reshape(-1, D)
    down_sum = lax.psum_scatter(down_parts, "shard", scatter_dimension=0, tiled=True)
    outputs = (hidden_state + down_sum.astype(F32)).astype(LOW)
    inverse_two = inverse_of(hidden_state)
    gain_two_part = jnp.sum(normed_two_grad * hidden_state * inverse_two, axis=0)
    hidden_grad = out_grad.astype(F32) + rms_backward(
        hidden_state, inverse_two, gain_two, normed_two_grad
    )
    hidden_low = hidden_grad.astype(LOW)
    query_pre_grad, kv_parts = attend_back(
        queries, kv_all, attended, hidden_low, out_full, lse, cosine, sine, order, own_order
    )
    inputs = tokens.astype(F32)
    gains = jnp.zeros((8, 8, 256), F32).at[:, 1].set(gain_two_part.reshape(8, 256))
    ffn_full, attn_full, normed_grad, gain_sum = comm_call(
        tail_kernel,
        4,
        [kv_parts, summed, hidden_low, query_pre_grad, attended_cols, cosine, sine, normed_rows]
        + [w_query, w_key, w_value, gains],
        [INSIDE, INSIDE, ANY, ANY] + [INSIDE] * 8,
        [shape((3 * ff, D), LOW), shape((640, D), LOW), shape((rows, D), F32), shape((8, 256), F32)],
        [ANY, ANY, INSIDE, INSIDE],
        [
            vmem(8 * rows, D),
            vmem(8 * rows, 256),
            vmem(8 * rows, 128),
            vmem(128, D),
            vmem(640, 8 * rows),
            vmem(8, rows, D),
            vmem(7, rows, D),
            vmem(3, rows, D),
            vmem(640, 1024),
            vmem(640, 1024),
            vmem(7, 640, LANES),
            vmem(3, 640, LANES),
            vmem(640, LANES),
            vmem(8, rows, 512),
            vmem(7, rows, 512),
            vmem(3, rows, 512),
            pltpu.VMEM((rows, 512), F32),
            vmem(rows, 512),
            pltpu.VMEM((8, 8, 256), F32),
            pltpu.VMEM((8, 8, 256), F32),
            pltpu.VMEM((3, 8, 256), F32),
            pltpu.VMEM((7, 8, 256), F32),
        ],
    )
    gate_wgrad, up_wgrad, down_wgrad = (
        ffn_full[i * ff : (i + 1) * ff].astype(F32) for i in range(3)
    )
    inverse_one = inverse_of(inputs)
    input_grad = hidden_grad + rms_backward(inputs, inverse_one, gain_one, normed_grad)
    attn_rows = lambda start, size: lax.dynamic_slice_in_dim(attn_full, start, size).astype(F32)
    query_wgrad, out_wgrad = attn_rows(0, 256), attn_rows(384, 256)
    key_wgrad, value_wgrad = attn_rows(256 + shard_pair * 32, 32), attn_rows(320 + shard_pair * 32, 32)
    return (
        outputs,
        input_grad,
        gain_sum[0] / attn_gain.astype(F32),
        query_wgrad,
        key_wgrad,
        value_wgrad,
        out_wgrad,
        gain_sum[1],
        gate_wgrad,
        up_wgrad,
        down_wgrad,
    )


def solution(mesh):
    rows = P(("shard", "ctx"), None)
    matrix = P("shard", None)
    vector = P("shard")
    in_specs = (rows, matrix, rows, vector, matrix, matrix, matrix, matrix, vector) + (matrix,) * 3
    out_specs = (rows, rows, vector, matrix, matrix, matrix, matrix, vector) + (matrix,) * 3
    return jax.shard_map(local, mesh=mesh, in_specs=in_specs, out_specs=out_specs, check_vma=False)
```
